128 devices in a mesh: grp: 4 (over z), fsdp: 32 (over y, x, core).
Axes of the slice: x: 4, y: 4, z: 4, core: 2. Of those that a mesh axis runs over, the one named last changes fastest.
Arguments:
- ids: int32 [128, 256], P(('grp', 'fsdp')), may hold values from 0 to 30719
- lengths: int32 [128], P(('grp', 'fsdp')), may hold values from 1 to 256, as said below
- picks: int32 [128, 64], P(('grp', 'fsdp')), may hold values from 0 to 255, as said below
- labels: int32 [128, 64], P(('grp', 'fsdp')), may hold values from 0 to 30719
- s_table: float32 [30720, 512], P('fsdp')
- s_pos: float32 [256, 512], P('fsdp'), may hold values from -0.25 to 0.25
- s_qkv: float32 [512, 1536], P('fsdp'), may hold values from -0.25 to 0.25
- s_out: float32 [512, 512], P('fsdp'), may hold values from -1 to 1
- s_up: float32 [512, 2048], P('fsdp'), may hold values from -0.25 to 0.25
- s_down: float32 [2048, 512], P('fsdp'), may hold values from -0.125 to 0.125
- s_norms: float32 [512, 6], P('fsdp')
- m_table: float32 [30720, 512], P('fsdp'), may hold values from -1.4305115e-06 to 1.4305115e-06
- m_pos: float32 [256, 512], P('fsdp'), may hold values from -1.4305115e-06 to 1.4305115e-06
- m_qkv: float32 [512, 1536], P('fsdp'), may hold values from -1.4305115e-06 to 1.4305115e-06
- m_out: float32 [512, 512], P('fsdp'), may hold values from -1.4305115e-06 to 1.4305115e-06
- m_up: float32 [512, 2048], P('fsdp'), may hold values from -1.4305115e-06 to 1.4305115e-06
- m_down: float32 [2048, 512], P('fsdp'), may hold values from -1.4305115e-06 to 1.4305115e-06
- m_norms: float32 [512, 6], P('fsdp'), may hold values from -5.722046e-06 to 5.722046e-06
- a_table: float32 [30720, 512], P('fsdp'), may hold values from -0.25 to 0.25
- a_pos: float32 [256, 512], P('fsdp'), may hold values from -0.25 to 0.25
- a_qkv: float32 [512, 1536], P('fsdp'), may hold values from -0.25 to 0.25
- a_out: float32 [512, 512], P('fsdp'), may hold values from -0.25 to 0.25
- a_up: float32 [512, 2048], P('fsdp'), may hold values from -0.25 to 0.25
- a_down: float32 [2048, 512], P('fsdp'), may hold values from -0.125 to 0.125
- a_norms: float32 [512, 6], P('fsdp'), may hold values from -3 to 3
- t_table: bfloat16 [4, 30720, 768], P('grp', 'fsdp')
- t_pos: bfloat16 [4, 256, 768], P('grp'), may hold values from -0.21875 to 0.21875
- t_qkv: bfloat16 [4, 768, 2304], P('grp'), may hold values from -0.21875 to 0.21875
- t_out: bfloat16 [4, 768, 768], P('grp'), may hold values from -0.875 to 0.875
- t_up: bfloat16 [4, 768, 3072], P('grp'), may hold values from -0.21875 to 0.21875
- t_down: bfloat16 [4, 3072, 768], P('grp'), may hold values from -0.109375 to 0.109375
- t_norms: bfloat16 [4, 768, 6], P('grp')
Outputs:
- loss_sum: float32 [], replicated
- count: float32 [], replicated
- clip_norm: float32 [], replicated
- new_table: float32 [30720, 512], P('fsdp')
- new_pos: float32 [256, 512], P('fsdp')
- new_qkv: float32 [512, 1536], P('fsdp')
- new_out: float32 [512, 512], P('fsdp')
- new_up: float32 [512, 2048], P('fsdp')
- new_down: float32 [2048, 512], P('fsdp')
- new_norms: float32 [512, 6], P('fsdp')
- mom_table: float32 [30720, 512], P('fsdp')
- mom_pos: float32 [256, 512], P('fsdp')
- mom_qkv: float32 [512, 1536], P('fsdp')
- mom_out: float32 [512, 512], P('fsdp')
- mom_up: float32 [512, 2048], P('fsdp')
- mom_down: float32 [2048, 512], P('fsdp')
- mom_norms: float32 [512, 6], P('fsdp')
- avg_table: float32 [30720, 512], P('fsdp')
- avg_pos: float32 [256, 512], P('fsdp')
- avg_qkv: float32 [512, 1536], P('fsdp')
- avg_out: float32 [512, 512], P('fsdp')
- avg_up: float32 [512, 2048], P('fsdp')
- avg_down: float32 [2048, 512], P('fsdp')
- avg_norms: float32 [512, 6], P('fsdp')
The draws below stay inside these ranges and needn't reach their ends.
Inputs may be any that keep to these rules, and one draw needn't show every extreme that they name: `lengths`: real tokens of each sequence; the sequence on the last device of fsdp in each teacher group has all 256. `picks`: all different within a row; positions at or beyond the sequence's length don't count.
All inputs are finite; a program needn't handle non-finite values.
Results may differ from the reference program's by a relative error of at most 0.018.
The reference program's roundings to bfloat16 on the way count: a program that leaves them out, or rounds other values in their place, can miss the bound.
Values may be sent and summed in bfloat16 or wider, within the bound.
A program may use at most 320 MiB of HBM per device.

```python
import math
import jax
import jax.numpy as jnp
import numpy as np
from jax import lax

D = 512
HD = 64
FF = 2048
TD = 768
TFF = 3072
VOCAB = 30720
TOK_DEV = 256
PICK = 64
TEACHERS = 4
SEQS = 128


def row_rise(count_rows, start, finish):
    return start + (finish - start) * jnp.arange(count_rows, dtype=jnp.float32) / max(count_rows - 1, 1)


def norm_columns(key, lead, width, start, finish):
    first, second = jax.random.split(key)
    rise = row_rise(width, start, finish)
    gains = rise[None, :, None] * jax.random.uniform(first, (lead, width, 3), minval=0.8, maxval=1.25)
    shifts = 0.3 * jax.random.normal(second, (lead, width, 3))
    return jnp.stack([gains, shifts], axis=-1).reshape(lead, width, 6)


def draw_lengths(key, part):
    key = jax.random.fold_in(key, 11)
    first, second = jax.random.split(key)
    per_group = SEQS // TEACHERS
    place = jnp.arange(SEQS, dtype=jnp.int32) % per_group
    least = TOK_DEV // 3
    top = least + (TOK_DEV - least) * place // max(per_group - 1, 1)
    tail = jax.random.randint(first, (SEQS,), 1, 17)
    keep = jax.random.randint(second, (SEQS,), 1, 17)
    drawn = jnp.maximum(top * tail * keep // 256, 1)
    return jnp.where(place == per_group - 1, TOK_DEV, drawn).astype(jnp.int32)


def draw_picks(key, part):
    key = jax.random.fold_in(key, 12)
    keys = jax.random.split(key, SEQS)
    rows = jax.vmap(lambda one: jax.random.permutation(one, TOK_DEV)[:PICK])(keys)
    return rows.astype(jnp.int32)


def draw_s_table(key, part):
    key = jax.random.fold_in(key, 13)
    base = jax.random.normal(key, (VOCAB, D))
    rise = row_rise(VOCAB, 1.0, 3.0)
    return (base * rise[:, None] * D ** (-0.5)).astype(jnp.float32)


def draw_t_table(key, part):
    key = jax.random.fold_in(key, 14)
    first, second = jax.random.split(key)
    factor = jax.random.uniform(second, (TEACHERS, 1, 1), minval=0.6, maxval=1.8)
    base = jax.random.normal(first, (TEACHERS, VOCAB, TD))
    rise = row_rise(VOCAB, 1.0, 3.0)
    return (base * rise[None, :, None] * factor * TD ** (-0.5)).astype(jnp.bfloat16)


def draw_s_norms(key, part):
    key = jax.random.fold_in(key, 15)
    table = norm_columns(key, 1, D, 0.5, 1.5)
    return table[0].astype(jnp.float32)


def draw_t_norms(key, part):
    key = jax.random.fold_in(key, 16)
    table = norm_columns(key, TEACHERS, TD, 0.5, 1.5)
    return table.astype(jnp.bfloat16)


def place_ends(values, own_key, low, top_value):
    longest = values.shape.index(max(values.shape))
    spots = []
    for shift in (0, 1):
        where = [jax.random.randint(jax.random.fold_in(own_key, axis), (), 0, length) for axis, length in enumerate(values.shape)]
        where[longest] = (where[longest] + shift) % values.shape[longest]
        spots.append(tuple(where))
    return values.at[spots[0]].set(low).at[spots[1]].set(top_value)


def shard_levels(key, dims, pieces, smallest, top_value):
    level, own = 1.0, jax.random.fold_in(key, 6)
    for dim, shards_of in pieces:
        draws = jnp.exp(jax.random.uniform(jax.random.fold_in(own, dim), (shards_of,), jnp.float32, smallest / len(pieces), top_value / len(pieces)))
        level = level * jnp.repeat(draws, dims[dim] // shards_of).reshape([-1 if axis == dim else 1 for axis in range(len(dims))])
    return level


def rank_table(count, lean):
    weights = [(1 << 20) // math.isqrt(grade ** lean) + 1 for grade in range(1, count + 1)]
    scale = 1 + sum(weights) // (1 << 30)
    return np.cumsum(np.array([max(1, weight // scale) for weight in weights]))


def ranked(stream_key, extent, count, slope):
    table = rank_table(count, slope)
    pick = jax.random.randint(jax.random.fold_in(stream_key, 1), extent, 0, int(table[count - 1]))
    standing = jnp.searchsorted(jnp.asarray(table, jnp.int32), pick, side="right")
    return jax.random.permutation(jax.random.fold_in(stream_key, 2), count)[standing].astype(jnp.int32)


def normal_values(rng, extent, scale, limit, cuts=(), kind=jnp.bfloat16):
    values = scale * jax.random.normal(rng, extent, jnp.float32)
    if cuts:
        values = values * shard_levels(rng, extent, cuts, -0.22, 0.18)
    return jnp.clip(values, -limit, limit).astype(kind)


def setup_inputs(seed: int = 0) -> dict:
    key_of = jax.random.split(jax.random.key(seed), 33)
    return {
        "ids": place_ends(ranked(key_of[0], (SEQS, TOK_DEV), VOCAB, 2), jax.random.fold_in(key_of[0], 3), 0, VOCAB - 1).astype(jnp.int32),
        "lengths": draw_lengths(jax.random.fold_in(key_of[32], 71), 0),
        "picks": draw_picks(jax.random.fold_in(key_of[32], 71), 0),
        "labels": place_ends(ranked(key_of[3], (SEQS, PICK), VOCAB, 2), jax.random.fold_in(key_of[3], 3), 0, VOCAB - 1).astype(jnp.int32),
        "s_table": draw_s_table(jax.random.fold_in(key_of[32], 71), 0),
        "s_pos": normal_values(key_of[5], (TOK_DEV, D), D ** -0.5, 0.25, ((0, 32),), jnp.float32),
        "s_qkv": normal_values(key_of[6], (D, 3 * D), D ** -0.5, 0.25, ((0, 32),), jnp.float32),
        "s_out": normal_values(key_of[7], (D, D), (D * 16 // TOK_DEV) ** -0.5, 1.0, ((0, 32),), jnp.float32),
        "s_up": normal_values(key_of[8], (D, FF), D ** -0.5, 0.25, ((0, 32),), jnp.float32),
        "s_down": normal_values(key_of[9], (FF, D), FF ** -0.5, 0.125, ((0, 32),), jnp.float32),
        "s_norms": draw_s_norms(jax.random.fold_in(key_of[32], 71), 0),
        "m_table": normal_values(key_of[11], (VOCAB, D), (0.001 * (VOCAB * D + TOK_DEV * D + 4 * D * D + 2 * D * FF + 6 * D) ** -0.5), 1.430511474609375e-06, ((0, 32),), jnp.float32),
        "m_pos": normal_values(key_of[12], (TOK_DEV, D), (0.001 * (VOCAB * D + TOK_DEV * D + 4 * D * D + 2 * D * FF + 6 * D) ** -0.5), 1.430511474609375e-06, ((0, 32),), jnp.float32),
        "m_qkv": normal_values(key_of[13], (D, 3 * D), (0.001 * (VOCAB * D + TOK_DEV * D + 4 * D * D + 2 * D * FF + 6 * D) ** -0.5), 1.430511474609375e-06, ((0, 32),), jnp.float32),
        "m_out": normal_values(key_of[14], (D, D), (0.001 * (VOCAB * D + TOK_DEV * D + 4 * D * D + 2 * D * FF + 6 * D) ** -0.5), 1.430511474609375e-06, ((0, 32),), jnp.float32),
        "m_up": normal_values(key_of[15], (D, FF), (0.001 * (VOCAB * D + TOK_DEV * D + 4 * D * D + 2 * D * FF + 6 * D) ** -0.5), 1.430511474609375e-06, ((0, 32),), jnp.float32),
        "m_down": normal_values(key_of[16], (FF, D), (0.001 * (VOCAB * D + TOK_DEV * D + 4 * D * D + 2 * D * FF + 6 * D) ** -0.5), 1.430511474609375e-06, ((0, 32),), jnp.float32),
        "m_norms": normal_values(key_of[17], (D, 6), (0.004 * (VOCAB * D + TOK_DEV * D + 4 * D * D + 2 * D * FF + 6 * D) ** -0.5), 5.7220458984375e-06, ((0, 32),), jnp.float32),
        "a_table": normal_values(key_of[18], (VOCAB, D), D ** -0.5, 0.25, ((0, 32),), jnp.float32),
        "a_pos": normal_values(key_of[19], (TOK_DEV, D), D ** -0.5, 0.25, ((0, 32),), jnp.float32),
        "a_qkv": normal_values(key_of[20], (D, 3 * D), D ** -0.5, 0.25, ((0, 32),), jnp.float32),
        "a_out": normal_values(key_of[21], (D, D), D ** -0.5, 0.25, ((0, 32),), jnp.float32),
        "a_up": normal_values(key_of[22], (D, FF), D ** -0.5, 0.25, ((0, 32),), jnp.float32),
        "a_down": normal_values(key_of[23], (FF, D), FF ** -0.5, 0.125, ((0, 32),), jnp.float32),
        "a_norms": normal_values(key_of[24], (D, 6), 0.5, 3.0, ((0, 32),), jnp.float32),
        "t_table": draw_t_table(jax.random.fold_in(key_of[32], 71), 0),
        "t_pos": normal_values(key_of[26], (TEACHERS, TOK_DEV, TD), TD ** -0.5, 0.21875, ((0, 4),)),
        "t_qkv": normal_values(key_of[27], (TEACHERS, TD, 3 * TD), TD ** -0.5, 0.21875, ((0, 4),)),
        "t_out": normal_values(key_of[28], (TEACHERS, TD, TD), (TD * 16 // TOK_DEV) ** -0.5, 0.875, ((0, 4),)),
        "t_up": normal_values(key_of[29], (TEACHERS, TD, TFF), TD ** -0.5, 0.21875, ((0, 4),)),
        "t_down": normal_values(key_of[30], (TEACHERS, TFF, TD), TFF ** -0.5, 0.109375, ((0, 4),)),
        "t_norms": draw_t_norms(jax.random.fold_in(key_of[32], 71), 0),
    }


@jax.custom_vjp
def low(v):
    return lax.optimization_barrier(v.astype(jnp.bfloat16)).astype(jnp.float32)

@jax.custom_vjp
def low_back(v):
    return v

def low_keep(v):
    return (low(v), None)

def low_pass(kept, grad):
    return (grad,)

def back_keep(v):
    return (v, None)

def back_low(kept, grad):
    return (low(grad),)
low.defvjp(low_keep, low_pass)
low_back.defvjp(back_keep, back_low)
HIGH = lax.Precision.HIGHEST
norm_eps = 1e-12
clip_limit = 0.001
learn_rate = 100000.0
momentum_decay = 0.9
average_decay = 0.9

def layer_norm(value, gain, shift):
    mean = lax.optimization_barrier(jnp.mean(value, -1, keepdims=True))
    centred = value - mean
    var = lax.optimization_barrier(jnp.mean(centred * centred, -1, keepdims=True))
    return centred * lax.rsqrt(var + norm_eps) * gain + shift

def encode(ids, length, weights, grads):
    table, positions, w_qkv, w_out, w_up, w_down, norms = weights
    span, width = positions.shape
    heads = width // HD
    emb = table[ids] + positions
    first = layer_norm(emb, norms[:, 0], norms[:, 1])
    packed = low(jnp.dot(low(first), w_qkv, precision=HIGH))
    if grads:
        packed = low_back(packed)
    query = packed[:, :width].reshape(span, heads, HD)
    keyed = packed[:, width:2 * width].reshape(span, heads, HD)
    valued = packed[:, 2 * width:].reshape(span, heads, HD)
    scores = jnp.einsum('qhd,khd->hqk', query, keyed, precision=HIGH) * HD ** (-0.5)
    valid = jnp.arange(span) < length
    scores = jnp.where(valid[None, None, :], scores, -1e+30)
    if grads:
        scores = low_back(scores)
    probs = low(jax.nn.softmax(scores, axis=-1))
    context = low(jnp.einsum('hqk,khd->qhd', probs, valued, precision=HIGH).reshape(span, width))
    if grads:
        context = low_back(context)
    attn = jnp.dot(context, w_out, precision=HIGH)
    if grads:
        attn = low_back(attn)
    second = layer_norm(first + attn, norms[:, 2], norms[:, 3])
    hidden_pre = jnp.dot(low(second), w_up, precision=HIGH)
    if grads:
        hidden_pre = low_back(hidden_pre)
    active = low(jax.nn.gelu(hidden_pre, approximate=False))
    ffn = jnp.dot(active, w_down, precision=HIGH)
    if grads:
        ffn = low_back(ffn)
    return layer_norm(second + ffn, norms[:, 4], norms[:, 5])

def teacher_logp(weights, ids, length, picks):
    final = encode(ids, length, weights, False)
    rows = low(final[picks])
    logits = jnp.dot(rows, weights[0].T, precision=HIGH)
    return jax.nn.log_softmax(logits, axis=-1)

def sequence_loss(student, teachers, ids, length, picks, labels):
    logp = jax.vmap(teacher_logp, in_axes=(0, None, None, None))(teachers, ids, length, picks)
    counted = (picks < length).astype(jnp.float32)
    hits = jnp.sum(counted)
    index = jnp.broadcast_to(labels[None, :, None], (logp.shape[0], labels.shape[0], 1))
    label_logp = jnp.take_along_axis(logp, index, axis=2)[:, :, 0]
    losses = -lax.optimization_barrier(jnp.sum(counted[None, :] * label_logp, -1)) / jnp.maximum(hits, 1.0)
    blend = jax.nn.softmax(-losses)
    probs = jnp.exp(logp)
    target = lax.optimization_barrier(jnp.sum(low(blend[:, None, None] * probs), 0))
    entropy = lax.optimization_barrier(jnp.sum(low(blend[:, None] * lax.optimization_barrier(jnp.sum(probs * logp, -1))), 0))
    final = encode(ids, length, student, True)
    rows = low(final[picks])
    logits = low_back(jnp.dot(rows, student[0].T, precision=HIGH))
    per_row = entropy - lax.optimization_barrier(jnp.sum(target * logits, -1)) + jax.scipy.special.logsumexp(logits, axis=-1)
    return (jnp.sum(counted * per_row), hits)

def reference(ids, lengths, picks, labels, s_table, s_pos, s_qkv, s_out, s_up, s_down, s_norms, m_table, m_pos, m_qkv, m_out, m_up, m_down, m_norms, a_table, a_pos, a_qkv, a_out, a_up, a_down, a_norms, t_table, t_pos, t_qkv, t_out, t_up, t_down, t_norms):
    teachers = tuple((w.astype(jnp.float32) for w in (t_table, t_pos, t_qkv, t_out, t_up, t_down, t_norms)))
    masters = (s_table, s_pos, s_qkv, s_out, s_up, s_down, s_norms)
    momenta = (m_table, m_pos, m_qkv, m_out, m_up, m_down, m_norms)
    averages = (a_table, a_pos, a_qkv, a_out, a_up, a_down, a_norms)

    def total_loss(params):
        student = tuple((low(w) for w in params))

        def one(items):
            return jax.checkpoint(sequence_loss)(student, teachers, items[0], items[1], items[2], items[3])
        losses, hits = lax.map(one, (ids, lengths, picks, labels))
        return (jnp.sum(losses), jnp.sum(hits))
    loss_sum, pull, count = jax.vjp(total_loss, masters, has_aux=True)
    grads = pull(jnp.ones_like(loss_sum))[0]
    squares = sum((jnp.sum(g * g) for g in grads))
    clip_norm = jnp.sqrt(squares) / count
    factor = jnp.minimum(1.0, clip_limit / clip_norm) / count
    new_weights, new_moments, new_averages = ([], [], [])
    for weight, moment, average, grad in zip(masters, momenta, averages, grads):
        clipped = grad * factor
        moment_new = momentum_decay * moment + clipped
        weight_new = weight - learn_rate * (clipped + momentum_decay * moment_new)
        new_weights.append(weight_new)
        new_moments.append(moment_new)
        new_averages.append(average_decay * average + (1.0 - average_decay) * weight_new)
    return (loss_sum, count, clip_norm, new_weights[0], new_weights[1], new_weights[2], new_weights[3], new_weights[4], new_weights[5], new_weights[6], new_moments[0], new_moments[1], new_moments[2], new_moments[3], new_moments[4], new_moments[5], new_moments[6], new_averages[0], new_averages[1], new_averages[2], new_averages[3], new_averages[4], new_averages[5], new_averages[6])
```

```python
import math
from functools import partial

import jax
import jax.numpy as jnp
from jax import lax
from jax.sharding import Mesh
from jax.sharding import PartitionSpec as P

HD = 64
FSDP = ("y", "x", "c")
GRP_FSDP = ("grp", "y", "x", "c")

norm_eps = 1e-12
clip_limit = 0.001
learn_rate = 100000.0
momentum_decay = 0.9
average_decay = 0.9


def from_everyone(value, axis):
    copies = jnp.broadcast_to(value, (lax.axis_size(axis), *value.shape))
    return lax.all_to_all(copies, axis, split_axis=0, concat_axis=0, tiled=True)


def sum_of_groups(value):
    groups = lax.axis_size("grp")
    me = lax.axis_index("grp")
    parts = [value]
    for step in range(1, groups):
        parts.append(lax.ppermute(value, "grp", [(g, (g + step) % groups) for g in range(groups)]))
    return jnp.stack(parts)[(me - jnp.arange(groups)) % groups].sum(0)


def sum_and_scatter(parts):
    shape = parts.shape[1:]
    parts = parts.reshape(4, 4, 2, *shape)
    parts = jnp.moveaxis(parts, (2, 1), (0, 1)).reshape(2, 16, *shape)
    for axis in ("c", "x", "y"):
        parts = lax.all_to_all(parts, axis, split_axis=0, concat_axis=0, tiled=True)
        parts = parts.astype(jnp.float32).sum(0)
        if axis != "y":
            parts = parts.astype(jnp.bfloat16)
            parts = parts.reshape(4, -1, *shape) if axis == "c" else parts
    return parts


def layer_norm(value, gain, shift):
    mean = jnp.mean(value, -1, keepdims=True)
    centred = value - mean
    var = jnp.mean(centred * centred, -1, keepdims=True)
    return centred * lax.rsqrt(var + norm_eps) * gain + shift


def norm_back(value, gain, shift, grad):
    _, pull = jax.vjp(layer_norm, value, gain, shift)
    return pull(grad)


def project(left, right):
    return jnp.einsum("blk,kn->bln", left, right, preferred_element_type=jnp.float32)


def project_back(grad, right):
    return jnp.einsum("bln,kn->blk", grad, right, preferred_element_type=jnp.float32)


def weight_grad(left, grad):
    return jnp.einsum("blk,bln->kn", left, grad, preferred_element_type=jnp.float32)


def split_heads(packed, width):
    batch, span = (packed.shape[0], packed.shape[1])
    return [
        packed[:, :, piece * width : (piece + 1) * width].reshape(batch, span, width // HD, HD)
        for piece in range(3)
    ]


def masked_scores(query, keyed, lengths):
    scores = jnp.einsum(
        "bqhd,bkhd->bhqk", query, keyed, preferred_element_type=jnp.float32
    ) * HD ** (-0.5)
    valid = jnp.arange(query.shape[1])[None, :] < lengths[:, None]
    return jnp.where(valid[:, None, None, :], scores, -1e30)


def forward(embedded, lengths, weights):
    w_qkv, w_out, w_up, w_down, norms = weights
    norms = norms.astype(jnp.float32)
    width = w_out.shape[1]
    first = layer_norm(embedded, norms[:, 0], norms[:, 1])
    first_low = first.astype(jnp.bfloat16)
    packed = project(first_low, w_qkv).astype(jnp.bfloat16)
    query, keyed, valued = split_heads(packed, width)
    scores = masked_scores(query, keyed, lengths)
    top = jnp.max(scores, -1, keepdims=True)
    total = jnp.sum(jnp.exp(scores - top), -1, keepdims=True)
    probs = (jnp.exp(scores - top) / total).astype(jnp.bfloat16)
    context = jnp.einsum("bhqk,bkhd->bqhd", probs, valued, preferred_element_type=jnp.float32)
    context = context.reshape(first.shape).astype(jnp.bfloat16)
    joined = first + project(context, w_out)
    second = layer_norm(joined, norms[:, 2], norms[:, 3])
    second_low = second.astype(jnp.bfloat16)
    hidden_pre = project(second_low, w_up)
    active = jax.nn.gelu(hidden_pre, approximate=False).astype(jnp.bfloat16)
    summed = second + project(active, w_down)
    final = layer_norm(summed, norms[:, 4], norms[:, 5])
    saved = (
        embedded,
        first_low,
        packed,
        top,
        total,
        context,
        joined,
        second_low,
        hidden_pre,
        active,
        summed,
    )
    return (final, saved)


def backward(lengths, weights, saved, grad_final):
    w_qkv, w_out, w_up, w_down, norms = weights
    norms = norms.astype(jnp.float32)
    (
        embedded,
        first_low,
        packed,
        top,
        total,
        context,
        joined,
        second_low,
        hidden_pre,
        active,
        summed,
    ) = saved
    width = w_out.shape[1]
    grad_summed, gain_c, shift_c = norm_back(summed, norms[:, 4], norms[:, 5], grad_final)
    grad_ffn = grad_summed.astype(jnp.bfloat16)
    g_down = weight_grad(active, grad_ffn)
    _, gelu_pull = jax.vjp(partial(jax.nn.gelu, approximate=False), hidden_pre)
    grad_up = gelu_pull(project_back(grad_ffn, w_down))[0].astype(jnp.bfloat16)
    g_up = weight_grad(second_low, grad_up)
    grad_second = grad_summed + project_back(grad_up, w_up)
    grad_joined, gain_b, shift_b = norm_back(joined, norms[:, 2], norms[:, 3], grad_second)
    grad_attn = grad_joined.astype(jnp.bfloat16)
    g_out = weight_grad(context, grad_attn)
    grad_context = project_back(grad_attn, w_out).astype(jnp.bfloat16)
    query, keyed, valued = split_heads(packed, width)
    scores = masked_scores(query, keyed, lengths)
    probs = jnp.exp(scores - top) / total
    grad_heads = grad_context.reshape(query.shape)
    grad_valued = jnp.einsum(
        "bhqk,bqhd->bkhd",
        probs.astype(jnp.bfloat16),
        grad_heads,
        preferred_element_type=jnp.float32,
    )
    grad_probs = jnp.einsum(
        "bqhd,bkhd->bhqk", grad_heads, valued, preferred_element_type=jnp.float32
    )
    grad_scores = (probs * (grad_probs - jnp.sum(probs * grad_probs, -1, keepdims=True))).astype(
        jnp.bfloat16
    )
    grad_query = jnp.einsum(
        "bhqk,bkhd->bqhd", grad_scores, keyed, preferred_element_type=jnp.float32
    ) * HD ** (-0.5)
    grad_keyed = jnp.einsum(
        "bhqk,bqhd->bkhd", grad_scores, query, preferred_element_type=jnp.float32
    ) * HD ** (-0.5)
    grad_packed = jnp.concatenate(
        [piece.reshape(first_low.shape) for piece in (grad_query, grad_keyed, grad_valued)], -1
    )
    grad_packed = grad_packed.astype(jnp.bfloat16)
    g_qkv = weight_grad(first_low, grad_packed)
    grad_first = grad_joined + project_back(grad_packed, w_qkv)
    grad_embedded, gain_a, shift_a = norm_back(embedded, norms[:, 0], norms[:, 1], grad_first)
    g_positions = jnp.sum(grad_embedded, 0)
    g_norms = jnp.stack([gain_a, shift_a, gain_b, shift_b, gain_c, shift_c], -1)
    return (grad_embedded, g_positions, g_qkv, g_out, g_up, g_down, g_norms)


def per_device(
    ids,
    lengths,
    picks,
    labels,
    s_table,
    s_pos,
    s_qkv,
    s_out,
    s_up,
    s_down,
    s_norms,
    m_table,
    m_pos,
    m_qkv,
    m_out,
    m_up,
    m_down,
    m_norms,
    a_table,
    a_pos,
    a_qkv,
    a_out,
    a_up,
    a_down,
    a_norms,
    t_table,
    t_pos,
    t_qkv,
    t_out,
    t_up,
    t_down,
    t_norms,
):
    masters = (s_table, s_pos, s_qkv, s_out, s_up, s_down, s_norms)
    momenta = (m_table, m_pos, m_qkv, m_out, m_up, m_down, m_norms)
    averages = (a_table, a_pos, a_qkv, a_out, a_up, a_down, a_norms)
    f32, bf16 = jnp.float32, jnp.bfloat16
    fsdp = lax.axis_size(FSDP)
    width, t_width = s_table.shape[1], t_table.shape[2]
    vocab_own = s_table.shape[0]
    picked = picks.shape[1]
    span = ids.shape[1]

    facts = jnp.concatenate([ids, picks, labels, lengths[:, None]], axis=1)

    def taken_apart(gathered):
        i, p, l, n = jnp.split(gathered, [span, span + picked, span + 2 * picked], axis=1)
        return i, p, l, n[:, 0]

    group_ids, group_picks, _, group_lengths = taken_apart(
        lax.all_gather(facts, "grp", axis=0, tiled=True)
    )
    teacher_rows = lax.all_gather(t_table[0], FSDP, axis=0, tiled=True)
    plane_ids, plane_picks, plane_labels, plane_lengths = taken_apart(
        lax.all_gather(facts, FSDP, axis=0, tiled=True)
    )

    lead = s_qkv.shape[0]
    cols = [s_qkv, s_out, s_up, s_down.reshape(lead, -1), s_pos.reshape(lead, -1), s_norms]
    widths = [c.shape[1] for c in cols]
    packed_width = -(-sum(widths) // 128) * 128
    starts = [sum(widths[:k]) for k in range(len(widths))]

    def pack(parts):
        pad = jnp.zeros((parts[0].shape[0], packed_width - sum(widths)), bf16)
        return jnp.concatenate([part.astype(bf16) for part in parts] + [pad], axis=1)

    own_packed, own_table, own_head, _ = lax.optimization_barrier(
        (pack(cols), s_table.astype(bf16), t_table[0], teacher_rows)
    )
    packed = lax.all_gather(own_packed, FSDP, axis=0, tiled=True)
    whole = [packed[:, at : at + w] for at, w in zip(starts, widths)]
    w_qkv, w_out, w_up, w_down, positions, norms = whole
    w_down = w_down.reshape(-1, width)
    positions = positions.reshape(-1, width)
    student = (w_qkv, w_out, w_up, w_down, norms)
    table = lax.all_gather(own_table, FSDP, axis=0, tiled=True)
    heads = lax.all_gather(own_head, "grp", axis=0, tiled=False)

    teacher = (t_qkv[0], t_out[0], t_up[0], t_down[0], t_norms[0])
    t_embedded = jnp.take(teacher_rows, group_ids, axis=0).astype(f32) + t_pos[0].astype(f32)[None]
    teacher_final, _ = forward(t_embedded, group_lengths, teacher)
    taken = jnp.take_along_axis(teacher_final, group_picks[:, :, None], axis=1).astype(bf16)
    rows = lax.all_to_all(taken, "grp", split_axis=0, concat_axis=0, tiled=True)
    rows = lax.all_gather(rows, FSDP, axis=0, tiled=False)

    table, _ = lax.optimization_barrier((table, taken))
    embedded = jnp.take(table, ids, axis=0).astype(f32) + positions.astype(f32)[None]
    final, saved = forward(embedded, lengths, student)
    own_rows = jnp.take_along_axis(final, picks[:, :, None], axis=1).astype(bf16)[0]
    h = lax.all_gather(own_rows, FSDP, axis=0, tiled=True)
    z = jnp.einsum("rd,vd->rv", h, own_table, preferred_element_type=f32)

    logits = jnp.einsum("fkpd,kvd->kfpv", rows, heads, preferred_element_type=f32)
    logits = logits.reshape(logits.shape[0], -1, vocab_own)
    base = lax.axis_index(FSDP) * vocab_own
    column = lax.broadcasted_iota(jnp.int32, (1, 1, vocab_own), 2) + base
    at_label = column == plane_labels.reshape(1, -1, 1)
    top = jnp.max(logits, -1)
    spread = jnp.exp(logits - top[..., None])
    stats = [
        top,
        jnp.sum(spread, -1),
        jnp.sum(spread * logits, -1),
        jnp.sum(jnp.where(at_label, logits, 0.0), -1),
    ]
    z_top = jnp.max(z, -1)
    z_stats = [z_top, jnp.sum(jnp.exp(z - z_top[:, None]), -1)]
    sent = jnp.concatenate(stats + [s[None] for s in z_stats], axis=0)
    sent = jnp.moveaxis(sent.reshape(-1, fsdp, picked), 1, 0)
    seen = lax.all_to_all(sent, FSDP, split_axis=0, concat_axis=0, tiled=True)
    tops, sums, dots, hits = [seen[:, 4 * j : 4 * j + 4] for j in range(4)]

    def log_sum(tops, sums):
        best = jnp.max(tops, 0)
        scale = jnp.exp(tops - best)
        return best, scale, jnp.sum(sums * scale, 0)

    best, scale, total = log_sum(tops, sums)
    t_lse = best + jnp.log(total)
    t_ent = jnp.sum(dots * scale, 0) / total - t_lse
    label_logp = jnp.sum(hits, 0) - t_lse
    s_best, _, s_total = log_sum(seen[:, 16], seen[:, 17])
    s_lse = s_best + jnp.log(s_total)
    counted = (picks < lengths[:, None]).astype(f32)[0]
    count_local = jnp.sum(counted)
    label_loss = -jnp.sum(counted[None] * label_logp, -1) / jnp.maximum(count_local, 1.0)
    log_blend = jax.nn.log_softmax(-label_loss)
    blend = jax.nn.softmax(-label_loss)
    entropy = jnp.sum((blend[:, None] * t_ent).astype(bf16).astype(f32), 0)
    shift = jnp.concatenate([log_blend[:, None] - t_lse, s_lse[None]], axis=0)
    shift = jnp.moveaxis(from_everyone(shift, FSDP), 0, 1).reshape(5, -1)

    plane_counted = (plane_picks < plane_lengths[:, None]).astype(f32).reshape(-1)
    target = jnp.sum(jnp.exp(logits + shift[:4, :, None]).astype(bf16).astype(f32), 0)
    loss_local = jnp.sum(counted * (entropy + s_lse)) - jnp.sum(
        plane_counted * jnp.sum(target * z, -1)
    )
    grad_logits = (plane_counted[:, None] * (jnp.exp(z - shift[4][:, None]) - target)).astype(bf16)
    grad_rows = jnp.einsum("rv,vd->rd", grad_logits, own_table, preferred_element_type=f32)
    grad_rows = sum_and_scatter(grad_rows.astype(bf16).reshape(fsdp, picked, width))
    head_grad = jnp.einsum("rv,rd->vd", grad_logits, h, preferred_element_type=f32)

    loss_count = sum_of_groups(jnp.stack([loss_local, count_local]))
    grad_final = jnp.zeros(final.shape, f32).at[0, picks[0]].add(grad_rows)
    terms = backward(lengths, student, saved, grad_final)
    grad_embedded = terms[0]
    everyones = lax.all_gather(grad_embedded[0].astype(bf16), FSDP, axis=0, tiled=True)
    own_id = lax.broadcasted_iota(jnp.int32, (vocab_own, 1), 0) + base
    at_id = (own_id == plane_ids.reshape(1, -1)).astype(bf16)
    g_lookup = jnp.dot(at_id, everyones, preferred_element_type=f32)
    table_part = (head_grad + g_lookup).astype(bf16)
    g_pos, g_qkv, g_out, g_up, g_down, g_norms = terms[1:]
    whole_lead = g_qkv.shape[0]
    parts = pack(
        [g_qkv, g_out, g_up, g_down.reshape(whole_lead, -1), g_pos.reshape(whole_lead, -1), g_norms]
    )
    rest = sum_and_scatter(parts.reshape(fsdp, lead, packed_width)).astype(bf16)
    table_sum, rest_sum = lax.psum((table_part, rest), "grp")
    table_sum, rest_sum = table_sum.astype(f32), rest_sum.astype(f32)
    squares = jnp.sum(table_sum * table_sum) + jnp.sum(rest_sum * rest_sum)
    scalars = jnp.concatenate([squares[None], loss_count])
    scalars = from_everyone(scalars, FSDP).sum(0)
    squares, loss_sum, count = scalars[0], scalars[1], scalars[2]
    r_qkv, r_out, r_up, r_down, r_pos, r_norms = [
        rest_sum[:, at : at + w] for at, w in zip(starts, widths)
    ]
    shards = (
        table_sum,
        r_pos.reshape(s_pos.shape),
        r_qkv,
        r_out,
        r_up,
        r_down.reshape(s_down.shape),
        r_norms,
    )
    clip_norm = jnp.sqrt(squares) / count
    factor = jnp.minimum(1.0, clip_limit / clip_norm) / count
    new_weights, new_moments, new_averages = ([], [], [])
    for weight, moment, average, grad in zip(masters, momenta, averages, shards):
        clipped = grad * factor
        moment_new = momentum_decay * moment + clipped
        weight_new = weight - learn_rate * (clipped + momentum_decay * moment_new)
        new_weights.append(weight_new)
        new_moments.append(moment_new)
        new_averages.append(average_decay * average + (1.0 - average_decay) * weight_new)
    return (
        (loss_sum, count, clip_norm) + tuple(new_weights) + tuple(new_moments) + tuple(new_averages)
    )


def solution(mesh):
    finer = Mesh(
        mesh.devices.reshape(mesh.shape["grp"], 4, 4, 2), ("grp", "y", "x", "c")
    )
    return jax.shard_map(
        per_device,
        mesh=finer,
        in_specs=(
            P(GRP_FSDP, None),
            P(GRP_FSDP),
            P(GRP_FSDP, None),
            P(GRP_FSDP, None),
            P(FSDP, None),
            P(FSDP, None),
            P(FSDP, None),
            P(FSDP, None),
            P(FSDP, None),
            P(FSDP, None),
            P(FSDP, None),
            P(FSDP, None),
            P(FSDP, None),
            P(FSDP, None),
            P(FSDP, None),
            P(FSDP, None),
            P(FSDP, None),
            P(FSDP, None),
            P(FSDP, None),
            P(FSDP, None),
            P(FSDP, None),
            P(FSDP, None),
            P(FSDP, None),
            P(FSDP, None),
            P(FSDP, None),
            P("grp", FSDP, None),
            P("grp", None, None),
            P("grp", None, None),
            P("grp", None, None),
            P("grp", None, None),
            P("grp", None, None),
            P("grp", None, None),
        ),
        out_specs=(
            P(),
            P(),
            P(),
            P(FSDP, None),
            P(FSDP, None),
            P(FSDP, None),
            P(FSDP, None),
            P(FSDP, None),
            P(FSDP, None),
            P(FSDP, None),
            P(FSDP, None),
            P(FSDP, None),
            P(FSDP, None),
            P(FSDP, None),
            P(FSDP, None),
            P(FSDP, None),
            P(FSDP, None),
            P(FSDP, None),
            P(FSDP, None),
            P(FSDP, None),
            P(FSDP, None),
            P(FSDP, None),
            P(FSDP, None),
            P(FSDP, None),
        ),
        check_vma=False,
    )
```

```python
import math
from functools import partial

import jax
import jax.numpy as jnp
from jax import lax
from jax.experimental import pallas as pl
from jax.experimental.pallas import tpu as pltpu
from jax.sharding import Mesh
from jax.sharding import PartitionSpec as P

HD = 64
FSDP = ("y", "x", "c")
GRP_FSDP = ("grp", "y", "x", "c")
T_ROOM = 48
S_ROOM = 24

norm_eps = 1e-12
clip_limit = 0.001
learn_rate = 100000.0
momentum_decay = 0.9
average_decay = 0.9


SIZES = {"y": 4, "x": 4, "c": 2}
MESH = pl.DeviceIdType.MESH
ANY = pl.BlockSpec(memory_space=pl.ANY)
VMEM = pl.BlockSpec(memory_space=pltpu.VMEM)
AROUND = [((11 * k) % 32 // 8, (11 * k) % 8 // 2, (11 * k) % 2) for k in range(1, 32)]


def here():
    return {axis: lax.axis_index(axis) for axis in SIZES}


def moved(me, dy, dx, dc):
    return {
        "y": lax.rem(me["y"] + dy, 4),
        "x": lax.rem(me["x"] + dx, 4),
        "c": lax.rem(me["c"] + dc, 2),
    }


def number(place):
    return (place["y"] * 4 + place["x"]) * 2 + place["c"]


def greet(places):
    barrier = pltpu.get_barrier_semaphore()
    for place in places:
        pl.semaphore_signal(barrier, inc=1, device_id=place, device_id_type=MESH)
    pl.semaphore_wait(barrier, len(places))


def remote(source, target, sends, arrivals, at, place):
    copy = pltpu.make_async_remote_copy(
        src_ref=source,
        dst_ref=target,
        send_sem=sends.at[at],
        recv_sem=arrivals.at[at],
        device_id=place,
        device_id_type=MESH,
    )
    copy.start()
    return copy


def exchange_kernel(source, target, sends, arrivals, local):
    me = here()
    greet([moved(me, *step) for step in AROUND])
    copies = []
    for k, step in enumerate(AROUND):
        place = moved(me, *step)
        copies.append(
            remote(source.at[number(place)], target.at[number(me)], sends, arrivals, k, place)
        )
    own = pltpu.make_async_copy(source.at[number(me)], target.at[number(me)], local)
    own.start()
    own.wait()
    for copy in copies:
        copy.wait()


def exchange(value, collective):
    return pl.pallas_call(
        exchange_kernel,
        out_shape=jax.ShapeDtypeStruct(value.shape, value.dtype),
        in_specs=[ANY],
        out_specs=ANY,
        scratch_shapes=[
            pltpu.SemaphoreType.DMA((len(AROUND),)),
            pltpu.SemaphoreType.DMA((len(AROUND),)),
            pltpu.SemaphoreType.DMA,
        ],
        compiler_params=pltpu.CompilerParams(collective_id=collective, has_side_effects=True),
    )(value)


def group_exchange_kernel(source, target, sends, arrivals, local):
    group = lax.axis_index("grp")
    groups = [lax.rem(group + d, 4) for d in (1, 2, 3)]
    greet([{"grp": g} for g in groups])
    copies = [
        remote(source.at[g], target.at[group], sends, arrivals, d, {"grp": g})
        for d, g in enumerate(groups)
    ]
    own = pltpu.make_async_copy(source.at[group], target.at[group], local)
    own.start()
    own.wait()
    for copy in copies:
        copy.wait()


def exchange_groups(value, collective):
    return pl.pallas_call(
        group_exchange_kernel,
        out_shape=jax.ShapeDtypeStruct(value.shape, value.dtype),
        in_specs=[ANY],
        out_specs=ANY,
        scratch_shapes=[
            pltpu.SemaphoreType.DMA((3,)),
            pltpu.SemaphoreType.DMA((3,)),
            pltpu.SemaphoreType.DMA,
        ],
        compiler_params=pltpu.CompilerParams(collective_id=collective, has_side_effects=True),
    )(value)


def gather_kernel(source, target, sends, arrivals, local):
    me = here()
    chip, core = me["y"] * 4 + me["x"], me["c"]
    chips = [moved(me, (7 * k) % 16 // 4, (7 * k) % 4, 0) for k in range(1, 16)]
    sibling = moved(me, 0, 0, 1)
    greet(chips + [sibling])
    copies = [
        remote(source, target.at[chip, core], sends, arrivals, k, place)
        for k, place in enumerate(chips)
    ]
    own = pltpu.make_async_copy(source, target.at[chip, core], local)
    own.start()
    own.wait()
    for copy in copies:
        copy.wait()
    remote(target.at[:, core], target.at[:, core], sends, arrivals, 15, sibling).wait()


def gather_plane(value, collective):
    rows, width = value.shape
    out = pl.pallas_call(
        gather_kernel,
        out_shape=jax.ShapeDtypeStruct((16, 2, rows, width), value.dtype),
        in_specs=[ANY],
        out_specs=ANY,
        scratch_shapes=[
            pltpu.SemaphoreType.DMA((16,)),
            pltpu.SemaphoreType.DMA((16,)),
            pltpu.SemaphoreType.DMA,
        ],
        compiler_params=pltpu.CompilerParams(collective_id=collective, has_side_effects=True),
    )(value)
    return out.reshape(32 * rows, width)


def update_kernel(factor_ref, table_grad, rest_grad, norms_grad, *refs):
    masters, momenta, averages = refs[:7], refs[7:14], refs[14:21]
    outs = refs[21:]
    factor = factor_ref[0, 0]

    def step(k, grad):
        clipped = grad * factor
        moment = momentum_decay * momenta[k][...] + clipped
        weight = masters[k][...] - learn_rate * (clipped + momentum_decay * moment)
        outs[k][...] = weight
        outs[7 + k][...] = moment
        outs[14 + k][...] = average_decay * averages[k][...] + (1.0 - average_decay) * weight

    step(0, table_grad[...].astype(jnp.float32))

    @pl.when(pl.program_id(0) == 0)
    def _():
        width = rest_grad.shape[1]
        at = 0
        for k in (2, 3, 4, 5):
            rows, columns = masters[k].shape
            blocks = []
            for _ in range(columns // width):
                blocks.append(rest_grad[at : at + rows].astype(jnp.float32))
                at += rows
            step(k, blocks[0] if len(blocks) == 1 else jnp.concatenate(blocks, axis=1))
        step(1, rest_grad[at : at + 16].astype(jnp.float32)[: masters[1].shape[0]])
        step(6, norms_grad[...])


def update(factor, table_grad, rest_grad, norms_grad, masters, momenta, averages):
    steps = 5
    rows, width = table_grad.shape

    def whole(shape):
        return pl.BlockSpec(shape, lambda i: (0, 0))

    tall = pl.BlockSpec((rows // steps, width), lambda i: (i, 0))
    states = [tall] + [whole(m.shape) for m in masters[1:]]
    outs = pl.pallas_call(
        update_kernel,
        grid=(steps,),
        out_shape=[jax.ShapeDtypeStruct(m.shape, m.dtype) for m in masters] * 3,
        in_specs=[
            pl.BlockSpec(memory_space=pltpu.SMEM),
            tall,
            whole(rest_grad.shape),
            whole(norms_grad.shape),
        ]
        + states * 3,
        out_specs=states * 3,
        compiler_params=pltpu.CompilerParams(vmem_limit_bytes=40 * 2**20),
    )(factor.reshape(1, 1), table_grad, rest_grad, norms_grad, *masters, *momenta, *averages)
    return tuple(outs)


def scatter_sum_kernel(plan, *refs):
    f32, bf16 = jnp.float32, jnp.bfloat16
    parts, refs = refs[: len(plan)], refs[len(plan) :]
    out, own, other, both, in_a, in_b, mid_a, mid_b, end_a, end_b, sends, arrivals, local = refs
    me = here()
    steps_x = [moved(me, 0, d, 0) for d in (1, 2, 3)]
    steps_y = [moved(me, d, 0, 0) for d in (1, 2, 3)]
    sibling = moved(me, 0, 0, 1)
    greet([sibling] + steps_x + steps_y)
    copies, at, k = [], 0, 13
    width = own.shape[-1]
    for part, (rows, columns) in zip(parts, plan):
        for column in range(0, columns, width):
            span = (slice(None), pl.ds(at, rows))
            cols = pl.ds(column, width)
            copies.append(
                remote(
                    part.at[:, sibling["c"], :, cols],
                    other.at[span],
                    sends,
                    arrivals,
                    k,
                    sibling,
                )
            )
            mine = pltpu.make_async_copy(
                part.at[:, me["c"], :, cols], own.at[span], local.at[k - 13]
            )
            mine.start()
            copies.append(mine)
            at += rows
            k += 1
    for copy in copies:
        copy.wait()

    @pl.loop(0, 16)
    def _(k):
        both[k // 4, lax.rem(k, 4)] = (own[k].astype(f32) + other[k].astype(f32)).astype(bf16)

    cut = in_a.shape[-1]
    left, right = pl.ds(0, cut), pl.ds(cut, width - cut)
    copies = []
    for d in range(3):
        to_x, to_y = steps_x[d], steps_y[d]
        copies.append(
            remote(both.at[:, to_x["x"], :, left], in_a.at[d], sends, arrivals, 1 + d, to_x)
        )
        copies.append(
            remote(both.at[to_y["y"], :, :, right], in_b.at[d], sends, arrivals, 4 + d, to_y)
        )
    for copy in copies:
        copy.wait()

    @pl.loop(0, 4)
    def _(k):
        total_a = both[k, me["x"], :, left].astype(f32)
        total_b = both[me["y"], k, :, right].astype(f32)
        for d in range(3):
            total_a += in_a[d, k].astype(f32)
            total_b += in_b[d, k].astype(f32)
        mid_a[k] = total_a.astype(bf16)
        mid_b[k] = total_b.astype(bf16)

    copies = []
    for d in range(3):
        to_x, to_y = steps_x[d], steps_y[d]
        copies.append(remote(mid_a.at[to_y["y"]], end_a.at[d], sends, arrivals, 7 + d, to_y))
        copies.append(remote(mid_b.at[to_x["x"]], end_b.at[d], sends, arrivals, 10 + d, to_x))
    for copy in copies:
        copy.wait()
    total_a = mid_a[me["y"]].astype(f32)
    total_b = mid_b[me["x"]].astype(f32)
    for d in range(3):
        total_a += end_a[d].astype(f32)
        total_b += end_b[d].astype(f32)
    out[:, left] = total_a.astype(out.dtype)
    out[:, right] = total_b.astype(out.dtype)


def sum_and_scatter(parts, width, dtype, collective):
    plan = [part.shape[1:] for part in parts]
    rows = sum(r * (c // width) for r, c in plan)
    pieces = sum(c // width for _, c in plan)
    cut = width // 2
    rest = width - cut
    bf16 = jnp.bfloat16
    return pl.pallas_call(
        partial(scatter_sum_kernel, plan),
        out_shape=jax.ShapeDtypeStruct((rows, width), dtype),
        in_specs=[ANY] * len(parts),
        out_specs=VMEM,
        scratch_shapes=[
            pltpu.VMEM((16, rows, width), bf16),
            pltpu.VMEM((16, rows, width), bf16),
            pltpu.VMEM((4, 4, rows, width), bf16),
            pltpu.VMEM((3, 4, rows, cut), bf16),
            pltpu.VMEM((3, 4, rows, rest), bf16),
            pltpu.VMEM((4, rows, cut), bf16),
            pltpu.VMEM((4, rows, rest), bf16),
            pltpu.VMEM((3, rows, cut), bf16),
            pltpu.VMEM((3, rows, rest), bf16),
            pltpu.SemaphoreType.DMA((13 + pieces,)),
            pltpu.SemaphoreType.DMA((13 + pieces,)),
            pltpu.SemaphoreType.DMA((pieces,)),
        ],
        compiler_params=pltpu.CompilerParams(
            collective_id=collective, has_side_effects=True, vmem_limit_bytes=40 * 2**20
        ),
    )(*[part.reshape(16, 2, *part.shape[1:]) for part in parts])


def group_sum_kernel(
    table, rest, facts, table_out, rest_out, seen, table_in, rest_in, told, sends, arrivals, local
):
    f32, bf16 = jnp.float32, jnp.bfloat16
    me = here()
    group = lax.axis_index("grp")
    groups = [{"grp": lax.rem(group + d, 4)} for d in (1, 2, 3)]
    plane = [moved(me, *step) for step in AROUND]
    greet(groups + plane)

    def quarter(g):
        return pl.ds(pl.multiple_of(g * 128, 128), 128)

    mine = quarter(group)
    copies = []
    for d in range(3):
        theirs = quarter(groups[d]["grp"])
        copies.append(remote(table.at[:, theirs], table_in.at[d], sends, arrivals, d, groups[d]))
        copies.append(remote(rest.at[:, theirs], rest_in.at[d], sends, arrivals, 3 + d, groups[d]))
    for copy in copies:
        copy.wait()

    def summed(source, arrived, target):
        rows = 16

        def body(k, squares):
            at = pl.ds(pl.multiple_of(k * rows, rows), rows)
            total = source[at, mine].astype(f32)
            for d in range(3):
                total += arrived[d, at].astype(f32)
            total = total.astype(bf16)
            target[at, mine] = total
            total = total.astype(f32)
            total = total * total
            return squares + total[:8] + total[8:]

        return lax.fori_loop(0, source.shape[0] // rows, body, jnp.zeros((8, 128), f32))

    squares = summed(table, table_in, table_out) + summed(rest, rest_in, rest_out)
    told[group, 0:8] = squares
    told[group, 8:16] = facts[...]
    copies = []
    for d in range(3):
        copies.append(
            remote(told.at[group], told.at[group], sends, arrivals, 6 + d, groups[d])
        )
    wide = []
    for d in range(3):
        wide.append(
            remote(table_out.at[:, mine], table_out.at[:, mine], sends, arrivals, 9 + d, groups[d])
        )
        wide.append(
            remote(rest_out.at[:, mine], rest_out.at[:, mine], sends, arrivals, 12 + d, groups[d])
        )
    for copy in copies:
        copy.wait()
    seen[number(me)] = told[0] + told[1] + told[2] + told[3]
    copies = []
    for k, place in enumerate(plane):
        copies.append(
            remote(seen.at[number(me)], seen.at[number(me)], sends, arrivals, 15 + k, place)
        )
    for copy in copies + wide:
        copy.wait()


def sum_of_groups(table, rest, facts, collective):
    count = 15 + len(AROUND)
    return pl.pallas_call(
        group_sum_kernel,
        out_shape=[
            jax.ShapeDtypeStruct(table.shape, table.dtype),
            jax.ShapeDtypeStruct(rest.shape, rest.dtype),
            jax.ShapeDtypeStruct((32, 16, 128), jnp.float32),
        ],
        in_specs=[VMEM, VMEM, VMEM],
        out_specs=[VMEM, VMEM, VMEM],
        scratch_shapes=[
            pltpu.VMEM((3, table.shape[0], 128), table.dtype),
            pltpu.VMEM((3, rest.shape[0], 128), rest.dtype),
            pltpu.VMEM((4, 16, 128), jnp.float32),
            pltpu.SemaphoreType.DMA((count,)),
            pltpu.SemaphoreType.DMA((count,)),
            pltpu.SemaphoreType.DMA,
        ],
        compiler_params=pltpu.CompilerParams(
            collective_id=collective, has_side_effects=True, vmem_limit_bytes=40 * 2**20
        ),
    )(table, rest, facts)


def slots(tokens, own_rows):
    count = tokens.shape[0]
    row, column = tokens[:, None], tokens[None, :]
    place = jnp.arange(count)
    repeated = jnp.any((row == column) & (place[:, None] < place[None, :]), axis=0)
    owner = tokens // own_rows
    counts = ~repeated[:, None] & (row >= (owner * own_rows)[None, :]) & (row < column)
    return owner, ~repeated, jnp.sum(counts.astype(jnp.int32), axis=0)


def slot_in_round(owner, rank, room, turn):
    at = rank - turn * room
    return jnp.where((at >= 0) & (at < room), owner * room + at, -1)


def wanted_rows(slot, first, local, places):
    hit = (jnp.where(first, slot, -1)[:, None] == jnp.arange(places)[None, :])
    return jnp.sum(jnp.where(hit, local[:, None] + 1, 0), axis=0) - 1


def one_hot(index, count):
    return (index[:, None] == jnp.arange(count)[None, :]).astype(jnp.bfloat16)


def product(left, right):
    return jnp.dot(left, right, preferred_element_type=jnp.float32)


def folded(rows):
    return jnp.concatenate(jnp.split(rows, 2, axis=2), axis=1)


def unfolded(rows):
    return jnp.concatenate(jnp.split(rows, 2, axis=1), axis=2)


def layer_norm(value, gain, shift):
    mean = jnp.mean(value, -1, keepdims=True)
    centred = value - mean
    var = jnp.mean(centred * centred, -1, keepdims=True)
    return centred * lax.rsqrt(var + norm_eps) * gain + shift


def norm_back(value, gain, shift, grad):
    _, pull = jax.vjp(layer_norm, value, gain, shift)
    return pull(grad)


def project(left, right):
    return jnp.einsum("blk,kn->bln", left, right, preferred_element_type=jnp.float32)


def project_back(grad, right):
    return jnp.einsum("bln,kn->blk", grad, right, preferred_element_type=jnp.float32)


def weight_grad(left, grad):
    return jnp.einsum("blk,bln->kn", left, grad, preferred_element_type=jnp.float32)


def split_heads(packed, width):
    batch, span = (packed.shape[0], packed.shape[1])
    return [
        packed[:, :, piece * width : (piece + 1) * width].reshape(batch, span, width // HD, HD)
        for piece in range(3)
    ]


def masked_scores(query, keyed, lengths):
    scores = jnp.einsum(
        "bqhd,bkhd->bhqk", query, keyed, preferred_element_type=jnp.float32
    ) * HD ** (-0.5)
    valid = jnp.arange(query.shape[1])[None, :] < lengths[:, None]
    return jnp.where(valid[:, None, None, :], scores, -1e30)


def forward(embedded, lengths, weights):
    w_qkv, w_out, w_up, w_down, norms = weights
    norms = norms.astype(jnp.float32)
    width = w_out.shape[1]
    first = layer_norm(embedded, norms[:, 0], norms[:, 1])
    first_low = first.astype(jnp.bfloat16)
    packed = project(first_low, w_qkv).astype(jnp.bfloat16)
    query, keyed, valued = split_heads(packed, width)
    scores = masked_scores(query, keyed, lengths)
    top = jnp.max(scores, -1, keepdims=True)
    total = jnp.sum(jnp.exp(scores - top), -1, keepdims=True)
    probs = (jnp.exp(scores - top) / total).astype(jnp.bfloat16)
    context = jnp.einsum("bhqk,bkhd->bqhd", probs, valued, preferred_element_type=jnp.float32)
    context = context.reshape(first.shape).astype(jnp.bfloat16)
    joined = first + project(context, w_out)
    second = layer_norm(joined, norms[:, 2], norms[:, 3])
    second_low = second.astype(jnp.bfloat16)
    hidden_pre = project(second_low, w_up)
    active = jax.nn.gelu(hidden_pre, approximate=False).astype(jnp.bfloat16)
    summed = second + project(active, w_down)
    final = layer_norm(summed, norms[:, 4], norms[:, 5])
    saved = (
        embedded,
        first_low,
        packed,
        top,
        total,
        context,
        joined,
        second_low,
        hidden_pre,
        active,
        summed,
    )
    return (final, saved)


def backward(lengths, weights, saved, grad_final):
    w_qkv, w_out, w_up, w_down, norms = weights
    norms = norms.astype(jnp.float32)
    (
        embedded,
        first_low,
        packed,
        top,
        total,
        context,
        joined,
        second_low,
        hidden_pre,
        active,
        summed,
    ) = saved
    width = w_out.shape[1]
    grad_summed, gain_c, shift_c = norm_back(summed, norms[:, 4], norms[:, 5], grad_final)
    grad_ffn = grad_summed.astype(jnp.bfloat16)
    g_down = weight_grad(active, grad_ffn)
    _, gelu_pull = jax.vjp(partial(jax.nn.gelu, approximate=False), hidden_pre)
    grad_up = gelu_pull(project_back(grad_ffn, w_down))[0].astype(jnp.bfloat16)
    g_up = weight_grad(second_low, grad_up)
    grad_second = grad_summed + project_back(grad_up, w_up)
    grad_joined, gain_b, shift_b = norm_back(joined, norms[:, 2], norms[:, 3], grad_second)
    grad_attn = grad_joined.astype(jnp.bfloat16)
    g_out = weight_grad(context, grad_attn)
    grad_context = project_back(grad_attn, w_out).astype(jnp.bfloat16)
    query, keyed, valued = split_heads(packed, width)
    scores = masked_scores(query, keyed, lengths)
    probs = jnp.exp(scores - top) / total
    grad_heads = grad_context.reshape(query.shape)
    grad_valued = jnp.einsum(
        "bhqk,bqhd->bkhd",
        probs.astype(jnp.bfloat16),
        grad_heads,
        preferred_element_type=jnp.float32,
    )
    grad_probs = jnp.einsum(
        "bqhd,bkhd->bhqk", grad_heads, valued, preferred_element_type=jnp.float32
    )
    grad_scores = (probs * (grad_probs - jnp.sum(probs * grad_probs, -1, keepdims=True))).astype(
        jnp.bfloat16
    )
    grad_query = jnp.einsum(
        "bhqk,bkhd->bqhd", grad_scores, keyed, preferred_element_type=jnp.float32
    ) * HD ** (-0.5)
    grad_keyed = jnp.einsum(
        "bhqk,bqhd->bkhd", grad_scores, query, preferred_element_type=jnp.float32
    ) * HD ** (-0.5)
    grad_packed = jnp.concatenate(
        [piece.reshape(first_low.shape) for piece in (grad_query, grad_keyed, grad_valued)], -1
    )
    grad_packed = grad_packed.astype(jnp.bfloat16)
    g_qkv = weight_grad(first_low, grad_packed)
    grad_first = grad_joined + project_back(grad_packed, w_qkv)
    grad_embedded, gain_a, shift_a = norm_back(embedded, norms[:, 0], norms[:, 1], grad_first)
    g_positions = jnp.sum(grad_embedded, 0)
    g_norms = jnp.stack([gain_a, shift_a, gain_b, shift_b, gain_c, shift_c], -1)
    return (grad_embedded, g_positions, g_qkv, g_out, g_up, g_down, g_norms)


def per_device(
    ids,
    lengths,
    picks,
    labels,
    s_table,
    s_pos,
    s_qkv,
    s_out,
    s_up,
    s_down,
    s_norms,
    m_table,
    m_pos,
    m_qkv,
    m_out,
    m_up,
    m_down,
    m_norms,
    a_table,
    a_pos,
    a_qkv,
    a_out,
    a_up,
    a_down,
    a_norms,
    t_table,
    t_pos,
    t_qkv,
    t_out,
    t_up,
    t_down,
    t_norms,
):
    masters = (s_table, s_pos, s_qkv, s_out, s_up, s_down, s_norms)
    momenta = (m_table, m_pos, m_qkv, m_out, m_up, m_down, m_norms)
    averages = (a_table, a_pos, a_qkv, a_out, a_up, a_down, a_norms)
    f32, bf16 = jnp.float32, jnp.bfloat16
    fsdp = lax.axis_size(FSDP)
    width, t_width = s_table.shape[1], t_table.shape[2]
    vocab_own = s_table.shape[0]
    picked = picks.shape[1]
    span = ids.shape[1]

    facts = jnp.concatenate([ids, picks, jnp.broadcast_to(lengths[:, None], (1, 64))], axis=1)
    facts = jnp.pad(facts.reshape(3, 128), ((0, 5), (0, 0)))
    facts = exchange_groups(jnp.broadcast_to(facts, (4, 8, 128)), 9)[:, :3].reshape(4, -1)
    group_ids, group_picks = facts[:, :span], facts[:, span : span + picked]
    group_lengths = facts[:, span + picked]
    own_table = s_table.astype(bf16)
    t_owner, t_first, t_rank = slots(group_ids.reshape(-1), vocab_own)
    s_owners, s_firsts, s_ranks = jax.vmap(lambda one: slots(one, vocab_own))(group_ids)
    my_group = lax.axis_index("grp")
    s_owner, s_first, s_rank = (
        lax.dynamic_index_in_dim(v, my_group, 0, keepdims=False)
        for v in (s_owners, s_firsts, s_ranks)
    )
    most = jnp.maximum(jnp.max(t_rank) // T_ROOM, jnp.max(s_ranks) // S_ROOM) + 1
    t_local = group_ids.reshape(-1) - t_owner * vocab_own
    s_local = ids[0] - s_owner * vocab_own

    def asked(turn):
        t_slot = slot_in_round(t_owner, t_rank, T_ROOM, turn)
        s_slot = slot_in_round(s_owner, s_rank, S_ROOM, turn)
        t_ask = wanted_rows(t_slot, t_first, t_local, fsdp * T_ROOM).reshape(fsdp, T_ROOM)
        s_ask = wanted_rows(s_slot, s_first, s_local, fsdp * S_ROOM).reshape(fsdp, S_ROOM)
        return t_slot, s_slot, t_ask, s_ask

    def answer(t_want, s_want):
        t_sent = product(one_hot(t_want.reshape(-1), vocab_own), t_table[0]).astype(bf16)
        s_sent = product(one_hot(s_want.reshape(-1), vocab_own), own_table).astype(bf16)
        return jnp.concatenate(
            [t_sent.reshape(fsdp, T_ROOM, t_width), folded(s_sent.reshape(fsdp, S_ROOM, width))],
            axis=2,
        )

    def placed(got, t_slot, s_slot):
        t_got = got[:, :, :t_width].reshape(-1, t_width)
        s_got = unfolded(got[:, :, t_width:]).reshape(-1, width)
        return (
            product(one_hot(t_slot, fsdp * T_ROOM), t_got),
            product(one_hot(s_slot, fsdp * S_ROOM), s_got),
        )

    def swap(value):
        return lax.all_to_all(value, FSDP, split_axis=0, concat_axis=0, tiled=True)

    def ask_again(turn):
        t_slot, s_slot, t_ask, s_ask = asked(turn)
        wants = swap(jnp.concatenate([t_ask, s_ask], axis=1))
        return t_slot, s_slot, wants[:, :T_ROOM], wants[:, T_ROOM:]

    def more_rows(state):
        turn, t_emb, s_emb = state
        t_slot, s_slot, t_want, s_want = ask_again(turn)
        t_more, s_more = placed(swap(answer(t_want, s_want)), t_slot, s_slot)
        return turn + 1, t_emb + t_more, s_emb + s_more

    t_slot, s_slot, t_ask, s_ask = asked(0)
    line = jnp.concatenate(
        [t_ask, s_ask, jnp.broadcast_to(most, (fsdp, 128 - T_ROOM - S_ROOM))], axis=1
    )
    lines = [
        line,
        jnp.broadcast_to(jnp.concatenate([picks, labels], axis=1), (fsdp, 2 * picked)),
        jnp.broadcast_to(lengths[:, None], (fsdp, 128)),
    ]
    notes = jnp.stack(lines + [jnp.zeros((fsdp, 128), jnp.int32)] * 5, axis=1)
    notes = exchange(notes, 1)
    t_want, s_want = notes[:, 0, :T_ROOM], notes[:, 0, T_ROOM : T_ROOM + S_ROOM]
    rounds = jnp.max(notes[:, 0, T_ROOM + S_ROOM])
    plane_picks, plane_labels = notes[:, 1, :picked], notes[:, 1, picked : 2 * picked]
    plane_lengths = notes[:, 2, 0]
    t_emb, s_emb = placed(exchange(answer(t_want, s_want), 2), t_slot, s_slot)
    _, t_emb, s_emb = lax.while_loop(
        lambda state: state[0] < rounds, more_rows, (jnp.int32(1), t_emb, s_emb)
    )

    def pieces(blocks, qkv, out, up, down, pos, norms):
        tail = norms.astype(f32).reshape(blocks, 1, -1)
        tail = jnp.pad(tail, ((0, 0), (0, 7), (0, width - tail.shape[2])))
        small = jnp.concatenate([pos.reshape(blocks, -1, width).astype(f32), tail], axis=1)
        big = [part.astype(bf16).reshape(blocks, -1, part.shape[1]) for part in (qkv, out, up, down)]
        return big + [lax.optimization_barrier(small.astype(bf16))]

    def pack(parts):
        columns = [
            part[:, :, at : at + width] for part in parts for at in range(0, part.shape[2], width)
        ]
        return jnp.concatenate(columns, axis=1)

    def unpack(packed):
        blocks, lead = packed.shape[0], s_qkv.shape[0]

        def across(at, count):
            return jnp.concatenate(
                [
                    packed[:, at + k * lead : at + (k + 1) * lead].reshape(-1, width)
                    for k in range(count)
                ],
                axis=1,
            )

        at_out = s_qkv.shape[1] // width * lead
        at_up = at_out + lead
        at_down = at_up + s_up.shape[1] // width * lead
        at_pos = at_down + s_down.shape[0]
        at_norms = at_pos + s_pos.shape[0]
        return (
            across(0, s_qkv.shape[1] // width),
            across(at_out, 1),
            across(at_up, s_up.shape[1] // width),
            packed[:, at_down:at_pos].reshape(-1, width),
            packed[:, at_pos:at_norms].reshape(-1, width),
            packed[:, at_norms, : s_norms.size].reshape(-1, s_norms.shape[1]),
        )

    own_packed = pack(pieces(1, s_qkv, s_out, s_up, s_down, s_pos, s_norms))
    w_qkv, w_out, w_up, w_down, positions, norms = unpack(
        lax.all_gather(own_packed, FSDP, axis=0, tiled=True)
    )
    student = (w_qkv, w_out, w_up, w_down, norms)
    heads = lax.all_gather(t_table[0], "grp", axis=0, tiled=False)

    teacher = (t_qkv[0], t_out[0], t_up[0], t_down[0], t_norms[0])
    t_embedded = t_emb.reshape(-1, span, t_width) + t_pos[0].astype(f32)[None]
    teacher_final, _ = forward(t_embedded, group_lengths, teacher)
    taken = jnp.take_along_axis(teacher_final, group_picks[:, :, None], axis=1).astype(bf16)
    taken, heads = lax.optimization_barrier((taken, heads))
    rows = exchange_groups(taken, 10)
    s_emb, rows = lax.optimization_barrier((s_emb, rows))
    rows = lax.all_gather(rows, FSDP, axis=0, tiled=False)

    embedded = s_emb[None] + positions.astype(f32)[None]
    final, saved = forward(embedded, lengths, student)
    own_rows = jnp.take_along_axis(final, picks[:, :, None], axis=1).astype(bf16)[0]
    h = gather_plane(own_rows, 11)
    z = jnp.einsum("rd,vd->rv", h, own_table, preferred_element_type=f32)

    logits = jnp.einsum("fkpd,kvd->kfpv", rows, heads, preferred_element_type=f32)
    logits = logits.reshape(logits.shape[0], -1, vocab_own)
    base = lax.axis_index(FSDP) * vocab_own
    column = lax.broadcasted_iota(jnp.int32, (1, 1, vocab_own), 2) + base
    at_label = column == plane_labels.reshape(1, -1, 1)
    top = jnp.max(logits, -1)
    spread = jnp.exp(logits - top[..., None])
    stats = [
        top,
        jnp.sum(spread, -1),
        jnp.sum(spread * logits, -1),
        jnp.sum(jnp.where(at_label, logits, 0.0), -1),
    ]
    z_top = jnp.max(z, -1)
    z_stats = [z_top, jnp.sum(jnp.exp(z - z_top[:, None]), -1)]
    sent = jnp.concatenate(stats + [s[None] for s in z_stats], axis=0)
    sent = jnp.moveaxis(sent.reshape(-1, fsdp, picked), 1, 0)
    sent = jnp.pad(sent, ((0, 0), (0, 24 - sent.shape[1]), (0, 128 - picked)))
    seen = exchange(sent, 3)[:, :, :picked]
    tops, sums, dots, hits = [seen[:, 4 * j : 4 * j + 4] for j in range(4)]

    def log_sum(tops, sums):
        best = jnp.max(tops, 0)
        scale = jnp.exp(tops - best)
        return best, scale, jnp.sum(sums * scale, 0)

    best, scale, total = log_sum(tops, sums)
    t_lse = best + jnp.log(total)
    t_ent = jnp.sum(dots * scale, 0) / total - t_lse
    label_logp = jnp.sum(hits, 0) - t_lse
    s_best, _, s_total = log_sum(seen[:, 16], seen[:, 17])
    s_lse = s_best + jnp.log(s_total)
    counted = (picks < lengths[:, None]).astype(f32)[0]
    count_local = jnp.sum(counted)
    label_loss = -jnp.sum(counted[None] * label_logp, -1) / jnp.maximum(count_local, 1.0)
    log_blend = jax.nn.log_softmax(-label_loss)
    blend = jax.nn.softmax(-label_loss)
    entropy = jnp.sum((blend[:, None] * t_ent).astype(bf16).astype(f32), 0)
    shift = jnp.concatenate([log_blend[:, None] - t_lse, s_lse[None]], axis=0)
    shift = jnp.pad(shift, ((0, 3), (0, 128 - picked)))
    shift = exchange(jnp.broadcast_to(shift, (fsdp, 8, 128)), 4)[:, :5, :picked]
    shift = jnp.moveaxis(shift, 0, 1).reshape(5, -1)

    plane_counted = (plane_picks < plane_lengths[:, None]).astype(f32).reshape(-1)
    target = jnp.sum(jnp.exp(logits + shift[:4, :, None]).astype(bf16).astype(f32), 0)
    loss_local = jnp.sum(counted * (entropy + s_lse)) - jnp.sum(
        plane_counted * jnp.sum(target * z, -1)
    )
    grad_logits = (plane_counted[:, None] * (jnp.exp(z - shift[4][:, None]) - target)).astype(bf16)
    grad_rows = jnp.einsum("rv,vd->rd", grad_logits, own_table, preferred_element_type=f32)
    grad_rows = sum_and_scatter([grad_rows.astype(bf16).reshape(fsdp, picked, width)], width, f32, 5)
    head_grad = jnp.einsum("rv,rd->vd", grad_logits, h, preferred_element_type=f32)

    grad_final = jnp.zeros(final.shape, f32).at[0, picks[0]].add(grad_rows)
    terms = backward(lengths, student, saved, grad_final)
    grad_embedded = terms[0]
    low_embedded = grad_embedded[0].astype(bf16)

    def given(s_slot):
        rows = product(one_hot(s_slot, fsdp * S_ROOM).T, low_embedded).astype(bf16)
        return folded(rows.reshape(fsdp, S_ROOM, width))

    def taken_in(got, s_want):
        rows = unfolded(got).reshape(-1, width)
        return product(one_hot(s_want.reshape(-1), vocab_own).T, rows)

    def more_grads(state):
        turn, total = state
        _, s_slot, _, s_want = ask_again(turn)
        return turn + 1, total + taken_in(swap(given(s_slot)), s_want)

    g_lookup = taken_in(exchange(given(s_slot), 6), s_want)
    _, g_table = lax.while_loop(
        lambda state: state[0] < rounds, more_grads, (jnp.int32(1), head_grad + g_lookup)
    )
    g_pos, g_qkv, g_out, g_up, g_down, g_norms = terms[1:]
    parts = pieces(fsdp, g_qkv, g_out, g_up, g_down, g_pos, g_norms)
    rest = sum_and_scatter(parts, width, bf16, 7)
    row = jnp.arange(8)[:, None]
    column_of = jnp.arange(128)[None, :]
    told = jnp.where((row == 0) & (column_of == 0), loss_local, 0.0)
    told += jnp.where((row == 1) & (column_of == 0), count_local, 0.0)
    table_sum, rest_sum, seen = sum_of_groups(g_table.astype(bf16), rest, told, 8)
    seen = seen.sum(0)
    squares, loss_sum, count = jnp.sum(seen[:8]), seen[8, 0], seen[9, 0]
    at_norms = rest_sum.shape[0] - 8
    norms_sum = rest_sum[at_norms, : s_norms.size].astype(f32).reshape(s_norms.shape)
    clip_norm = jnp.sqrt(squares) / count
    factor = jnp.minimum(1.0, clip_limit / clip_norm) / count
    return (loss_sum, count, clip_norm) + update(
        factor, table_sum, rest_sum, norms_sum, masters, momenta, averages
    )


def solution(mesh):
    finer = Mesh(
        mesh.devices.reshape(mesh.shape["grp"], 4, 4, 2), ("grp", "y", "x", "c")
    )
    return jax.shard_map(
        per_device,
        mesh=finer,
        in_specs=(
            P(GRP_FSDP, None),
            P(GRP_FSDP),
            P(GRP_FSDP, None),
            P(GRP_FSDP, None),
            P(FSDP, None),
            P(FSDP, None),
            P(FSDP, None),
            P(FSDP, None),
            P(FSDP, None),
            P(FSDP, None),
            P(FSDP, None),
            P(FSDP, None),
            P(FSDP, None),
            P(FSDP, None),
            P(FSDP, None),
            P(FSDP, None),
            P(FSDP, None),
            P(FSDP, None),
            P(FSDP, None),
            P(FSDP, None),
            P(FSDP, None),
            P(FSDP, None),
            P(FSDP, None),
            P(FSDP, None),
            P(FSDP, None),
            P("grp", FSDP, None),
            P("grp", None, None),
            P("grp", None, None),
            P("grp", None, None),
            P("grp", None, None),
            P("grp", None, None),
            P("grp", None, None),
        ),
        out_specs=(
            P(),
            P(),
            P(),
            P(FSDP, None),
            P(FSDP, None),
            P(FSDP, None),
            P(FSDP, None),
            P(FSDP, None),
            P(FSDP, None),
            P(FSDP, None),
            P(FSDP, None),
            P(FSDP, None),
            P(FSDP, None),
            P(FSDP, None),
            P(FSDP, None),
            P(FSDP, None),
            P(FSDP, None),
            P(FSDP, None),
            P(FSDP, None),
            P(FSDP, None),
            P(FSDP, None),
            P(FSDP, None),
            P(FSDP, None),
            P(FSDP, None),
        ),
        check_vma=False,
    )
```

```python
import functools
from functools import partial

import jax
import jax.numpy as jnp
from jax import lax
from jax.experimental import pallas as pl
from jax.experimental.pallas import tpu as pltpu
from jax.sharding import Mesh
from jax.sharding import PartitionSpec as P

HD = 64
FSDP = ("y", "x", "c")
GRP_FSDP = ("grp", "y", "x", "c")
T_ROOM = 48
S_ROOM = 24
WIDE = 56 * 2**20

norm_eps = 1e-12
clip_limit = 0.001
learn_rate = 100000.0
momentum_decay = 0.9
average_decay = 0.9


SIZES = {"y": 4, "x": 4, "c": 2}
MESH = pl.DeviceIdType.MESH
ANY = pl.BlockSpec(memory_space=pl.ANY)
VMEM = pl.BlockSpec(memory_space=pltpu.VMEM)
AROUND = [((11 * k) % 32 // 8, (11 * k) % 8 // 2, (11 * k) % 2) for k in range(1, 32)]


def here():
    return {axis: lax.axis_index(axis) for axis in SIZES}


def moved(me, dy, dx, dc):
    return {
        "y": lax.rem(me["y"] + dy, 4),
        "x": lax.rem(me["x"] + dx, 4),
        "c": lax.rem(me["c"] + dc, 2),
    }


def number(place):
    return (place["y"] * 4 + place["x"]) * 2 + place["c"]


def greet(places):
    barrier = pltpu.get_barrier_semaphore()
    for place in places:
        pl.semaphore_signal(barrier, inc=1, device_id=place, device_id_type=MESH)
    pl.semaphore_wait(barrier, len(places))


def remote(source, target, sends, arrivals, at, place):
    copy = pltpu.make_async_remote_copy(
        src_ref=source,
        dst_ref=target,
        send_sem=sends.at[at],
        recv_sem=arrivals.at[at],
        device_id=place,
        device_id_type=MESH,
    )
    copy.start()
    return copy


def exchange_kernel(source, target, sends, arrivals, local):
    me = here()
    greet([moved(me, *step) for step in AROUND])
    copies = []
    for k, step in enumerate(AROUND):
        place = moved(me, *step)
        copies.append(
            remote(source.at[number(place)], target.at[number(me)], sends, arrivals, k, place)
        )
    own = pltpu.make_async_copy(source.at[number(me)], target.at[number(me)], local)
    own.start()
    own.wait()
    for copy in copies:
        copy.wait()


def exchange(value, collective):
    return pl.pallas_call(
        exchange_kernel,
        out_shape=jax.ShapeDtypeStruct(value.shape, value.dtype),
        in_specs=[ANY],
        out_specs=ANY,
        scratch_shapes=[
            pltpu.SemaphoreType.DMA((len(AROUND),)),
            pltpu.SemaphoreType.DMA((len(AROUND),)),
            pltpu.SemaphoreType.DMA,
        ],
        compiler_params=pltpu.CompilerParams(collective_id=collective, has_side_effects=True),
    )(value)


def route_kernel(notes, t_table, s_table, heard, got, sent, sends, arrivals, local):
    f32, bf16 = jnp.float32, jnp.bfloat16
    me = here()
    greet([moved(me, *step) for step in AROUND])
    copies = []
    for k, step in enumerate(AROUND):
        place = moved(me, *step)
        copies.append(
            remote(notes.at[number(place)], heard.at[number(me)], sends, arrivals, k, place)
        )
    heard[number(me)] = notes[number(me)]
    for copy in copies:
        copy.wait()
    wants = heard[:, 0, :].astype(f32).T
    vocab, t_width = t_table.shape
    half = s_table.shape[1] // 2
    batch = 8

    def rows_of(at, room, peers, table):
        index = jnp.concatenate([wants[at : at + room, p : p + 1] for p in peers], axis=0)
        entry = lax.broadcasted_iota(jnp.int32, (index.shape[0], vocab), 1).astype(f32)
        hot = jnp.where(entry == index, 1.0, 0.0).astype(bf16)
        return product(hot, table[...])

    for first in range(0, 32, batch):
        peers = range(first, first + batch)
        t_rows = rows_of(0, T_ROOM, peers, t_table)
        s_rows = rows_of(T_ROOM, S_ROOM, peers, s_table)
        for j, p in enumerate(peers):
            sent[p, :, :t_width] = t_rows[j * T_ROOM : (j + 1) * T_ROOM].astype(bf16)
            own = s_rows[j * S_ROOM : (j + 1) * S_ROOM]
            own = jnp.concatenate([own[:, :half], own[:, half:]], axis=0)
            sent[p, :, t_width:] = own.astype(bf16)
    copies = []
    for k, step in enumerate(AROUND):
        place = moved(me, *step)
        copies.append(
            remote(
                sent.at[number(place)], got.at[number(me)], sends, arrivals, len(AROUND) + k, place
            )
        )
    mine = pltpu.make_async_copy(sent.at[number(me)], got.at[number(me)], local)
    mine.start()
    mine.wait()
    for copy in copies:
        copy.wait()


def route(notes, t_table, s_table, collective):
    width = t_table.shape[1] + s_table.shape[1] // 2
    return pl.pallas_call(
        route_kernel,
        out_shape=[
            jax.ShapeDtypeStruct(notes.shape, notes.dtype),
            jax.ShapeDtypeStruct((32, T_ROOM, width), jnp.bfloat16),
        ],
        in_specs=[VMEM, VMEM, VMEM],
        out_specs=[VMEM, ANY],
        scratch_shapes=[
            pltpu.VMEM((32, T_ROOM, width), jnp.bfloat16),
            pltpu.SemaphoreType.DMA((2 * len(AROUND),)),
            pltpu.SemaphoreType.DMA((2 * len(AROUND),)),
            pltpu.SemaphoreType.DMA,
        ],
        compiler_params=pltpu.CompilerParams(
            collective_id=collective, has_side_effects=True, vmem_limit_bytes=40 * 2**20
        ),
    )(notes, t_table, s_table)


def group_exchange_kernel(source, target, sends, arrivals, local):
    group = lax.axis_index("grp")
    groups = [lax.rem(group + d, 4) for d in (1, 2, 3)]
    greet([{"grp": g} for g in groups])
    copies = [
        remote(source.at[g], target.at[group], sends, arrivals, d, {"grp": g})
        for d, g in enumerate(groups)
    ]
    own = pltpu.make_async_copy(source.at[group], target.at[group], local)
    own.start()
    own.wait()
    for copy in copies:
        copy.wait()


def exchange_groups(value, collective):
    return pl.pallas_call(
        group_exchange_kernel,
        out_shape=jax.ShapeDtypeStruct(value.shape, value.dtype),
        in_specs=[ANY],
        out_specs=ANY,
        scratch_shapes=[
            pltpu.SemaphoreType.DMA((3,)),
            pltpu.SemaphoreType.DMA((3,)),
            pltpu.SemaphoreType.DMA,
        ],
        compiler_params=pltpu.CompilerParams(collective_id=collective, has_side_effects=True),
    )(value)


def gather_kernel(source, target, sends, arrivals, local):
    me = here()
    chip, core = me["y"] * 4 + me["x"], me["c"]
    chips = [moved(me, (7 * k) % 16 // 4, (7 * k) % 4, 0) for k in range(1, 16)]
    sibling = moved(me, 0, 0, 1)
    greet(chips + [sibling])
    copies = [
        remote(source, target.at[chip, core], sends, arrivals, k, place)
        for k, place in enumerate(chips)
    ]
    own = pltpu.make_async_copy(source, target.at[chip, core], local)
    own.start()
    own.wait()
    for copy in copies:
        copy.wait()
    remote(target.at[:, core], target.at[:, core], sends, arrivals, 15, sibling).wait()


def gather_plane(value, collective):
    rows, width = value.shape
    out = pl.pallas_call(
        gather_kernel,
        out_shape=jax.ShapeDtypeStruct((16, 2, rows, width), value.dtype),
        in_specs=[ANY],
        out_specs=ANY,
        scratch_shapes=[
            pltpu.SemaphoreType.DMA((16,)),
            pltpu.SemaphoreType.DMA((16,)),
            pltpu.SemaphoreType.DMA,
        ],
        compiler_params=pltpu.CompilerParams(collective_id=collective, has_side_effects=True),
    )(value)
    return out.reshape(32 * rows, width)


def update_kernel(factor_ref, table_grad, rest_grad, norms_grad, *refs):
    masters, momenta, averages = refs[:7], refs[7:14], refs[14:21]
    outs = refs[21:]
    factor = factor_ref[0, 0]

    def step(k, grad):
        clipped = grad * factor
        moment = momentum_decay * momenta[k][...] + clipped
        weight = masters[k][...] - learn_rate * (clipped + momentum_decay * moment)
        outs[k][...] = weight
        outs[7 + k][...] = moment
        outs[14 + k][...] = average_decay * averages[k][...] + (1.0 - average_decay) * weight

    step(0, table_grad[...].astype(jnp.float32))

    @pl.when(pl.program_id(0) == 0)
    def _():
        width = rest_grad.shape[1]
        at = 0
        for k in (2, 3, 4, 5):
            rows, columns = masters[k].shape
            blocks = []
            for _ in range(columns // width):
                blocks.append(rest_grad[at : at + rows].astype(jnp.float32))
                at += rows
            step(k, blocks[0] if len(blocks) == 1 else jnp.concatenate(blocks, axis=1))
        step(1, rest_grad[at : at + 16].astype(jnp.float32)[: masters[1].shape[0]])
        step(6, norms_grad[...])


def update(factor, table_grad, rest_grad, norms_grad, masters, momenta, averages):
    steps = 5
    rows, width = table_grad.shape

    def whole(shape):
        return pl.BlockSpec(shape, lambda i: (0, 0))

    tall = pl.BlockSpec((rows // steps, width), lambda i: (i, 0))
    states = [tall] + [whole(m.shape) for m in masters[1:]]
    outs = pl.pallas_call(
        update_kernel,
        grid=(steps,),
        out_shape=[jax.ShapeDtypeStruct(m.shape, m.dtype) for m in masters] * 3,
        in_specs=[
            pl.BlockSpec(memory_space=pltpu.SMEM),
            tall,
            whole(rest_grad.shape),
            whole(norms_grad.shape),
        ]
        + states * 3,
        out_specs=states * 3,
        compiler_params=pltpu.CompilerParams(vmem_limit_bytes=WIDE),
    )(factor.reshape(1, 1), table_grad, rest_grad, norms_grad, *masters, *momenta, *averages)
    return tuple(outs)


def normed(value, gain, shift):
    mean = jnp.mean(value, -1, keepdims=True)
    centred = value - mean
    var = jnp.mean(centred * centred, -1, keepdims=True)
    return centred * lax.rsqrt(var + norm_eps) * gain + shift


def teacher_kernel(
    lengths, slot, picks, got, extra, pos, norms, w_qkv, w_out, w_up, w_down, out, qkv, ctx
):
    f32, bf16 = jnp.float32, jnp.bfloat16
    span, width = pos.shape
    length = lengths[0, pl.program_id(0)]

    def pick(index, count):
        wide = lax.broadcasted_iota(jnp.int32, (index.shape[0], count), 1)
        return jnp.where(wide == index, 1.0, 0.0).astype(bf16)

    def scale(k):
        return norms[2 * k : 2 * k + 1], norms[2 * k + 1 : 2 * k + 2]

    emb = product(pick(slot[0], got.shape[0]), got[...])
    emb = emb + extra[0].astype(f32) + pos[...].astype(f32)
    first = normed(emb, *scale(0))
    qkv[...] = product(first.astype(bf16), w_qkv[...]).astype(bf16)
    lane = lax.broadcasted_iota(jnp.int32, (span, 2 * HD), 1)
    halves = [jnp.where(lane < HD, 1.0, 0.0), jnp.where(lane < HD, 0.0, 1.0)]
    valid = lax.broadcasted_iota(jnp.int32, (span, span), 1) < length
    for pair in range(width // (2 * HD)):
        at = 2 * HD * pair
        query = qkv[:, at : at + 2 * HD]
        keyed = qkv[:, width + at : width + at + 2 * HD]
        valued = qkv[:, 2 * width + at : 2 * width + at + 2 * HD]
        total = jnp.zeros((span, 2 * HD), f32)
        for half in halves:
            scores = lax.dot_general(
                query * half.astype(bf16),
                keyed,
                (((1,), (1,)), ((), ())),
                preferred_element_type=f32,
            ) * HD ** (-0.5)
            scores = jnp.where(valid, scores, -1e30)
            spread = jnp.exp(scores - jnp.max(scores, -1, keepdims=True))
            probs = spread * (1.0 / jnp.sum(spread, -1, keepdims=True))
            total += half * product(probs.astype(bf16), valued)
        ctx[:, at : at + 2 * HD] = total.astype(bf16)
    second = normed(first + product(ctx[...], w_out[...]), *scale(1))
    low = second.astype(bf16)
    ffn = jnp.zeros((span, width), f32)
    for at in range(0, w_up.shape[1], width):
        pre = product(low, w_up[:, at : at + width])
        active = (0.5 * pre * (1.0 + lax.erf(pre * (0.5**0.5)))).astype(bf16)
        ffn += product(active, w_down[at : at + width, :])
    final = normed(second + ffn, *scale(2))
    out[0] = product(pick(picks[0], span), final.astype(bf16)).astype(bf16)


def teacher_rows(lengths, slot, picks, got, extra, pos, norms, w_qkv, w_out, w_up, w_down):
    count, picked = picks.shape
    span, width = pos.shape

    def whole(array, *shape):
        shape = shape or array.shape
        return pl.BlockSpec(shape, lambda i: (0,) * len(shape), pipeline_mode=pl.Buffered(1))

    def each(*shape):
        return pl.BlockSpec((1,) + shape, lambda i: (i, 0, 0))

    return pl.pallas_call(
        teacher_kernel,
        grid=(count,),
        out_shape=jax.ShapeDtypeStruct((count, picked, width), jnp.bfloat16),
        in_specs=[
            pl.BlockSpec(memory_space=pltpu.SMEM),
            each(span, 1),
            each(picked, 1),
            whole(got, got.shape[0], width),
            each(span, width),
            whole(pos),
            whole(norms),
            whole(w_qkv),
            whole(w_out),
            whole(w_up),
            whole(w_down),
        ],
        out_specs=each(picked, width),
        scratch_shapes=[
            pltpu.VMEM((span, 3 * width), jnp.bfloat16),
            pltpu.VMEM((span, width), jnp.bfloat16),
        ],
        compiler_params=pltpu.CompilerParams(vmem_limit_bytes=WIDE),
    )(
        lengths[None],
        slot.reshape(count, span, 1),
        picks[:, :, None],
        got,
        extra,
        pos,
        norms,
        w_qkv,
        w_out,
        w_up,
        w_down,
    )


DEEP = 64
WING = 256


def by_eight(value):
    return value.reshape(value.shape[0] // 8, 8, value.shape[1])


def logits_kernel(labels, rows, head, out, stats):
    f32 = jnp.float32
    taken = rows[...].reshape(-1, rows.shape[-1])
    vocab = out.shape[1]
    parts = []
    for at in range(0, taken.shape[0], WING):
        logits = lax.dot_general(
            head[0], taken[at : at + WING], (((1,), (1,)), ((), ())), preferred_element_type=f32
        )
        out[0, :, at : at + WING] = logits
        parts.append(logits)
    for k, logits in enumerate(parts):
        cols = slice(k * WING, (k + 1) * WING)
        top = jnp.max(jnp.max(by_eight(logits), 0), 0, keepdims=True)
        row = lax.broadcasted_iota(jnp.int32, (DEEP, WING), 0) - labels[:, cols]
        totals = [jnp.zeros((8, WING), f32)] * 3
        for deep in range(0, vocab, DEEP):
            part = logits[deep : deep + DEEP]
            spread = jnp.exp(part - top)
            hit = jnp.where(row == -deep, part, 0.0)
            totals = [
                total + jnp.sum(by_eight(more), 0)
                for total, more in zip(totals, (spread, spread * part, hit))
            ]
        lines = [top] + [jnp.sum(total, 0, keepdims=True) for total in totals]
        stats[0, :, cols] = jnp.concatenate(lines, axis=0)


def vocabulary_logits(labels, rows, heads):
    devices, count, picked, width = rows.shape
    vocab = heads.shape[1]
    block = 2 * WING // picked
    wide = block * picked
    return pl.pallas_call(
        logits_kernel,
        grid=(count, devices // block),
        out_shape=[
            jax.ShapeDtypeStruct((count, vocab, devices * picked), jnp.float32),
            jax.ShapeDtypeStruct((count, 4, devices * picked), jnp.float32),
        ],
        in_specs=[
            pl.BlockSpec((1, wide), lambda k, j: (0, j)),
            pl.BlockSpec((block, 1, picked, width), lambda k, j: (j, k, 0, 0)),
            pl.BlockSpec((1, vocab, width), lambda k, j: (k, 0, 0)),
        ],
        out_specs=[
            pl.BlockSpec((1, vocab, wide), lambda k, j: (k, 0, j)),
            pl.BlockSpec((1, 4, wide), lambda k, j: (k, 0, j)),
        ],
        compiler_params=pltpu.CompilerParams(vmem_limit_bytes=WIDE),
    )(labels, rows, heads)


def blend_kernel(stats, counted_ref, shift, loss, seen, sends, arrivals, local):
    f32, bf16 = jnp.float32, jnp.bfloat16
    me = here()
    greet([moved(me, *step) for step in AROUND])

    def columns(place):
        chip = place["y"] * 4 + place["x"]
        return stats.at[:, :, pl.ds(pl.multiple_of(chip * 128, 128), 128)]

    copies = []
    for k, step in enumerate(AROUND):
        place = moved(me, *step)
        copies.append(remote(columns(place), seen.at[number(me)], sends, arrivals, k, place))
    own = pltpu.make_async_copy(columns(me), seen.at[number(me)], local)
    own.start()
    own.wait()
    for copy in copies:
        copy.wait()

    def over_parts(k):
        tops = seen[:, k, 0, :]
        best = jnp.max(tops, 0, keepdims=True)
        scale = jnp.exp(tops - best)
        total = jnp.sum(seen[:, k, 1, :] * scale, 0, keepdims=True)
        return best + jnp.log(total), scale, total

    counted = counted_ref[...]
    lane = lax.broadcasted_iota(jnp.int32, (1, 128), 1)
    left = lane < 64
    totals, entropies, chances = [], [], []
    for k in range(4):
        lse, scale, total = over_parts(k)
        entropies.append(jnp.sum(seen[:, k, 2, :] * scale, 0, keepdims=True) / total - lse)
        chances.append(counted * (jnp.sum(seen[:, k, 3, :], 0, keepdims=True) - lse))
        totals.append(lse)
    student, _, _ = over_parts(4)

    def of_sequence(values):
        first = jnp.sum(jnp.where(left, values, 0.0), -1, keepdims=True)
        second = jnp.sum(jnp.where(left, 0.0, values), -1, keepdims=True)
        return jnp.where(left, first, second)

    hits = jnp.maximum(of_sequence(counted), 1.0)
    gains = [of_sequence(chance) / hits for chance in chances]
    best = functools.reduce(jnp.maximum, gains)
    powers = [jnp.exp(gain - best) for gain in gains]
    power = functools.reduce(jnp.add, powers)
    entropy = jnp.zeros((1, 128), f32)
    lines = []
    for k in range(4):
        lines.append(gains[k] - best - jnp.log(power) - totals[k])
        entropy += (powers[k] / power * entropies[k]).astype(bf16).astype(f32)
    lines += [student, counted, jnp.zeros((2, 128), f32)]
    chip = me["y"] * 4 + me["x"]
    shift[chip] = jnp.concatenate(lines, axis=0)
    ours = jnp.where(left, 0, 1) == me["c"]
    loss[...] = jnp.where(ours, counted * (entropy + student), 0.0)
    copies = []
    for k in range(1, 16):
        place = moved(me, (7 * k) % 16 // 4, (7 * k) % 4, 0)
        copies.append(remote(shift.at[chip], shift.at[chip], sends, arrivals, 30 + k, place))
    for copy in copies:
        copy.wait()


def blend(stats, counted, collective):
    return pl.pallas_call(
        blend_kernel,
        out_shape=[
            jax.ShapeDtypeStruct((16, 8, 128), jnp.float32),
            jax.ShapeDtypeStruct((1, 128), jnp.float32),
        ],
        in_specs=[VMEM, VMEM],
        out_specs=[VMEM, VMEM],
        scratch_shapes=[
            pltpu.VMEM((32, 5, 4, 128), jnp.float32),
            pltpu.SemaphoreType.DMA((46,)),
            pltpu.SemaphoreType.DMA((46,)),
            pltpu.SemaphoreType.DMA,
        ],
        compiler_params=pltpu.CompilerParams(collective_id=collective, has_side_effects=True),
    )(stats, counted)


def head_grads_kernel(logits, z, shift, h, table, head_grad, grad_rows, crossed, low):
    f32, bf16 = jnp.float32, jnp.bfloat16
    grad = jnp.zeros(head_grad.shape, f32)
    for at in range(0, z.shape[2], WING):
        cols = slice(at, at + WING)
        lines = jnp.concatenate([shift[at // 128], shift[at // 128 + 1]], axis=1)
        lse, counted = lines[4:5], lines[5:6]
        total = jnp.zeros((8, WING), f32)
        for deep in range(0, z.shape[1], DEEP):
            rows = slice(deep, deep + DEEP)
            target = jnp.zeros((DEEP, WING), f32)
            for t in range(4):
                share = jnp.exp(logits[t, rows, cols] + lines[t : t + 1])
                target += share.astype(bf16).astype(f32)
            student = z[0, rows, cols]
            low[rows, cols] = (counted * (jnp.exp(student - lse) - target)).astype(bf16)
            total += jnp.sum(by_eight(target * student), 0)
        crossed[:, cols] = counted * jnp.sum(total, 0, keepdims=True)
        grad_rows[cols] = lax.dot_general(
            low[:, cols], table[...], (((0,), (0,)), ((), ())), preferred_element_type=f32
        ).astype(bf16)
        grad += product(low[:, cols], h[cols])

    @pl.when(pl.program_id(0) == 0)
    def _():
        head_grad[...] = grad

    @pl.when(pl.program_id(0) > 0)
    def _():
        head_grad[...] += grad


def head_grads(logits, z, shift, h, table):
    teachers, vocab, rows = logits.shape
    width = table.shape[1]
    wide = 2 * WING
    return pl.pallas_call(
        head_grads_kernel,
        grid=(rows // wide,),
        out_shape=[
            jax.ShapeDtypeStruct((vocab, width), jnp.float32),
            jax.ShapeDtypeStruct((rows, width), jnp.bfloat16),
            jax.ShapeDtypeStruct((1, rows), jnp.float32),
        ],
        in_specs=[
            pl.BlockSpec((teachers, vocab, wide), lambda j: (0, 0, j)),
            pl.BlockSpec((1, vocab, wide), lambda j: (0, 0, j)),
            pl.BlockSpec((wide // 128, 8, 128), lambda j: (j, 0, 0)),
            pl.BlockSpec((wide, width), lambda j: (j, 0)),
            pl.BlockSpec((vocab, width), lambda j: (0, 0)),
        ],
        out_specs=[
            pl.BlockSpec((vocab, width), lambda j: (0, 0)),
            pl.BlockSpec((wide, width), lambda j: (j, 0)),
            pl.BlockSpec((1, wide), lambda j: (0, j)),
        ],
        scratch_shapes=[pltpu.VMEM((vocab, wide), jnp.bfloat16)],
        compiler_params=pltpu.CompilerParams(vmem_limit_bytes=WIDE),
    )(logits, z, shift, h, table)


def scatter_sum_kernel(plan, *refs):
    f32, bf16 = jnp.float32, jnp.bfloat16
    parts, refs = refs[: len(plan)], refs[len(plan) :]
    out, own, other, both, in_a, in_b, mid_a, mid_b, end_a, end_b, sends, arrivals, local = refs
    me = here()
    steps_x = [moved(me, 0, d, 0) for d in (1, 2, 3)]
    steps_y = [moved(me, d, 0, 0) for d in (1, 2, 3)]
    sibling = moved(me, 0, 0, 1)
    greet([sibling] + steps_x + steps_y)
    copies, at, k = [], 0, 13
    width = own.shape[-1]
    for part, (rows, columns) in zip(parts, plan):
        for column in range(0, columns, width):
            span = (slice(None), pl.ds(at, rows))
            cols = pl.ds(column, width)
            copies.append(
                remote(
                    part.at[:, sibling["c"], :, cols],
                    other.at[span],
                    sends,
                    arrivals,
                    k,
                    sibling,
                )
            )
            mine = pltpu.make_async_copy(
                part.at[:, me["c"], :, cols], own.at[span], local.at[k - 13]
            )
            mine.start()
            copies.append(mine)
            at += rows
            k += 1
    for copy in copies:
        copy.wait()

    @pl.loop(0, 16)
    def _(k):
        both[k // 4, lax.rem(k, 4)] = (own[k].astype(f32) + other[k].astype(f32)).astype(bf16)

    cut = in_a.shape[-1]
    left, right = pl.ds(0, cut), pl.ds(cut, width - cut)
    copies = []
    for d in range(3):
        to_x, to_y = steps_x[d], steps_y[d]
        copies.append(
            remote(both.at[:, to_x["x"], :, left], in_a.at[d], sends, arrivals, 1 + d, to_x)
        )
        copies.append(
            remote(both.at[to_y["y"], :, :, right], in_b.at[d], sends, arrivals, 4 + d, to_y)
        )
    for copy in copies:
        copy.wait()

    @pl.loop(0, 4)
    def _(k):
        total_a = both[k, me["x"], :, left].astype(f32)
        total_b = both[me["y"], k, :, right].astype(f32)
        for d in range(3):
            total_a += in_a[d, k].astype(f32)
            total_b += in_b[d, k].astype(f32)
        mid_a[k] = total_a.astype(bf16)
        mid_b[k] = total_b.astype(bf16)

    copies = []
    for d in range(3):
        to_x, to_y = steps_x[d], steps_y[d]
        copies.append(remote(mid_a.at[to_y["y"]], end_a.at[d], sends, arrivals, 7 + d, to_y))
        copies.append(remote(mid_b.at[to_x["x"]], end_b.at[d], sends, arrivals, 10 + d, to_x))
    for copy in copies:
        copy.wait()
    total_a = mid_a[me["y"]].astype(f32)
    total_b = mid_b[me["x"]].astype(f32)
    for d in range(3):
        total_a += end_a[d].astype(f32)
        total_b += end_b[d].astype(f32)
    out[:, left] = total_a.astype(out.dtype)
    out[:, right] = total_b.astype(out.dtype)


def sum_and_scatter(parts, width, dtype, collective):
    plan = [part.shape[1:] for part in parts]
    rows = sum(r * (c // width) for r, c in plan)
    pieces = sum(c // width for _, c in plan)
    cut = width // 2
    rest = width - cut
    bf16 = jnp.bfloat16
    return pl.pallas_call(
        partial(scatter_sum_kernel, plan),
        out_shape=jax.ShapeDtypeStruct((rows, width), dtype),
        in_specs=[ANY] * len(parts),
        out_specs=VMEM,
        scratch_shapes=[
            pltpu.VMEM((16, rows, width), bf16),
            pltpu.VMEM((16, rows, width), bf16),
            pltpu.VMEM((4, 4, rows, width), bf16),
            pltpu.VMEM((3, 4, rows, cut), bf16),
            pltpu.VMEM((3, 4, rows, rest), bf16),
            pltpu.VMEM((4, rows, cut), bf16),
            pltpu.VMEM((4, rows, rest), bf16),
            pltpu.VMEM((3, rows, cut), bf16),
            pltpu.VMEM((3, rows, rest), bf16),
            pltpu.SemaphoreType.DMA((13 + pieces,)),
            pltpu.SemaphoreType.DMA((13 + pieces,)),
            pltpu.SemaphoreType.DMA((pieces,)),
        ],
        compiler_params=pltpu.CompilerParams(
            collective_id=collective, has_side_effects=True, vmem_limit_bytes=WIDE
        ),
    )(*[part.reshape(16, 2, *part.shape[1:]) for part in parts])


def group_sum_kernel(
    table, rest, facts, table_out, rest_out, seen, table_in, rest_in, told, sends, arrivals, local
):
    f32, bf16 = jnp.float32, jnp.bfloat16
    me = here()
    group = lax.axis_index("grp")
    groups = [{"grp": lax.rem(group + d, 4)} for d in (1, 2, 3)]
    plane = [moved(me, *step) for step in AROUND]
    greet(groups + plane)

    def quarter(g):
        return pl.ds(pl.multiple_of(g * 128, 128), 128)

    mine = quarter(group)
    copies = []
    for d in range(3):
        theirs = quarter(groups[d]["grp"])
        copies.append(remote(table.at[:, theirs], table_in.at[d], sends, arrivals, d, groups[d]))
        copies.append(remote(rest.at[:, theirs], rest_in.at[d], sends, arrivals, 3 + d, groups[d]))
    for copy in copies:
        copy.wait()

    def summed(source, arrived, target):
        rows = 16

        def body(k, squares):
            at = pl.ds(pl.multiple_of(k * rows, rows), rows)
            total = source[at, mine].astype(f32)
            for d in range(3):
                total += arrived[d, at].astype(f32)
            total = total.astype(bf16)
            target[at, mine] = total
            total = total.astype(f32)
            total = total * total
            return squares + total[:8] + total[8:]

        return lax.fori_loop(0, source.shape[0] // rows, body, jnp.zeros((8, 128), f32))

    squares = summed(table, table_in, table_out) + summed(rest, rest_in, rest_out)
    told[group, 0:8] = squares
    told[group, 8:16] = facts[...]
    copies = []
    for d in range(3):
        copies.append(
            remote(told.at[group], told.at[group], sends, arrivals, 6 + d, groups[d])
        )
    wide = []
    for d in range(3):
        wide.append(
            remote(table_out.at[:, mine], table_out.at[:, mine], sends, arrivals, 9 + d, groups[d])
        )
        wide.append(
            remote(rest_out.at[:, mine], rest_out.at[:, mine], sends, arrivals, 12 + d, groups[d])
        )
    for copy in copies:
        copy.wait()
    seen[number(me)] = told[0] + told[1] + told[2] + told[3]
    copies = []
    for k, place in enumerate(plane):
        copies.append(
            remote(seen.at[number(me)], seen.at[number(me)], sends, arrivals, 15 + k, place)
        )
    for copy in copies + wide:
        copy.wait()


def sum_of_groups(table, rest, facts, collective):
    count = 15 + len(AROUND)
    return pl.pallas_call(
        group_sum_kernel,
        out_shape=[
            jax.ShapeDtypeStruct(table.shape, table.dtype),
            jax.ShapeDtypeStruct(rest.shape, rest.dtype),
            jax.ShapeDtypeStruct((32, 16, 128), jnp.float32),
        ],
        in_specs=[VMEM, VMEM, VMEM],
        out_specs=[VMEM, VMEM, VMEM],
        scratch_shapes=[
            pltpu.VMEM((3, table.shape[0], 128), table.dtype),
            pltpu.VMEM((3, rest.shape[0], 128), rest.dtype),
            pltpu.VMEM((4, 16, 128), jnp.float32),
            pltpu.SemaphoreType.DMA((count,)),
            pltpu.SemaphoreType.DMA((count,)),
            pltpu.SemaphoreType.DMA,
        ],
        compiler_params=pltpu.CompilerParams(
            collective_id=collective, has_side_effects=True, vmem_limit_bytes=40 * 2**20
        ),
    )(table, rest, facts)


def slots(tokens, own_rows):
    count = tokens.shape[0]
    row, column = tokens[:, None], tokens[None, :]
    place = jnp.arange(count)
    repeated = jnp.any((row == column) & (place[:, None] < place[None, :]), axis=0)
    owner = tokens // own_rows
    counts = ~repeated[:, None] & (row >= (owner * own_rows)[None, :]) & (row < column)
    return owner, ~repeated, jnp.sum(counts.astype(jnp.int32), axis=0)


def slot_in_round(owner, rank, room, turn):
    at = rank - turn * room
    return jnp.where((at >= 0) & (at < room), owner * room + at, -1)


def wanted_rows(slot, first, local, places):
    hit = (jnp.where(first, slot, -1)[:, None] == jnp.arange(places)[None, :])
    return jnp.sum(jnp.where(hit, local[:, None] + 1, 0), axis=0) - 1


def one_hot(index, count):
    return (index[:, None] == jnp.arange(count)[None, :]).astype(jnp.bfloat16)


def product(left, right):
    return jnp.dot(left, right, preferred_element_type=jnp.float32)


def folded(rows):
    return jnp.concatenate(jnp.split(rows, 2, axis=2), axis=1)


def unfolded(rows):
    return jnp.concatenate(jnp.split(rows, 2, axis=1), axis=2)


def layer_norm(value, gain, shift):
    mean = jnp.mean(value, -1, keepdims=True)
    centred = value - mean
    var = jnp.mean(centred * centred, -1, keepdims=True)
    return centred * lax.rsqrt(var + norm_eps) * gain + shift


def norm_back(value, gain, shift, grad):
    _, pull = jax.vjp(layer_norm, value, gain, shift)
    return pull(grad)


def project(left, right):
    return jnp.einsum("blk,kn->bln", left, right, preferred_element_type=jnp.float32)


def project_back(grad, right):
    return jnp.einsum("bln,kn->blk", grad, right, preferred_element_type=jnp.float32)


def weight_grad(left, grad):
    return jnp.einsum("blk,bln->kn", left, grad, preferred_element_type=jnp.float32)


def split_heads(packed, width):
    batch, span = (packed.shape[0], packed.shape[1])
    return [
        packed[:, :, piece * width : (piece + 1) * width].reshape(batch, span, width // HD, HD)
        for piece in range(3)
    ]


def masked_scores(query, keyed, lengths):
    scores = jnp.einsum(
        "bqhd,bkhd->bhqk", query, keyed, preferred_element_type=jnp.float32
    ) * HD ** (-0.5)
    valid = jnp.arange(query.shape[1])[None, :] < lengths[:, None]
    return jnp.where(valid[:, None, None, :], scores, -1e30)


def forward(embedded, lengths, weights):
    w_qkv, w_out, w_up, w_down, norms = weights
    norms = norms.astype(jnp.float32)
    width = w_out.shape[1]
    first = layer_norm(embedded, norms[:, 0], norms[:, 1])
    first_low = first.astype(jnp.bfloat16)
    packed = project(first_low, w_qkv).astype(jnp.bfloat16)
    query, keyed, valued = split_heads(packed, width)
    scores = masked_scores(query, keyed, lengths)
    top = jnp.max(scores, -1, keepdims=True)
    total = jnp.sum(jnp.exp(scores - top), -1, keepdims=True)
    probs = (jnp.exp(scores - top) / total).astype(jnp.bfloat16)
    context = jnp.einsum("bhqk,bkhd->bqhd", probs, valued, preferred_element_type=jnp.float32)
    context = context.reshape(first.shape).astype(jnp.bfloat16)
    joined = first + project(context, w_out)
    second = layer_norm(joined, norms[:, 2], norms[:, 3])
    second_low = second.astype(jnp.bfloat16)
    hidden_pre = project(second_low, w_up)
    active = jax.nn.gelu(hidden_pre, approximate=False).astype(jnp.bfloat16)
    summed = second + project(active, w_down)
    final = layer_norm(summed, norms[:, 4], norms[:, 5])
    saved = (
        embedded,
        first_low,
        packed,
        top,
        total,
        context,
        joined,
        second_low,
        hidden_pre,
        active,
        summed,
    )
    return (final, saved)


def backward(lengths, weights, saved, grad_final):
    w_qkv, w_out, w_up, w_down, norms = weights
    norms = norms.astype(jnp.float32)
    (
        embedded,
        first_low,
        packed,
        top,
        total,
        context,
        joined,
        second_low,
        hidden_pre,
        active,
        summed,
    ) = saved
    width = w_out.shape[1]
    grad_summed, gain_c, shift_c = norm_back(summed, norms[:, 4], norms[:, 5], grad_final)
    grad_ffn = grad_summed.astype(jnp.bfloat16)
    g_down = weight_grad(active, grad_ffn)
    _, gelu_pull = jax.vjp(partial(jax.nn.gelu, approximate=False), hidden_pre)
    grad_up = gelu_pull(project_back(grad_ffn, w_down))[0].astype(jnp.bfloat16)
    g_up = weight_grad(second_low, grad_up)
    grad_second = grad_summed + project_back(grad_up, w_up)
    grad_joined, gain_b, shift_b = norm_back(joined, norms[:, 2], norms[:, 3], grad_second)
    grad_attn = grad_joined.astype(jnp.bfloat16)
    g_out = weight_grad(context, grad_attn)
    grad_context = project_back(grad_attn, w_out).astype(jnp.bfloat16)
    query, keyed, valued = split_heads(packed, width)
    scores = masked_scores(query, keyed, lengths)
    probs = jnp.exp(scores - top) / total
    grad_heads = grad_context.reshape(query.shape)
    grad_valued = jnp.einsum(
        "bhqk,bqhd->bkhd",
        probs.astype(jnp.bfloat16),
        grad_heads,
        preferred_element_type=jnp.float32,
    )
    grad_probs = jnp.einsum(
        "bqhd,bkhd->bhqk", grad_heads, valued, preferred_element_type=jnp.float32
    )
    grad_scores = (probs * (grad_probs - jnp.sum(probs * grad_probs, -1, keepdims=True))).astype(
        jnp.bfloat16
    )
    grad_query = jnp.einsum(
        "bhqk,bkhd->bqhd", grad_scores, keyed, preferred_element_type=jnp.float32
    ) * HD ** (-0.5)
    grad_keyed = jnp.einsum(
        "bhqk,bqhd->bkhd", grad_scores, query, preferred_element_type=jnp.float32
    ) * HD ** (-0.5)
    grad_packed = jnp.concatenate(
        [piece.reshape(first_low.shape) for piece in (grad_query, grad_keyed, grad_valued)], -1
    )
    grad_packed = grad_packed.astype(jnp.bfloat16)
    g_qkv = weight_grad(first_low, grad_packed)
    grad_first = grad_joined + project_back(grad_packed, w_qkv)
    grad_embedded, gain_a, shift_a = norm_back(embedded, norms[:, 0], norms[:, 1], grad_first)
    g_positions = jnp.sum(grad_embedded, 0)
    g_norms = jnp.stack([gain_a, shift_a, gain_b, shift_b, gain_c, shift_c], -1)
    return (grad_embedded, g_positions, g_qkv, g_out, g_up, g_down, g_norms)


def per_device(
    ids,
    lengths,
    picks,
    labels,
    s_table,
    s_pos,
    s_qkv,
    s_out,
    s_up,
    s_down,
    s_norms,
    m_table,
    m_pos,
    m_qkv,
    m_out,
    m_up,
    m_down,
    m_norms,
    a_table,
    a_pos,
    a_qkv,
    a_out,
    a_up,
    a_down,
    a_norms,
    t_table,
    t_pos,
    t_qkv,
    t_out,
    t_up,
    t_down,
    t_norms,
):
    masters = (s_table, s_pos, s_qkv, s_out, s_up, s_down, s_norms)
    momenta = (m_table, m_pos, m_qkv, m_out, m_up, m_down, m_norms)
    averages = (a_table, a_pos, a_qkv, a_out, a_up, a_down, a_norms)
    f32, bf16 = jnp.float32, jnp.bfloat16
    fsdp = lax.axis_size(FSDP)
    width, t_width = s_table.shape[1], t_table.shape[2]
    vocab_own = s_table.shape[0]
    picked = picks.shape[1]
    span = ids.shape[1]

    facts = jnp.concatenate([ids, picks, jnp.broadcast_to(lengths[:, None], (1, 64))], axis=1)
    facts = jnp.pad(facts.reshape(3, 128), ((0, 5), (0, 0)))
    facts = exchange_groups(jnp.broadcast_to(facts, (4, 8, 128)), 9)[:, :3].reshape(4, -1)
    group_ids, group_picks = facts[:, :span], facts[:, span : span + picked]
    group_lengths = facts[:, span + picked]
    own_table = s_table.astype(bf16)
    t_owner, t_first, t_rank = slots(group_ids.reshape(-1), vocab_own)
    s_owners, s_firsts, s_ranks = jax.vmap(lambda one: slots(one, vocab_own))(group_ids)
    my_group = lax.axis_index("grp")
    s_owner, s_first, s_rank = (
        lax.dynamic_index_in_dim(v, my_group, 0, keepdims=False)
        for v in (s_owners, s_firsts, s_ranks)
    )
    most = jnp.maximum(jnp.max(t_rank) // T_ROOM, jnp.max(s_ranks) // S_ROOM) + 1
    t_local = group_ids.reshape(-1) - t_owner * vocab_own
    s_local = ids[0] - s_owner * vocab_own

    def asked(turn):
        t_slot = slot_in_round(t_owner, t_rank, T_ROOM, turn)
        s_slot = slot_in_round(s_owner, s_rank, S_ROOM, turn)
        t_ask = wanted_rows(t_slot, t_first, t_local, fsdp * T_ROOM).reshape(fsdp, T_ROOM)
        s_ask = wanted_rows(s_slot, s_first, s_local, fsdp * S_ROOM).reshape(fsdp, S_ROOM)
        return t_slot, s_slot, t_ask, s_ask

    def answer(t_want, s_want):
        t_sent = product(one_hot(t_want.reshape(-1), vocab_own), t_table[0]).astype(bf16)
        s_sent = product(one_hot(s_want.reshape(-1), vocab_own), own_table).astype(bf16)
        return jnp.concatenate(
            [t_sent.reshape(fsdp, T_ROOM, t_width), folded(s_sent.reshape(fsdp, S_ROOM, width))],
            axis=2,
        )

    def placed(got, t_slot, s_slot):
        t_got = got[:, :, :t_width].reshape(-1, t_width)
        s_got = unfolded(got[:, :, t_width:]).reshape(-1, width)
        return (
            product(one_hot(t_slot, fsdp * T_ROOM), t_got),
            product(one_hot(s_slot, fsdp * S_ROOM), s_got),
        )

    def swap(value):
        return lax.all_to_all(value, FSDP, split_axis=0, concat_axis=0, tiled=True)

    def ask_again(turn):
        t_slot, s_slot, t_ask, s_ask = asked(turn)
        wants = swap(jnp.concatenate([t_ask, s_ask], axis=1))
        return t_slot, s_slot, wants[:, :T_ROOM], wants[:, T_ROOM:]

    def more_rows(state):
        turn, t_emb, s_emb = state
        t_slot, s_slot, t_want, s_want = ask_again(turn)
        t_more, s_more = placed(swap(answer(t_want, s_want)), t_slot, s_slot)
        return turn + 1, t_emb + t_more.astype(bf16), s_emb + s_more.astype(bf16)

    t_slot, s_slot, t_ask, s_ask = asked(0)
    line = jnp.concatenate(
        [t_ask, s_ask, jnp.broadcast_to(most, (fsdp, 128 - T_ROOM - S_ROOM))], axis=1
    )
    lines = [
        line,
        jnp.broadcast_to(jnp.concatenate([picks, labels], axis=1), (fsdp, 2 * picked)),
        jnp.broadcast_to(lengths[:, None], (fsdp, 128)),
    ]
    notes = jnp.stack(lines + [jnp.zeros((fsdp, 128), jnp.int32)] * 5, axis=1)
    notes, got = route(notes, t_table[0], own_table, 1)
    s_want = notes[:, 0, T_ROOM : T_ROOM + S_ROOM]
    rounds = jnp.max(notes[:, 0, T_ROOM + S_ROOM])
    plane_picks, plane_labels = notes[:, 1, :picked], notes[:, 1, picked : 2 * picked]
    plane_lengths = notes[:, 2, 0]
    nothing = (jnp.zeros((t_slot.shape[0], t_width), bf16), jnp.zeros((span, width), bf16))
    _, t_extra, s_extra = lax.while_loop(
        lambda state: state[0] < rounds, more_rows, (jnp.int32(1), *nothing)
    )

    def pieces(blocks, qkv, out, up, down, pos, norms):
        tail = norms.astype(f32).reshape(blocks, 1, -1)
        tail = jnp.pad(tail, ((0, 0), (0, 7), (0, width - tail.shape[2])))
        small = jnp.concatenate([pos.reshape(blocks, -1, width).astype(f32), tail], axis=1)
        big = [part.astype(bf16).reshape(blocks, -1, part.shape[1]) for part in (qkv, out, up, down)]
        return big + [lax.optimization_barrier(small.astype(bf16))]

    def pack(parts):
        columns = [
            part[:, :, at : at + width] for part in parts for at in range(0, part.shape[2], width)
        ]
        return jnp.concatenate(columns, axis=1)

    def unpack(packed):
        blocks, lead = packed.shape[0], s_qkv.shape[0]

        def across(at, count):
            return jnp.concatenate(
                [
                    packed[:, at + k * lead : at + (k + 1) * lead].reshape(-1, width)
                    for k in range(count)
                ],
                axis=1,
            )

        at_out = s_qkv.shape[1] // width * lead
        at_up = at_out + lead
        at_down = at_up + s_up.shape[1] // width * lead
        at_pos = at_down + s_down.shape[0]
        at_norms = at_pos + s_pos.shape[0]
        return (
            across(0, s_qkv.shape[1] // width),
            across(at_out, 1),
            across(at_up, s_up.shape[1] // width),
            packed[:, at_down:at_pos].reshape(-1, width),
            packed[:, at_pos:at_norms].reshape(-1, width),
            packed[:, at_norms, : s_norms.size].reshape(-1, s_norms.shape[1]),
        )

    own_packed = pack(pieces(1, s_qkv, s_out, s_up, s_down, s_pos, s_norms))
    w_qkv, w_out, w_up, w_down, positions, norms = unpack(
        lax.all_gather(own_packed, FSDP, axis=0, tiled=True)
    )
    student = (w_qkv, w_out, w_up, w_down, norms)
    heads = lax.all_gather(t_table[0], "grp", axis=0, tiled=False)

    taken = teacher_rows(
        group_lengths,
        t_slot,
        group_picks,
        got.reshape(-1, got.shape[2]),
        t_extra.reshape(-1, span, t_width),
        t_pos[0],
        t_norms[0].astype(f32).T,
        t_qkv[0],
        t_out[0],
        t_up[0],
        t_down[0],
    )
    taken, heads = lax.optimization_barrier((taken, heads))
    rows = exchange_groups(taken, 10)
    s_extra, got, rows = lax.optimization_barrier((s_extra, got, rows))
    rows = lax.all_gather(rows, FSDP, axis=0, tiled=False)

    s_got = unfolded(got[:, :, t_width:]).reshape(-1, width)
    s_emb = product(one_hot(s_slot, fsdp * S_ROOM), s_got) + s_extra.astype(f32)
    embedded = s_emb[None] + positions.astype(f32)[None]
    final, saved = forward(embedded, lengths, student)
    own_rows = jnp.take_along_axis(final, picks[:, :, None], axis=1).astype(bf16)[0]
    h = gather_plane(own_rows, 11)
    base = lax.axis_index(FSDP) * vocab_own
    labels_here = plane_labels.reshape(1, -1) - base
    z, z_stats = vocabulary_logits(labels_here, h.reshape(fsdp, 1, picked, width), own_table[None])
    logits, stats = vocabulary_logits(labels_here, rows, heads)
    stats = jnp.concatenate([stats, z_stats], axis=0)
    plane_counted = (plane_picks < plane_lengths[:, None]).astype(f32).reshape(-1, 1, 2 * picked)
    chip = lax.axis_index(("y", "x"))
    chip_counted = lax.dynamic_index_in_dim(plane_counted, chip, 0, keepdims=False)
    shift, own_loss = blend(stats, chip_counted, 3)
    head_grad, grad_rows, crossed = head_grads(logits, z, shift, h, own_table)
    count_local = jnp.sum((picks < lengths[:, None]).astype(f32))
    loss_local = jnp.sum(own_loss) - jnp.sum(crossed)
    grad_rows = sum_and_scatter([grad_rows.reshape(fsdp, picked, width)], width, f32, 5)

    grad_final = jnp.zeros(final.shape, f32).at[0, picks[0]].add(grad_rows)
    terms = backward(lengths, student, saved, grad_final)
    grad_embedded = terms[0]
    low_embedded = grad_embedded[0].astype(bf16)

    def given(s_slot):
        rows = product(one_hot(s_slot, fsdp * S_ROOM).T, low_embedded).astype(bf16)
        return folded(rows.reshape(fsdp, S_ROOM, width))

    def taken_in(got, s_want):
        rows = unfolded(got).reshape(-1, width)
        return product(one_hot(s_want.reshape(-1), vocab_own).T, rows)

    def more_grads(state):
        turn, total = state
        _, s_slot, _, s_want = ask_again(turn)
        return turn + 1, total + taken_in(swap(given(s_slot)), s_want)

    g_lookup = taken_in(exchange(given(s_slot), 6), s_want)
    _, g_table = lax.while_loop(
        lambda state: state[0] < rounds, more_grads, (jnp.int32(1), head_grad + g_lookup)
    )
    g_pos, g_qkv, g_out, g_up, g_down, g_norms = terms[1:]
    parts = pieces(fsdp, g_qkv, g_out, g_up, g_down, g_pos, g_norms)
    rest = sum_and_scatter(parts, width, bf16, 7)
    row = jnp.arange(8)[:, None]
    column_of = jnp.arange(128)[None, :]
    told = jnp.where((row == 0) & (column_of == 0), loss_local, 0.0)
    told += jnp.where((row == 1) & (column_of == 0), count_local, 0.0)
    table_sum, rest_sum, seen = sum_of_groups(g_table.astype(bf16), rest, told, 8)
    seen = seen.sum(0)
    squares, loss_sum, count = jnp.sum(seen[:8]), seen[8, 0], seen[9, 0]
    at_norms = rest_sum.shape[0] - 8
    norms_sum = rest_sum[at_norms, : s_norms.size].astype(f32).reshape(s_norms.shape).T
    turned = [group[:6] + (group[6].T,) for group in (masters, momenta, averages)]
    clip_norm = jnp.sqrt(squares) / count
    factor = jnp.minimum(1.0, clip_limit / clip_norm) / count
    outs = update(factor, table_sum, rest_sum, norms_sum, *turned)
    outs = tuple(out.T if k % 7 == 6 else out for k, out in enumerate(outs))
    return (loss_sum, count, clip_norm) + outs


def solution(mesh):
    finer = Mesh(
        mesh.devices.reshape(mesh.shape["grp"], 4, 4, 2), ("grp", "y", "x", "c")
    )
    return jax.shard_map(
        per_device,
        mesh=finer,
        in_specs=(
            P(GRP_FSDP, None),
            P(GRP_FSDP),
            P(GRP_FSDP, None),
            P(GRP_FSDP, None),
            P(FSDP, None),
            P(FSDP, None),
            P(FSDP, None),
            P(FSDP, None),
            P(FSDP, None),
            P(FSDP, None),
            P(FSDP, None),
            P(FSDP, None),
            P(FSDP, None),
            P(FSDP, None),
            P(FSDP, None),
            P(FSDP, None),
            P(FSDP, None),
            P(FSDP, None),
            P(FSDP, None),
            P(FSDP, None),
            P(FSDP, None),
            P(FSDP, None),
            P(FSDP, None),
            P(FSDP, None),
            P(FSDP, None),
            P("grp", FSDP, None),
            P("grp", None, None),
            P("grp", None, None),
            P("grp", None, None),
            P("grp", None, None),
            P("grp", None, None),
            P("grp", None, None),
        ),
        out_specs=(
            P(),
            P(),
            P(),
            P(FSDP, None),
            P(FSDP, None),
            P(FSDP, None),
            P(FSDP, None),
            P(FSDP, None),
            P(FSDP, None),
            P(FSDP, None),
            P(FSDP, None),
            P(FSDP, None),
            P(FSDP, None),
            P(FSDP, None),
            P(FSDP, None),
            P(FSDP, None),
            P(FSDP, None),
            P(FSDP, None),
            P(FSDP, None),
            P(FSDP, None),
            P(FSDP, None),
            P(FSDP, None),
            P(FSDP, None),
            P(FSDP, None),
        ),
        check_vma=False,
    )
```

```python
import functools
import math
from functools import partial

import jax
import jax.numpy as jnp
from jax import lax
from jax.experimental import pallas as pl
from jax.experimental.pallas import tpu as pltpu
from jax.sharding import Mesh
from jax.sharding import PartitionSpec as P

HD = 64
FSDP = ("y", "x", "c")
GRP_FSDP = ("grp", "y", "x", "c")
T_ROOM = 48
S_ROOM = 24
S_APART = 32
WIDE = 56 * 2**20

norm_eps = 1e-12
clip_limit = 0.001
learn_rate = 100000.0
momentum_decay = 0.9
average_decay = 0.9


SIZES = {"y": 4, "x": 4, "c": 2}
MESH = pl.DeviceIdType.MESH
ANY = pl.BlockSpec(memory_space=pl.ANY)
VMEM = pl.BlockSpec(memory_space=pltpu.VMEM)
AROUND = [((11 * k) % 32 // 8, (11 * k) % 8 // 2, (11 * k) % 2) for k in range(1, 32)]


def here():
    return {axis: lax.axis_index(axis) for axis in SIZES}


def moved(me, dy, dx, dc):
    return {
        "y": lax.rem(me["y"] + dy, 4),
        "x": lax.rem(me["x"] + dx, 4),
        "c": lax.rem(me["c"] + dc, 2),
    }


def number(place):
    return (place["y"] * 4 + place["x"]) * 2 + place["c"]


def greet(places):
    barrier = pltpu.get_barrier_semaphore()
    for place in places:
        pl.semaphore_signal(barrier, inc=1, device_id=place, device_id_type=MESH)
    pl.semaphore_wait(barrier, len(places))


def remote(source, target, sends, arrivals, at, place):
    copy = pltpu.make_async_remote_copy(
        src_ref=source,
        dst_ref=target,
        send_sem=sends.at[at],
        recv_sem=arrivals.at[at],
        device_id=place,
        device_id_type=MESH,
    )
    copy.start()
    return copy


def route_kernel(notes, t_table, s_table, heard, got, sent, wants, sends, arrivals, local):
    f32, bf16 = jnp.float32, jnp.bfloat16
    me = here()
    greet([moved(me, *step) for step in AROUND])
    copies = []
    for k, step in enumerate(AROUND):
        place = moved(me, *step)
        copies.append(
            remote(notes.at[number(place)], heard.at[number(me)], sends, arrivals, k, place)
        )
    heard[number(me)] = notes[number(me)]
    for copy in copies:
        copy.wait()
    all_wants = heard[:, 0, :].astype(f32).T
    vocab, t_width = t_table.shape
    half = s_table.shape[1] // 2
    batch = wants.shape[2]
    for k in range(wants.shape[0]):
        wants[k] = all_wants[:, k * batch : (k + 1) * batch]

    def rows_of(k, at, room, table):
        index = jnp.concatenate(
            [wants[k, at : at + room, p : p + 1] for p in range(batch)], axis=0
        )
        entry = lax.broadcasted_iota(jnp.int32, (index.shape[0], vocab), 1).astype(f32)
        hot = jnp.where(entry == index, 1.0, 0.0).astype(bf16)
        return product(hot, table[...])

    @pl.loop(0, wants.shape[0])
    def _(k):
        t_rows = rows_of(k, 0, T_ROOM, t_table)
        s_rows = rows_of(k, T_ROOM, S_ROOM, s_table)
        for j in range(batch):
            p = k * batch + j
            sent[p, :, :t_width] = t_rows[j * T_ROOM : (j + 1) * T_ROOM].astype(bf16)
            own = s_rows[j * S_ROOM : (j + 1) * S_ROOM]
            own = jnp.concatenate([own[:, :half], own[:, half:]], axis=0)
            sent[p, :, t_width:] = own.astype(bf16)

    copies = []
    for k, step in enumerate(AROUND):
        place = moved(me, *step)
        copies.append(
            remote(
                sent.at[number(place)], got.at[number(me)], sends, arrivals, len(AROUND) + k, place
            )
        )
    mine = pltpu.make_async_copy(sent.at[number(me)], got.at[number(me)], local)
    mine.start()
    mine.wait()
    for copy in copies:
        copy.wait()


def route(notes, t_table, s_table, collective):
    width = t_table.shape[1] + s_table.shape[1] // 2
    return pl.pallas_call(
        route_kernel,
        out_shape=[
            jax.ShapeDtypeStruct(notes.shape, notes.dtype),
            jax.ShapeDtypeStruct((32, T_ROOM, width), jnp.bfloat16),
        ],
        in_specs=[VMEM, VMEM, VMEM],
        out_specs=[VMEM, ANY],
        scratch_shapes=[
            pltpu.VMEM((32, T_ROOM, width), jnp.bfloat16),
            pltpu.VMEM((4, 128, 8), jnp.float32),
            pltpu.SemaphoreType.DMA((2 * len(AROUND),)),
            pltpu.SemaphoreType.DMA((2 * len(AROUND),)),
            pltpu.SemaphoreType.DMA,
        ],
        compiler_params=pltpu.CompilerParams(
            collective_id=collective, has_side_effects=True, vmem_limit_bytes=40 * 2**20
        ),
    )(notes, t_table, s_table)


def group_exchange_kernel(source, target, sends, arrivals, local):
    group = lax.axis_index("grp")
    groups = [lax.rem(group + d, 4) for d in (1, 2, 3)]
    greet([{"grp": g} for g in groups])
    copies = [
        remote(source.at[g], target.at[group], sends, arrivals, d, {"grp": g})
        for d, g in enumerate(groups)
    ]
    own = pltpu.make_async_copy(source.at[group], target.at[group], local)
    own.start()
    own.wait()
    for copy in copies:
        copy.wait()


def exchange_groups(value, collective):
    return pl.pallas_call(
        group_exchange_kernel,
        out_shape=jax.ShapeDtypeStruct(value.shape, value.dtype),
        in_specs=[ANY],
        out_specs=ANY,
        scratch_shapes=[
            pltpu.SemaphoreType.DMA((3,)),
            pltpu.SemaphoreType.DMA((3,)),
            pltpu.SemaphoreType.DMA,
        ],
        compiler_params=pltpu.CompilerParams(collective_id=collective, has_side_effects=True),
    )(value)


def gather_kernel(source, target, sends, arrivals, local):
    me = here()
    chip, core = me["y"] * 4 + me["x"], me["c"]
    chips = [moved(me, (7 * k) % 16 // 4, (7 * k) % 4, 0) for k in range(1, 16)]
    sibling = moved(me, 0, 0, 1)
    greet(chips + [sibling])
    copies = [
        remote(source, target.at[chip, core], sends, arrivals, k, place)
        for k, place in enumerate(chips)
    ]
    own = pltpu.make_async_copy(source, target.at[chip, core], local)
    own.start()
    own.wait()
    for copy in copies:
        copy.wait()
    remote(target.at[:, core], target.at[:, core], sends, arrivals, 15, sibling).wait()


def gather_plane(value, collective):
    rows, width = value.shape
    out = pl.pallas_call(
        gather_kernel,
        out_shape=jax.ShapeDtypeStruct((16, 2, rows, width), value.dtype),
        in_specs=[ANY],
        out_specs=ANY,
        scratch_shapes=[
            pltpu.SemaphoreType.DMA((16,)),
            pltpu.SemaphoreType.DMA((16,)),
            pltpu.SemaphoreType.DMA,
        ],
        compiler_params=pltpu.CompilerParams(collective_id=collective, has_side_effects=True),
    )(value)
    return out.reshape(32 * rows, width)


def update_kernel(factor_ref, table_grad, rest_grad, norms_grad, *refs):
    masters, momenta, averages = refs[:7], refs[7:14], refs[14:21]
    outs = refs[21:]
    factor = factor_ref[0, 0]

    def step(k, grad):
        clipped = grad * factor
        moment = momentum_decay * momenta[k][...] + clipped
        weight = masters[k][...] - learn_rate * (clipped + momentum_decay * moment)
        outs[k][...] = weight
        outs[7 + k][...] = moment
        outs[14 + k][...] = average_decay * averages[k][...] + (1.0 - average_decay) * weight

    step(0, table_grad[...].astype(jnp.float32))

    @pl.when(pl.program_id(0) == 0)
    def _():
        width = rest_grad.shape[1]
        at = 0
        for k in (2, 3, 4, 5):
            rows, columns = masters[k].shape
            blocks = []
            for _ in range(columns // width):
                blocks.append(rest_grad[at : at + rows].astype(jnp.float32))
                at += rows
            step(k, blocks[0] if len(blocks) == 1 else jnp.concatenate(blocks, axis=1))
        step(1, rest_grad[at : at + 16].astype(jnp.float32)[: masters[1].shape[0]])
        step(6, norms_grad[...])


def update(factor, table_grad, rest_grad, norms_grad, masters, momenta, averages):
    steps = 5
    rows, width = table_grad.shape

    def whole(shape):
        return pl.BlockSpec(shape, lambda i: (0, 0))

    tall = pl.BlockSpec((rows // steps, width), lambda i: (i, 0))
    states = [tall] + [whole(m.shape) for m in masters[1:]]
    outs = pl.pallas_call(
        update_kernel,
        grid=(steps,),
        out_shape=[jax.ShapeDtypeStruct(m.shape, m.dtype) for m in masters] * 3,
        in_specs=[
            pl.BlockSpec(memory_space=pltpu.SMEM),
            tall,
            whole(rest_grad.shape),
            whole(norms_grad.shape),
        ]
        + states * 3,
        out_specs=states * 3,
        compiler_params=pltpu.CompilerParams(vmem_limit_bytes=WIDE),
    )(factor.reshape(1, 1), table_grad, rest_grad, norms_grad, *masters, *momenta, *averages)
    return tuple(outs)


def normed(value, gain, shift):
    mean = jnp.mean(value, -1, keepdims=True)
    centred = value - mean
    var = jnp.mean(centred * centred, -1, keepdims=True)
    return centred * lax.rsqrt(var + norm_eps) * gain + shift


def teacher_kernel(
    lengths, slot, picks, got, extra, pos, norms, w_qkv, w_out, w_up, w_down, out, qkv, ctx
):
    f32, bf16 = jnp.float32, jnp.bfloat16
    span, width = pos.shape
    length = lengths[0, pl.program_id(0)]

    def pick(index, count):
        wide = lax.broadcasted_iota(jnp.int32, (index.shape[0], count), 1)
        return jnp.where(wide == index, 1.0, 0.0).astype(bf16)

    def scale(k):
        return norms[2 * k : 2 * k + 1], norms[2 * k + 1 : 2 * k + 2]

    emb = product(pick(slot[0], got.shape[0]), got[...])
    emb = emb + extra[0].astype(f32) + pos[...].astype(f32)
    first = normed(emb, *scale(0))
    qkv[...] = product(first.astype(bf16), w_qkv[...]).astype(bf16)
    lane = lax.broadcasted_iota(jnp.int32, (span, 2 * HD), 1)
    halves = [jnp.where(lane < HD, 1.0, 0.0), jnp.where(lane < HD, 0.0, 1.0)]
    valid = lax.broadcasted_iota(jnp.int32, (span, span), 1) < length

    def heads_at(at):
        query = qkv[:, pl.ds(at, 2 * HD)]
        keyed = qkv[:, pl.ds(width + at, 2 * HD)]
        valued = qkv[:, pl.ds(2 * width + at, 2 * HD)]
        total = jnp.zeros((span, 2 * HD), f32)
        for half in halves:
            scores = lax.dot_general(
                query * half.astype(bf16),
                keyed,
                (((1,), (1,)), ((), ())),
                preferred_element_type=f32,
            ) * HD ** (-0.5)
            scores = jnp.where(valid, scores, -1e30)
            spread = jnp.exp(scores - jnp.max(scores, -1, keepdims=True))
            probs = spread * (1.0 / jnp.sum(spread, -1, keepdims=True))
            total += half * product(probs.astype(bf16), valued)
        ctx[:, pl.ds(at, 2 * HD)] = total.astype(bf16)

    for at in range(0, width, 2 * HD):
        heads_at(at)

    second = normed(first + product(ctx[...], w_out[...]), *scale(1))
    low = second.astype(bf16)
    ffn = jnp.zeros((span, width), f32)
    for at in range(0, w_up.shape[1], width):
        pre = product(low, w_up[:, at : at + width])
        active = (0.5 * pre * (1.0 + lax.erf(pre * (0.5**0.5)))).astype(bf16)
        ffn += product(active, w_down[at : at + width, :])
    final = normed(second + ffn, *scale(2))
    out[0] = product(pick(picks[0], span), final.astype(bf16)).astype(bf16)


def teacher_rows(lengths, slot, picks, got, extra, pos, norms, w_qkv, w_out, w_up, w_down):
    count, picked = picks.shape
    span, width = pos.shape

    def whole(array, *shape):
        shape = shape or array.shape
        return pl.BlockSpec(shape, lambda i: (0,) * len(shape), pipeline_mode=pl.Buffered(1))

    def each(*shape):
        return pl.BlockSpec((1,) + shape, lambda i: (i, 0, 0))

    return pl.pallas_call(
        teacher_kernel,
        grid=(count,),
        out_shape=jax.ShapeDtypeStruct((count, picked, width), jnp.bfloat16),
        in_specs=[
            pl.BlockSpec(memory_space=pltpu.SMEM),
            each(span, 1),
            each(picked, 1),
            whole(got, got.shape[0], width),
            each(span, width),
            whole(pos),
            whole(norms),
            whole(w_qkv),
            whole(w_out),
            whole(w_up),
            whole(w_down),
        ],
        out_specs=each(picked, width),
        scratch_shapes=[
            pltpu.VMEM((span, 3 * width), jnp.bfloat16),
            pltpu.VMEM((span, width), jnp.bfloat16),
        ],
        compiler_params=pltpu.CompilerParams(vmem_limit_bytes=WIDE),
    )(
        lengths[None],
        slot.reshape(count, span, 1),
        picks[:, :, None],
        got,
        extra,
        pos,
        norms,
        w_qkv,
        w_out,
        w_up,
        w_down,
    )


DEEP = 64
WING = 256


def by_eight(value):
    return value.reshape(value.shape[0] // 8, 8, value.shape[1])


def logits_kernel(labels, rows, head, out, stats):
    f32 = jnp.float32
    taken = rows[...].reshape(-1, rows.shape[-1])
    vocab = out.shape[1]
    parts = []
    for at in range(0, taken.shape[0], WING):
        logits = lax.dot_general(
            head[0], taken[at : at + WING], (((1,), (1,)), ((), ())), preferred_element_type=f32
        )
        out[0, :, at : at + WING] = logits
        parts.append(logits)
    for k, logits in enumerate(parts):
        cols = slice(k * WING, (k + 1) * WING)
        top = jnp.max(jnp.max(by_eight(logits), 0), 0, keepdims=True)
        row = lax.broadcasted_iota(jnp.int32, (DEEP, WING), 0) - labels[:, cols]
        totals = [jnp.zeros((8, WING), f32)] * 3
        for deep in range(0, vocab, DEEP):
            part = logits[deep : deep + DEEP]
            spread = jnp.exp(part - top)
            hit = jnp.where(row == -deep, part, 0.0)
            totals = [
                total + jnp.sum(by_eight(more), 0)
                for total, more in zip(totals, (spread, spread * part, hit))
            ]
        lines = [top] + [jnp.sum(total, 0, keepdims=True) for total in totals]
        stats[0, :, cols] = jnp.concatenate(lines, axis=0)


def vocabulary_logits(labels, rows, heads):
    devices, count, picked, width = rows.shape
    vocab = heads.shape[1]
    block = 2 * WING // picked
    wide = block * picked
    return pl.pallas_call(
        logits_kernel,
        grid=(count, devices // block),
        out_shape=[
            jax.ShapeDtypeStruct((count, vocab, devices * picked), jnp.float32),
            jax.ShapeDtypeStruct((count, 4, devices * picked), jnp.float32),
        ],
        in_specs=[
            pl.BlockSpec((1, wide), lambda k, j: (0, j)),
            pl.BlockSpec((block, 1, picked, width), lambda k, j: (j, k, 0, 0)),
            pl.BlockSpec((1, vocab, width), lambda k, j: (k, 0, 0)),
        ],
        out_specs=[
            pl.BlockSpec((1, vocab, wide), lambda k, j: (k, 0, j)),
            pl.BlockSpec((1, 4, wide), lambda k, j: (k, 0, j)),
        ],
        compiler_params=pltpu.CompilerParams(vmem_limit_bytes=WIDE),
    )(labels, rows, heads)


def blend_kernel(stats, counted_ref, shift, loss, seen, sends, arrivals, local):
    f32, bf16 = jnp.float32, jnp.bfloat16
    me = here()
    greet([moved(me, *step) for step in AROUND])

    def columns(place):
        chip = place["y"] * 4 + place["x"]
        return stats.at[:, :, pl.ds(pl.multiple_of(chip * 128, 128), 128)]

    copies = []
    for k, step in enumerate(AROUND):
        place = moved(me, *step)
        copies.append(remote(columns(place), seen.at[number(me)], sends, arrivals, k, place))
    own = pltpu.make_async_copy(columns(me), seen.at[number(me)], local)
    own.start()
    own.wait()
    for copy in copies:
        copy.wait()

    def over_parts(k):
        tops = seen[:, k, 0, :]
        best = jnp.max(tops, 0, keepdims=True)
        scale = jnp.exp(tops - best)
        total = jnp.sum(seen[:, k, 1, :] * scale, 0, keepdims=True)
        return best + jnp.log(total), scale, total

    counted = counted_ref[...]
    lane = lax.broadcasted_iota(jnp.int32, (1, 128), 1)
    left = lane < 64
    totals, entropies, chances = [], [], []
    for k in range(4):
        lse, scale, total = over_parts(k)
        entropies.append(jnp.sum(seen[:, k, 2, :] * scale, 0, keepdims=True) / total - lse)
        chances.append(counted * (jnp.sum(seen[:, k, 3, :], 0, keepdims=True) - lse))
        totals.append(lse)
    student, _, _ = over_parts(4)

    def of_sequence(values):
        first = jnp.sum(jnp.where(left, values, 0.0), -1, keepdims=True)
        second = jnp.sum(jnp.where(left, 0.0, values), -1, keepdims=True)
        return jnp.where(left, first, second)

    hits = jnp.maximum(of_sequence(counted), 1.0)
    gains = [of_sequence(chance) / hits for chance in chances]
    best = functools.reduce(jnp.maximum, gains)
    powers = [jnp.exp(gain - best) for gain in gains]
    power = functools.reduce(jnp.add, powers)
    entropy = jnp.zeros((1, 128), f32)
    lines = []
    for k in range(4):
        lines.append(gains[k] - best - jnp.log(power) - totals[k])
        entropy += (powers[k] / power * entropies[k]).astype(bf16).astype(f32)
    lines += [student, counted, jnp.zeros((2, 128), f32)]
    chip = me["y"] * 4 + me["x"]
    shift[chip] = jnp.concatenate(lines, axis=0)
    ours = jnp.where(left, 0, 1) == me["c"]
    loss[...] = jnp.where(ours, counted * (entropy + student), 0.0)
    copies = []
    for k in range(1, 16):
        place = moved(me, (7 * k) % 16 // 4, (7 * k) % 4, 0)
        copies.append(remote(shift.at[chip], shift.at[chip], sends, arrivals, 30 + k, place))
    for copy in copies:
        copy.wait()


def blend(stats, counted, collective):
    return pl.pallas_call(
        blend_kernel,
        out_shape=[
            jax.ShapeDtypeStruct((16, 8, 128), jnp.float32),
            jax.ShapeDtypeStruct((1, 128), jnp.float32),
        ],
        in_specs=[VMEM, VMEM],
        out_specs=[VMEM, VMEM],
        scratch_shapes=[
            pltpu.VMEM((32, 5, 4, 128), jnp.float32),
            pltpu.SemaphoreType.DMA((46,)),
            pltpu.SemaphoreType.DMA((46,)),
            pltpu.SemaphoreType.DMA,
        ],
        compiler_params=pltpu.CompilerParams(collective_id=collective, has_side_effects=True),
    )(stats, counted)


def head_grads_kernel(
    logits, z, shift, h, table, head_grad, head_low, grad_rows, crossed, low
):
    f32, bf16 = jnp.float32, jnp.bfloat16
    grad = jnp.zeros(head_grad.shape, f32)
    for at in range(0, z.shape[2], WING):
        cols = slice(at, at + WING)
        lines = jnp.concatenate([shift[at // 128], shift[at // 128 + 1]], axis=1)
        lse, counted = lines[4:5], lines[5:6]
        total = jnp.zeros((8, WING), f32)
        for deep in range(0, z.shape[1], DEEP):
            rows = slice(deep, deep + DEEP)
            target = jnp.zeros((DEEP, WING), f32)
            for t in range(4):
                share = jnp.exp(logits[t, rows, cols] + lines[t : t + 1])
                target += share.astype(bf16).astype(f32)
            student = z[0, rows, cols]
            low[rows, cols] = (counted * (jnp.exp(student - lse) - target)).astype(bf16)
            total += jnp.sum(by_eight(target * student), 0)
        crossed[:, cols] = counted * jnp.sum(total, 0, keepdims=True)
        grad_rows[cols] = lax.dot_general(
            low[:, cols], table[...], (((0,), (0,)), ((), ())), preferred_element_type=f32
        ).astype(bf16)
        grad += product(low[:, cols], h[cols])

    @pl.when(pl.program_id(0) == 0)
    def _():
        head_grad[...] = grad

    @pl.when(pl.program_id(0) > 0)
    def _():
        head_grad[...] += grad

    @pl.when(pl.program_id(0) == pl.num_programs(0) - 1)
    def _():
        head_low[...] = head_grad[...].astype(bf16)


def head_grads(logits, z, shift, h, table):
    teachers, vocab, rows = logits.shape
    width = table.shape[1]
    wide = 2 * WING
    return pl.pallas_call(
        head_grads_kernel,
        grid=(rows // wide,),
        out_shape=[
            jax.ShapeDtypeStruct((vocab, width), jnp.float32),
            jax.ShapeDtypeStruct((vocab, width), jnp.bfloat16),
            jax.ShapeDtypeStruct((rows, width), jnp.bfloat16),
            jax.ShapeDtypeStruct((1, rows), jnp.float32),
        ],
        in_specs=[
            pl.BlockSpec((teachers, vocab, wide), lambda j: (0, 0, j)),
            pl.BlockSpec((1, vocab, wide), lambda j: (0, 0, j)),
            pl.BlockSpec((wide // 128, 8, 128), lambda j: (j, 0, 0)),
            pl.BlockSpec((wide, width), lambda j: (j, 0)),
            pl.BlockSpec((vocab, width), lambda j: (0, 0)),
        ],
        out_specs=[
            pl.BlockSpec((vocab, width), lambda j: (0, 0)),
            pl.BlockSpec((vocab, width), lambda j: (0, 0)),
            pl.BlockSpec((wide, width), lambda j: (j, 0)),
            pl.BlockSpec((1, wide), lambda j: (0, j)),
        ],
        scratch_shapes=[pltpu.VMEM((vocab, wide), jnp.bfloat16)],
        compiler_params=pltpu.CompilerParams(vmem_limit_bytes=40 * 2**20),
    )(logits, z, shift, h, table)


def quarter(group):
    return pl.ds(pl.multiple_of(group * 128, 128), 128)


def scatter_sum_kernel(plan, side, *refs):
    f32, bf16 = jnp.float32, jnp.bfloat16
    parts, refs = refs[: len(plan)], refs[len(plan) :]
    if side == "head":
        exact, sided, out, side_out, mine_exact, side_in, *refs = refs
    else:
        sided, out, side_out, side_in, *refs = refs
    own, other, both, in_a, in_b, mid_a, mid_b, end_a, end_b, sends, arrivals, local = refs
    me = here()
    group = lax.axis_index("grp")
    groups = [{"grp": lax.rem(group + d, 4)} for d in (1, 2, 3)]
    steps_x = [moved(me, 0, d, 0) for d in (1, 2, 3)]
    steps_y = [moved(me, d, 0, 0) for d in (1, 2, 3)]
    sibling = moved(me, 0, 0, 1)
    plane = [moved(me, *step) for step in AROUND]
    greet(groups + (plane if side == "rows" else [sibling] + steps_x + steps_y))
    copies, at, k = [], 0, 16
    width = own.shape[-1]
    for part, (rows, columns) in zip(parts, plan):
        for column in range(0, columns, width):
            span = (slice(None), pl.ds(at, rows))
            cols = pl.ds(column, width)
            copies.append(
                remote(
                    part.at[:, sibling["c"], :, cols],
                    other.at[span],
                    sends,
                    arrivals,
                    k,
                    sibling,
                )
            )
            mine = pltpu.make_async_copy(
                part.at[:, me["c"], :, cols], own.at[span], local.at[k - 15]
            )
            mine.start()
            copies.append(mine)
            at += rows
            k += 1
    over = [
        remote(
            sided.at[:, quarter(place["grp"])],
            side_in.at[group] if side == "rows" else side_in.at[d],
            sends,
            arrivals,
            13 + d,
            place,
        )
        for d, place in enumerate(groups)
    ]
    kept = pltpu.make_async_copy(
        (sided if side == "rows" else exact).at[:, quarter(group)],
        side_in.at[group] if side == "rows" else mine_exact,
        local.at[0],
    )
    kept.start()
    over.append(kept)
    for copy in copies:
        copy.wait()

    @pl.loop(0, 16)
    def _(k):
        both[k // 4, lax.rem(k, 4)] = (own[k].astype(f32) + other[k].astype(f32)).astype(bf16)

    cut = in_a.shape[-1]
    left, right = pl.ds(0, cut), pl.ds(cut, width - cut)
    copies = []
    for d in range(3):
        to_x, to_y = steps_x[d], steps_y[d]
        copies.append(
            remote(both.at[:, to_x["x"], :, left], in_a.at[d], sends, arrivals, 1 + d, to_x)
        )
        copies.append(
            remote(both.at[to_y["y"], :, :, right], in_b.at[d], sends, arrivals, 4 + d, to_y)
        )
    last = []
    if side == "rows":
        for copy in over:
            copy.wait()
        room = side_in.shape[1] // 32

        def of(place):
            return side_in.at[:, pl.ds(pl.multiple_of(number(place) * room, room), room)]

        for j, place in enumerate(plane):
            last.append(remote(of(place), side_out.at[number(me)], sends, arrivals, k + j, place))
        kept = pltpu.make_async_copy(of(me), side_out.at[number(me)], local.at[0])
        kept.start()
        last.append(kept)
    for copy in copies:
        copy.wait()

    @pl.loop(0, 4)
    def _(k):
        total_a = both[k, me["x"], :, left].astype(f32)
        total_b = both[me["y"], k, :, right].astype(f32)
        for d in range(3):
            total_a += in_a[d, k].astype(f32)
            total_b += in_b[d, k].astype(f32)
        mid_a[k] = total_a.astype(bf16)
        mid_b[k] = total_b.astype(bf16)

    copies = []
    for d in range(3):
        to_x, to_y = steps_x[d], steps_y[d]
        copies.append(remote(mid_a.at[to_y["y"]], end_a.at[d], sends, arrivals, 7 + d, to_y))
        copies.append(remote(mid_b.at[to_x["x"]], end_b.at[d], sends, arrivals, 10 + d, to_x))
    if side == "head":
        for copy in over:
            copy.wait()
        total = mine_exact[...]
        for d in range(3):
            total += side_in[d].astype(f32)
        side_out[...] = total
    for copy in copies:
        copy.wait()
    total_a = mid_a[me["y"]].astype(f32)
    total_b = mid_b[me["x"]].astype(f32)
    for d in range(3):
        total_a += end_a[d].astype(f32)
        total_b += end_b[d].astype(f32)
    out[:, left] = total_a.astype(out.dtype)
    out[:, right] = total_b.astype(out.dtype)
    for copy in last:
        copy.wait()


def sum_and_scatter(parts, width, dtype, side, sided, collective):
    plan = [part.shape[1:] for part in parts]
    rows = sum(r * (c // width) for r, c in plan)
    pieces = sum(c // width for _, c in plan)
    cut = width // 2
    rest = width - cut
    bf16 = jnp.bfloat16
    room = (12 if side == "head" else 28) * 2**20
    tall = sided[0].shape[0]
    if side == "head":
        side_out = jax.ShapeDtypeStruct((tall, 128), jnp.float32)
        side_scratch = [pltpu.VMEM((tall, 128), jnp.float32), pltpu.VMEM((3, tall, 128), bf16)]
    else:
        side_out = jax.ShapeDtypeStruct((32, 4, tall // 32, 128), bf16)
        side_scratch = [pltpu.VMEM((4, tall, 128), bf16)]
    semaphores = 16 + pieces + (len(AROUND) if side == "rows" else 0)
    return pl.pallas_call(
        partial(scatter_sum_kernel, plan, side),
        out_shape=[jax.ShapeDtypeStruct((rows, width), dtype), side_out],
        in_specs=[ANY] * (len(parts) + len(sided)),
        out_specs=[VMEM, VMEM],
        scratch_shapes=side_scratch
        + [
            pltpu.VMEM((16, rows, width), bf16),
            pltpu.VMEM((16, rows, width), bf16),
            pltpu.VMEM((4, 4, rows, width), bf16),
            pltpu.VMEM((3, 4, rows, cut), bf16),
            pltpu.VMEM((3, 4, rows, rest), bf16),
            pltpu.VMEM((4, rows, cut), bf16),
            pltpu.VMEM((4, rows, rest), bf16),
            pltpu.VMEM((3, rows, cut), bf16),
            pltpu.VMEM((3, rows, rest), bf16),
            pltpu.SemaphoreType.DMA((semaphores,)),
            pltpu.SemaphoreType.DMA((semaphores,)),
            pltpu.SemaphoreType.DMA((1 + pieces,)),
        ],
        compiler_params=pltpu.CompilerParams(
            collective_id=collective, has_side_effects=True, vmem_limit_bytes=room
        ),
    )(*[part.reshape(16, 2, *part.shape[1:]) for part in parts], *sided)


def group_sum_kernel(
    head, wants, given, rest, facts, table_out, rest_out, seen, total, rest_in, told, sends, arrivals
):
    f32, bf16 = jnp.float32, jnp.bfloat16
    me = here()
    group = lax.axis_index("grp")
    groups = [{"grp": lax.rem(group + d, 4)} for d in (1, 2, 3)]
    plane = [moved(me, *step) for step in AROUND]
    greet(groups + plane)
    mine = quarter(group)
    early = [
        remote(rest.at[:, quarter(groups[d]["grp"])], rest_in.at[d], sends, arrivals, d, groups[d])
        for d in range(3)
    ]
    total[...] = head[...]

    @pl.loop(0, wants.shape[0])
    def _(k):
        row = lax.broadcasted_iota(jnp.int32, (head.shape[0], wants.shape[1]), 0)
        hot = jnp.where(row == wants[pl.ds(k, 1), :], 1.0, 0.0).astype(bf16)
        total[...] += product(hot, given[k])

    rounded = total[...].astype(bf16)
    table_out[:, mine] = rounded
    rounded = rounded.astype(f32)
    squares = jnp.sum(by_eight(rounded * rounded), 0)
    wide = [
        remote(table_out.at[:, mine], table_out.at[:, mine], sends, arrivals, 3 + d, groups[d])
        for d in range(3)
    ]
    for copy in early:
        copy.wait()
    summed = rest[:, mine].astype(f32)
    for d in range(3):
        summed += rest_in[d].astype(f32)
    summed = summed.astype(bf16)
    rest_out[:, mine] = summed
    summed = summed.astype(f32)
    squares += jnp.sum(by_eight(summed * summed), 0)
    told[group, 0:8] = squares
    told[group, 8:16] = facts[...]
    copies = []
    for d in range(3):
        copies.append(remote(told.at[group], told.at[group], sends, arrivals, 6 + d, groups[d]))
        wide.append(
            remote(rest_out.at[:, mine], rest_out.at[:, mine], sends, arrivals, 9 + d, groups[d])
        )
    for copy in copies:
        copy.wait()
    seen[number(me)] = told[0] + told[1] + told[2] + told[3]
    copies = []
    for k, place in enumerate(plane):
        copies.append(
            remote(seen.at[number(me)], seen.at[number(me)], sends, arrivals, 12 + k, place)
        )
    for copy in copies + wide:
        copy.wait()


def sum_of_groups(head, wants, given, rest, facts, collective):
    count = 12 + len(AROUND)
    bf16 = jnp.bfloat16
    return pl.pallas_call(
        group_sum_kernel,
        out_shape=[
            jax.ShapeDtypeStruct((head.shape[0], 512), bf16),
            jax.ShapeDtypeStruct(rest.shape, rest.dtype),
            jax.ShapeDtypeStruct((32, 16, 128), jnp.float32),
        ],
        in_specs=[VMEM] * 5,
        out_specs=[VMEM, VMEM, VMEM],
        scratch_shapes=[
            pltpu.VMEM(head.shape, jnp.float32),
            pltpu.VMEM((3, rest.shape[0], 128), rest.dtype),
            pltpu.VMEM((4, 16, 128), jnp.float32),
            pltpu.SemaphoreType.DMA((count,)),
            pltpu.SemaphoreType.DMA((count,)),
        ],
        compiler_params=pltpu.CompilerParams(
            collective_id=collective, has_side_effects=True, vmem_limit_bytes=40 * 2**20
        ),
    )(head, wants, given, rest, facts)


def slots(tokens, own_rows):
    count = tokens.shape[0]
    row, column = tokens[:, None], tokens[None, :]
    place = jnp.arange(count)
    repeated = jnp.any((row == column) & (place[:, None] < place[None, :]), axis=0)
    owner = tokens // own_rows
    counts = ~repeated[:, None] & (row >= (owner * own_rows)[None, :]) & (row < column)
    return owner, ~repeated, jnp.sum(counts.astype(jnp.int32), axis=0)


def slot_in_round(owner, rank, room, turn, apart=None):
    at = rank - turn * room
    return jnp.where((at >= 0) & (at < room), owner * (apart or room) + at, -1)


def wanted_rows(slot, first, local, places):
    hit = (jnp.where(first, slot, -1)[:, None] == jnp.arange(places)[None, :])
    return jnp.sum(jnp.where(hit, local[:, None] + 1, 0), axis=0) - 1


def one_hot(index, count):
    return (index[:, None] == jnp.arange(count)[None, :]).astype(jnp.bfloat16)


def product(left, right):
    return jnp.dot(left, right, preferred_element_type=jnp.float32)


def folded(rows):
    return jnp.concatenate(jnp.split(rows, 2, axis=2), axis=1)


def unfolded(rows):
    return jnp.concatenate(jnp.split(rows, 2, axis=1), axis=2)


def layer_norm(value, gain, shift):
    mean = jnp.mean(value, -1, keepdims=True)
    centred = value - mean
    var = jnp.mean(centred * centred, -1, keepdims=True)
    return centred * lax.rsqrt(var + norm_eps) * gain + shift


def project(left, right):
    return jnp.einsum("blk,kn->bln", left, right, preferred_element_type=jnp.float32)


def split_heads(packed, width):
    batch, span = (packed.shape[0], packed.shape[1])
    return [
        packed[:, :, piece * width : (piece + 1) * width].reshape(batch, span, width // HD, HD)
        for piece in range(3)
    ]


def masked_scores(query, keyed, lengths):
    scores = jnp.einsum(
        "bqhd,bkhd->bhqk", query, keyed, preferred_element_type=jnp.float32
    ) * HD ** (-0.5)
    valid = jnp.arange(query.shape[1])[None, :] < lengths[:, None]
    return jnp.where(valid[:, None, None, :], scores, -1e30)


def forward(embedded, lengths, weights):
    w_qkv, w_out, w_up, w_down, norms = weights
    norms = norms.astype(jnp.float32)
    width = w_out.shape[1]
    first = layer_norm(embedded, norms[:, 0], norms[:, 1])
    first_low = first.astype(jnp.bfloat16)
    packed = project(first_low, w_qkv).astype(jnp.bfloat16)
    query, keyed, valued = split_heads(packed, width)
    scores = masked_scores(query, keyed, lengths)
    top = jnp.max(scores, -1, keepdims=True)
    total = jnp.sum(jnp.exp(scores - top), -1, keepdims=True)
    probs = (jnp.exp(scores - top) / total).astype(jnp.bfloat16)
    context = jnp.einsum("bhqk,bkhd->bqhd", probs, valued, preferred_element_type=jnp.float32)
    context = context.reshape(first.shape).astype(jnp.bfloat16)
    joined = first + project(context, w_out)
    second = layer_norm(joined, norms[:, 2], norms[:, 3])
    second_low = second.astype(jnp.bfloat16)
    hidden_pre = project(second_low, w_up)
    active = jax.nn.gelu(hidden_pre, approximate=False).astype(jnp.bfloat16)
    summed = second + project(active, w_down)
    final = layer_norm(summed, norms[:, 4], norms[:, 5])
    saved = (
        embedded,
        first_low,
        packed,
        context,
        joined,
        second_low,
        hidden_pre,
        active,
        summed,
    )
    return (final, saved)


def norm_back(value, gain, grad):
    mean = jnp.mean(value, -1, keepdims=True)
    centred = value - mean
    scale = lax.rsqrt(jnp.mean(centred * centred, -1, keepdims=True) + norm_eps)
    unit = centred * scale
    scaled = grad * gain
    back = scaled - jnp.mean(scaled, -1, keepdims=True)
    back = scale * (back - unit * jnp.mean(scaled * unit, -1, keepdims=True))
    return back, jnp.sum(grad * unit, 0, keepdims=True), jnp.sum(grad, 0, keepdims=True)


def product_of(left, right, dims):
    return lax.dot_general(left, right, (dims, ((), ())), preferred_element_type=jnp.float32)


def backward_kernel(
    lengths,
    picks,
    slot,
    grad_rows,
    embedded,
    first_low,
    packed,
    context,
    joined,
    second_low,
    hidden_pre,
    active,
    summed,
    norms,
    w_qkv,
    w_out,
    w_up,
    w_down,
    g_qkv,
    g_out,
    g_up,
    g_down,
    g_emb,
    g_norms,
    given,
    d_packed,
    d_context,
    carried,
):
    f32, bf16 = jnp.float32, jnp.bfloat16
    span, width = embedded.shape
    rows, columns, both = ((0,), (0,)), ((1,), (1,)), ((1,), (0,))
    row = lax.broadcasted_iota(jnp.int32, (span, picks.shape[1]), 0)
    hot = jnp.where(row == picks[...], 1.0, 0.0)
    d_final = jnp.dot(
        hot, grad_rows[...], preferred_element_type=f32, precision=lax.Precision.HIGHEST
    )
    d_summed, gain_c, shift_c = norm_back(summed[...], norms[4:5], d_final)
    d_ffn = d_summed.astype(bf16)
    carried[...] = d_summed

    @pl.loop(0, w_up.shape[1] // width)
    def _(k):
        cols = pl.ds(pl.multiple_of(k * width, width), width)
        g_down[cols] = product_of(active[:, cols], d_ffn, rows).astype(bf16)
        pre = hidden_pre[:, cols]
        slope = 0.5 * (1.0 + lax.erf(pre * (0.5**0.5)))
        slope += pre * (jnp.exp(-0.5 * pre * pre) * (0.5 / math.pi) ** 0.5)
        d_up = (slope * product_of(d_ffn, w_down[cols], columns)).astype(bf16)
        g_up[:, cols] = product_of(second_low[...], d_up, rows).astype(bf16)
        carried[...] += product_of(d_up, w_up[:, cols], columns)

    d_joined, gain_b, shift_b = norm_back(joined[...], norms[2:3], carried[...])
    d_attn = d_joined.astype(bf16)
    g_out[...] = product_of(context[...], d_attn, rows).astype(bf16)
    d_context[...] = product_of(d_attn, w_out[...], columns).astype(bf16)
    lane = lax.broadcasted_iota(jnp.int32, (span, 2 * HD), 1)
    halves = [jnp.where(lane < HD, 1.0, 0.0), jnp.where(lane < HD, 0.0, 1.0)]
    valid = lax.broadcasted_iota(jnp.int32, (span, span), 1) < lengths[0, 0]

    @pl.loop(0, width // (2 * HD))
    def _(k):
        at = pl.multiple_of(k * 2 * HD, 2 * HD)
        query, keyed, valued = [
            packed[:, pl.ds(piece * width + at, 2 * HD)] for piece in range(3)
        ]
        d_heads = d_context[:, pl.ds(at, 2 * HD)]
        d_query, d_keyed, d_valued = [jnp.zeros((span, 2 * HD), f32)] * 3
        for half in halves:
            low = half.astype(bf16)
            scores = product_of(query * low, keyed, columns) * HD ** (-0.5)
            scores = jnp.where(valid, scores, -1e30)
            spread = jnp.exp(scores - jnp.max(scores, -1, keepdims=True))
            probs = spread * (1.0 / jnp.sum(spread, -1, keepdims=True))
            d_valued += half * product_of(probs.astype(bf16), d_heads, rows)
            d_probs = product_of(d_heads * low, valued, columns)
            d_scores = probs * (d_probs - jnp.sum(probs * d_probs, -1, keepdims=True))
            d_scores = d_scores.astype(bf16)
            d_query += half * product_of(d_scores, keyed, both)
            d_keyed += half * product_of(d_scores, query, rows)
        for piece, value in enumerate((d_query * HD ** (-0.5), d_keyed * HD ** (-0.5), d_valued)):
            d_packed[:, pl.ds(piece * width + at, 2 * HD)] = value.astype(bf16)

    carried[...] = d_joined

    @pl.loop(0, 3)
    def _(k):
        cols = pl.ds(pl.multiple_of(k * width, width), width)
        g_qkv[:, cols] = product_of(first_low[...], d_packed[:, cols], rows).astype(bf16)
        carried[...] += product_of(d_packed[:, cols], w_qkv[:, cols], columns)

    d_emb, gain_a, shift_a = norm_back(embedded[...], norms[0:1], carried[...])
    g_emb[...] = d_emb
    lines = [gain_a, shift_a, gain_b, shift_b, gain_c, shift_c, jnp.zeros((2, width), f32)]
    g_norms[...] = jnp.concatenate(lines, axis=0)
    low = d_emb.astype(bf16)

    @pl.loop(0, given.shape[0] // span)
    def _(k):
        place = lax.broadcasted_iota(jnp.int32, (span, span), 0) + k * span
        place = jnp.where(place == slot[...], 1.0, 0.0).astype(bf16)
        given[pl.ds(pl.multiple_of(k * span, span), span)] = product(place, low).astype(bf16)


def backward(lengths, picks, slot, places, weights, saved, grad_rows):
    w_qkv, w_out, w_up, w_down, norms = weights
    span, width = saved[0].shape[1:]
    f32, bf16 = jnp.float32, jnp.bfloat16
    return pl.pallas_call(
        backward_kernel,
        out_shape=[
            jax.ShapeDtypeStruct(w_qkv.shape, bf16),
            jax.ShapeDtypeStruct(w_out.shape, bf16),
            jax.ShapeDtypeStruct(w_up.shape, bf16),
            jax.ShapeDtypeStruct(w_down.shape, bf16),
            jax.ShapeDtypeStruct((span, width), f32),
            jax.ShapeDtypeStruct((8, width), f32),
            jax.ShapeDtypeStruct((places, width), bf16),
        ],
        in_specs=[pl.BlockSpec(memory_space=pltpu.SMEM)] + [VMEM] * 17,
        out_specs=[VMEM] * 7,
        scratch_shapes=[
            pltpu.VMEM((span, 3 * width), bf16),
            pltpu.VMEM((span, width), bf16),
            pltpu.VMEM((span, width), f32),
        ],
        compiler_params=pltpu.CompilerParams(vmem_limit_bytes=32 * 2**20),
    )(
        lengths[None],
        picks,
        slot[None],
        grad_rows,
        *[value[0] for value in saved],
        norms.astype(f32).T,
        w_qkv,
        w_out,
        w_up,
        w_down,
    )


def per_device(
    ids,
    lengths,
    picks,
    labels,
    s_table,
    s_pos,
    s_qkv,
    s_out,
    s_up,
    s_down,
    s_norms,
    m_table,
    m_pos,
    m_qkv,
    m_out,
    m_up,
    m_down,
    m_norms,
    a_table,
    a_pos,
    a_qkv,
    a_out,
    a_up,
    a_down,
    a_norms,
    t_table,
    t_pos,
    t_qkv,
    t_out,
    t_up,
    t_down,
    t_norms,
):
    masters = (s_table, s_pos, s_qkv, s_out, s_up, s_down, s_norms)
    momenta = (m_table, m_pos, m_qkv, m_out, m_up, m_down, m_norms)
    averages = (a_table, a_pos, a_qkv, a_out, a_up, a_down, a_norms)
    f32, bf16 = jnp.float32, jnp.bfloat16
    fsdp = lax.axis_size(FSDP)
    width, t_width = s_table.shape[1], t_table.shape[2]
    vocab_own = s_table.shape[0]
    picked = picks.shape[1]
    span = ids.shape[1]

    facts = jnp.concatenate([ids, picks, jnp.broadcast_to(lengths[:, None], (1, 64))], axis=1)
    facts = jnp.pad(facts.reshape(3, 128), ((0, 5), (0, 0)))
    facts = exchange_groups(jnp.broadcast_to(facts, (4, 8, 128)), 9)[:, :3].reshape(4, -1)
    group_ids, group_picks = facts[:, :span], facts[:, span : span + picked]
    group_lengths = facts[:, span + picked]
    own_table = s_table.astype(bf16)
    t_owner, t_first, t_rank = slots(group_ids.reshape(-1), vocab_own)
    s_owners, s_firsts, s_ranks = jax.vmap(lambda one: slots(one, vocab_own))(group_ids)
    my_group = lax.axis_index("grp")
    s_owner, s_rank = (
        lax.dynamic_index_in_dim(v, my_group, 0, keepdims=False) for v in (s_owners, s_ranks)
    )
    most = jnp.maximum(jnp.max(t_rank) // T_ROOM, jnp.max(s_ranks) // S_ROOM) + 1
    t_local = group_ids.reshape(-1) - t_owner * vocab_own
    s_locals = group_ids - s_owners * vocab_own

    def asked(turn):
        t_slot = slot_in_round(t_owner, t_rank, T_ROOM, turn)
        s_slot = slot_in_round(s_owner, s_rank, S_ROOM, turn)
        t_ask = wanted_rows(t_slot, t_first, t_local, fsdp * T_ROOM).reshape(fsdp, T_ROOM)
        s_asks = jax.vmap(partial(wanted_rows, places=fsdp * S_APART))(
            slot_in_round(s_owners, s_ranks, S_ROOM, turn, S_APART), s_firsts, s_locals
        ).reshape(-1, fsdp, S_APART)
        s_ask = lax.dynamic_index_in_dim(s_asks, my_group, 0, keepdims=False)[:, :S_ROOM]
        s_asks = jnp.moveaxis(s_asks, 0, 1).reshape(fsdp, -1)
        return t_slot, s_slot, t_ask, s_ask, s_asks

    def answer(t_want, s_want):
        t_sent = product(one_hot(t_want.reshape(-1), vocab_own), t_table[0]).astype(bf16)
        s_sent = product(one_hot(s_want.reshape(-1), vocab_own), own_table).astype(bf16)
        return jnp.concatenate(
            [t_sent.reshape(fsdp, T_ROOM, t_width), folded(s_sent.reshape(fsdp, S_ROOM, width))],
            axis=2,
        )

    def placed(got, t_slot, s_slot):
        t_got = got[:, :, :t_width].reshape(-1, t_width)
        s_got = unfolded(got[:, :, t_width:]).reshape(-1, width)
        return (
            product(one_hot(t_slot, fsdp * T_ROOM), t_got),
            product(one_hot(s_slot, fsdp * S_ROOM), s_got),
        )

    def swap(value):
        return lax.all_to_all(value, FSDP, split_axis=0, concat_axis=0, tiled=True)

    def ask_again(turn):
        t_slot, s_slot, t_ask, s_ask, s_asks = asked(turn)
        wants = swap(jnp.concatenate([t_ask, s_ask, s_asks], axis=1))
        both = T_ROOM + S_ROOM
        return t_slot, s_slot, wants[:, :T_ROOM], wants[:, T_ROOM:both], wants[:, both:]

    def more_rows(state):
        turn, t_emb, s_emb = state
        t_slot, s_slot, t_want, s_want, _ = ask_again(turn)
        t_more, s_more = placed(swap(answer(t_want, s_want)), t_slot, s_slot)
        return turn + 1, t_emb + t_more.astype(bf16), s_emb + s_more.astype(bf16)

    t_slot, s_slot, t_ask, s_ask, s_asks = asked(0)
    line = jnp.concatenate(
        [t_ask, s_ask, jnp.broadcast_to(most, (fsdp, 128 - T_ROOM - S_ROOM))], axis=1
    )
    lines = [
        line,
        jnp.broadcast_to(jnp.concatenate([picks, labels], axis=1), (fsdp, 2 * picked)),
        jnp.broadcast_to(lengths[:, None], (fsdp, 128)),
        s_asks,
    ]
    notes = jnp.stack(lines + [jnp.zeros((fsdp, 128), jnp.int32)] * 4, axis=1)
    notes, got = route(notes, t_table[0], own_table, 1)
    wants = notes[:, 3]
    rounds = jnp.max(notes[:, 0, T_ROOM + S_ROOM])
    plane_picks, plane_labels = notes[:, 1, :picked], notes[:, 1, picked : 2 * picked]
    plane_lengths = notes[:, 2, 0]
    nothing = (jnp.zeros((t_slot.shape[0], t_width), bf16), jnp.zeros((span, width), bf16))
    _, t_extra, s_extra = lax.while_loop(
        lambda state: state[0] < rounds, more_rows, (jnp.int32(1), *nothing)
    )

    def pieces(blocks, qkv, out, up, down, pos, norms):
        tail = norms.astype(f32).reshape(blocks, 1, -1)
        tail = jnp.pad(tail, ((0, 0), (0, 7), (0, width - tail.shape[2])))
        small = jnp.concatenate([pos.reshape(blocks, -1, width).astype(f32), tail], axis=1)
        big = [part.astype(bf16).reshape(blocks, -1, part.shape[1]) for part in (qkv, out, up, down)]
        return big + [lax.optimization_barrier(small.astype(bf16))]

    def pack(parts):
        columns = [
            part[:, :, at : at + width] for part in parts for at in range(0, part.shape[2], width)
        ]
        return jnp.concatenate(columns, axis=1)

    def unpack(packed):
        blocks, lead = packed.shape[0], s_qkv.shape[0]

        def across(at, count):
            return jnp.concatenate(
                [
                    packed[:, at + k * lead : at + (k + 1) * lead].reshape(-1, width)
                    for k in range(count)
                ],
                axis=1,
            )

        at_out = s_qkv.shape[1] // width * lead
        at_up = at_out + lead
        at_down = at_up + s_up.shape[1] // width * lead
        at_pos = at_down + s_down.shape[0]
        at_norms = at_pos + s_pos.shape[0]
        return (
            across(0, s_qkv.shape[1] // width),
            across(at_out, 1),
            across(at_up, s_up.shape[1] // width),
            packed[:, at_down:at_pos].reshape(-1, width),
            packed[:, at_pos:at_norms].reshape(-1, width),
            packed[:, at_norms, : s_norms.size].reshape(-1, s_norms.shape[1]),
        )

    own_packed = pack(pieces(1, s_qkv, s_out, s_up, s_down, s_pos, s_norms))
    w_qkv, w_out, w_up, w_down, positions, norms = unpack(
        lax.all_gather(own_packed, FSDP, axis=0, tiled=True)
    )
    student = (w_qkv, w_out, w_up, w_down, norms)
    heads = lax.all_gather(t_table[0], "grp", axis=0, tiled=False)

    taken = teacher_rows(
        group_lengths,
        t_slot,
        group_picks,
        got.reshape(-1, got.shape[2]),
        t_extra.reshape(-1, span, t_width),
        t_pos[0],
        t_norms[0].astype(f32).T,
        t_qkv[0],
        t_out[0],
        t_up[0],
        t_down[0],
    )
    taken, heads = lax.optimization_barrier((taken, heads))
    rows = exchange_groups(taken, 10)
    s_extra, got, rows = lax.optimization_barrier((s_extra, got, rows))
    rows = lax.all_gather(rows, FSDP, axis=0, tiled=False)

    s_got = unfolded(got[:, :, t_width:]).reshape(-1, width)
    s_emb = product(one_hot(s_slot, fsdp * S_ROOM), s_got) + s_extra.astype(f32)
    embedded = s_emb[None] + positions.astype(f32)[None]
    final, saved = forward(embedded, lengths, student)
    own_rows = jnp.take_along_axis(final, picks[:, :, None], axis=1).astype(bf16)[0]
    h = gather_plane(own_rows, 11)
    base = lax.axis_index(FSDP) * vocab_own
    labels_here = plane_labels.reshape(1, -1) - base
    z, z_stats = vocabulary_logits(labels_here, h.reshape(fsdp, 1, picked, width), own_table[None])
    logits, stats = vocabulary_logits(labels_here, rows, heads)
    stats = jnp.concatenate([stats, z_stats], axis=0)
    plane_counted = (plane_picks < plane_lengths[:, None]).astype(f32).reshape(-1, 1, 2 * picked)
    chip = lax.axis_index(("y", "x"))
    chip_counted = lax.dynamic_index_in_dim(plane_counted, chip, 0, keepdims=False)
    shift, own_loss = blend(stats, chip_counted, 3)
    head_grad, head_low, grad_rows, crossed = head_grads(logits, z, shift, h, own_table)
    count_local = jnp.sum((picks < lengths[:, None]).astype(f32))
    loss_local = jnp.sum(own_loss) - jnp.sum(crossed)
    grad_rows, head_grad = sum_and_scatter(
        [grad_rows.reshape(fsdp, picked, width)], width, f32, "head", [head_grad, head_low], 5
    )

    g_slot = slot_in_round(s_owner, s_rank, S_ROOM, 0, S_APART)
    g_qkv, g_out, g_up, g_down, g_pos, g_norms, given_rows = backward(
        lengths, picks, g_slot, fsdp * S_APART, student, saved, grad_rows
    )
    low_embedded = g_pos.astype(bf16)

    def given(turn):
        slot = slot_in_round(s_owner, s_rank, S_ROOM, turn, S_APART)
        hot = (jnp.arange(fsdp * S_APART)[:, None] == slot[None, :]).astype(bf16)
        return product(hot, low_embedded).astype(bf16)

    def more_grads(state):
        turn, total = state
        wants = ask_again(turn)[4]
        rows = jnp.stack(jnp.split(given(turn), 4, axis=1))
        rows = lax.all_to_all(rows, "grp", split_axis=0, concat_axis=0, tiled=True)
        rows = swap(jnp.moveaxis(rows.reshape(4, fsdp, S_APART, -1), 0, 1))
        hot = one_hot(wants.reshape(-1), vocab_own).T
        return turn + 1, total + product(hot, rows.reshape(-1, rows.shape[3]))

    _, head_grad = lax.while_loop(
        lambda state: state[0] < rounds, more_grads, (jnp.int32(1), head_grad)
    )
    g_norms = g_norms[:6].T
    parts = pieces(fsdp, g_qkv, g_out, g_up, g_down, g_pos, g_norms)
    rest, got = sum_and_scatter(parts, width, bf16, "rows", [given_rows], 7)
    row = jnp.arange(8)[:, None]
    column_of = jnp.arange(128)[None, :]
    told = jnp.where((row == 0) & (column_of == 0), loss_local, 0.0)
    told += jnp.where((row == 1) & (column_of == 0), count_local, 0.0)
    table_sum, rest_sum, seen = sum_of_groups(
        head_grad, wants.reshape(4, -1), got.reshape(4, -1, got.shape[3]), rest, told, 8
    )
    seen = seen.sum(0)
    squares, loss_sum, count = jnp.sum(seen[:8]), seen[8, 0], seen[9, 0]
    at_norms = rest_sum.shape[0] - 8
    norms_sum = rest_sum[at_norms, : s_norms.size].astype(f32).reshape(s_norms.shape).T
    turned = [group[:6] + (group[6].T,) for group in (masters, momenta, averages)]
    clip_norm = jnp.sqrt(squares) / count
    factor = jnp.minimum(1.0, clip_limit / clip_norm) / count
    outs = update(factor, table_sum, rest_sum, norms_sum, *turned)
    outs = tuple(out.T if k % 7 == 6 else out for k, out in enumerate(outs))
    return (loss_sum, count, clip_norm) + outs


def solution(mesh):
    finer = Mesh(
        mesh.devices.reshape(mesh.shape["grp"], 4, 4, 2), ("grp", "y", "x", "c")
    )
    return jax.shard_map(
        per_device,
        mesh=finer,
        in_specs=(
            P(GRP_FSDP, None),
            P(GRP_FSDP),
            P(GRP_FSDP, None),
            P(GRP_FSDP, None),
            P(FSDP, None),
            P(FSDP, None),
            P(FSDP, None),
            P(FSDP, None),
            P(FSDP, None),
            P(FSDP, None),
            P(FSDP, None),
            P(FSDP, None),
            P(FSDP, None),
            P(FSDP, None),
            P(FSDP, None),
            P(FSDP, None),
            P(FSDP, None),
            P(FSDP, None),
            P(FSDP, None),
            P(FSDP, None),
            P(FSDP, None),
            P(FSDP, None),
            P(FSDP, None),
            P(FSDP, None),
            P(FSDP, None),
            P("grp", FSDP, None),
            P("grp", None, None),
            P("grp", None, None),
            P("grp", None, None),
            P("grp", None, None),
            P("grp", None, None),
            P("grp", None, None),
        ),
        out_specs=(
            P(),
            P(),
            P(),
            P(FSDP, None),
            P(FSDP, None),
            P(FSDP, None),
            P(FSDP, None),
            P(FSDP, None),
            P(FSDP, None),
            P(FSDP, None),
            P(FSDP, None),
            P(FSDP, None),
            P(FSDP, None),
            P(FSDP, None),
            P(FSDP, None),
            P(FSDP, None),
            P(FSDP, None),
            P(FSDP, None),
            P(FSDP, None),
            P(FSDP, None),
            P(FSDP, None),
            P(FSDP, None),
            P(FSDP, None),
            P(FSDP, None),
        ),
        check_vma=False,
    )
```

```python
import functools
import math
from functools import partial

import jax
import jax.numpy as jnp
from jax import lax
from jax.experimental import pallas as pl
from jax.experimental.pallas import tpu as pltpu
from jax.sharding import Mesh
from jax.sharding import PartitionSpec as P

HD = 64
FSDP = ("y", "x", "c")
GRP_FSDP = ("grp", "y", "x", "c")
T_ROOM = 48
S_ROOM = 24
S_APART = 32
WIDE = 56 * 2**20

norm_eps = 1e-12
clip_limit = 0.001
learn_rate = 100000.0
momentum_decay = 0.9
average_decay = 0.9


SIZES = {"y": 4, "x": 4, "c": 2}
MESH = pl.DeviceIdType.MESH
ANY = pl.BlockSpec(memory_space=pl.ANY)
VMEM = pl.BlockSpec(memory_space=pltpu.VMEM)
AROUND = [((11 * k) % 32 // 8, (11 * k) % 8 // 2, (11 * k) % 2) for k in range(1, 32)]


def here():
    return {axis: lax.axis_index(axis) for axis in SIZES}


def moved(me, dy, dx, dc):
    return {
        "y": lax.rem(me["y"] + dy, 4),
        "x": lax.rem(me["x"] + dx, 4),
        "c": lax.rem(me["c"] + dc, 2),
    }


def number(place):
    return (place["y"] * 4 + place["x"]) * 2 + place["c"]


def greet(places):
    barrier = pltpu.get_barrier_semaphore()
    for place in places:
        pl.semaphore_signal(barrier, inc=1, device_id=place, device_id_type=MESH)
    pl.semaphore_wait(barrier, len(places))


def remote(source, target, sends, arrivals, at, place):
    copy = pltpu.make_async_remote_copy(
        src_ref=source,
        dst_ref=target,
        send_sem=sends.at[at],
        recv_sem=arrivals.at[at],
        device_id=place,
        device_id_type=MESH,
    )
    copy.start()
    return copy


def route_kernel(notes, t_table, s_table, heard, got, sent, wants, sends, arrivals, local):
    f32, bf16 = jnp.float32, jnp.bfloat16
    me = here()
    greet([moved(me, *step) for step in AROUND])
    copies = []
    for k, step in enumerate(AROUND):
        place = moved(me, *step)
        copies.append(
            remote(notes.at[number(place)], heard.at[number(me)], sends, arrivals, k, place)
        )
    heard[number(me)] = notes[number(me)]
    for copy in copies:
        copy.wait()
    all_wants = heard[:, 0, :].astype(f32).T
    vocab, t_width = t_table.shape
    half = s_table.shape[1] // 2
    batch = wants.shape[2]
    for k in range(wants.shape[0]):
        wants[k] = all_wants[:, k * batch : (k + 1) * batch]

    def rows_of(k, at, room, table):
        index = jnp.concatenate(
            [wants[k, at : at + room, p : p + 1] for p in range(batch)], axis=0
        )
        entry = lax.broadcasted_iota(jnp.int32, (index.shape[0], vocab), 1).astype(f32)
        hot = jnp.where(entry == index, 1.0, 0.0).astype(bf16)
        return product(hot, table[...])

    @pl.loop(0, wants.shape[0])
    def _(k):
        t_rows = rows_of(k, 0, T_ROOM, t_table)
        s_rows = rows_of(k, T_ROOM, S_ROOM, s_table)
        for j in range(batch):
            p = k * batch + j
            sent[p, :, :t_width] = t_rows[j * T_ROOM : (j + 1) * T_ROOM].astype(bf16)
            own = s_rows[j * S_ROOM : (j + 1) * S_ROOM]
            own = jnp.concatenate([own[:, :half], own[:, half:]], axis=0)
            sent[p, :, t_width:] = own.astype(bf16)

    copies = []
    for k, step in enumerate(AROUND):
        place = moved(me, *step)
        copies.append(
            remote(
                sent.at[number(place)], got.at[number(me)], sends, arrivals, len(AROUND) + k, place
            )
        )
    mine = pltpu.make_async_copy(sent.at[number(me)], got.at[number(me)], local)
    mine.start()
    mine.wait()
    for copy in copies:
        copy.wait()


def route(notes, t_table, s_table, collective):
    width = t_table.shape[1] + s_table.shape[1] // 2
    return pl.pallas_call(
        route_kernel,
        out_shape=[
            jax.ShapeDtypeStruct(notes.shape, notes.dtype),
            jax.ShapeDtypeStruct((32, T_ROOM, width), jnp.bfloat16),
        ],
        in_specs=[VMEM, VMEM, VMEM],
        out_specs=[VMEM, ANY],
        scratch_shapes=[
            pltpu.VMEM((32, T_ROOM, width), jnp.bfloat16),
            pltpu.VMEM((4, 128, 8), jnp.float32),
            pltpu.SemaphoreType.DMA((2 * len(AROUND),)),
            pltpu.SemaphoreType.DMA((2 * len(AROUND),)),
            pltpu.SemaphoreType.DMA,
        ],
        compiler_params=pltpu.CompilerParams(
            collective_id=collective, has_side_effects=True, vmem_limit_bytes=40 * 2**20
        ),
    )(notes, t_table, s_table)


def group_exchange_kernel(source, target, sends, arrivals, local):
    group = lax.axis_index("grp")
    groups = [lax.rem(group + d, 4) for d in (1, 2, 3)]
    greet([{"grp": g} for g in groups])
    copies = [
        remote(source.at[g], target.at[group], sends, arrivals, d, {"grp": g})
        for d, g in enumerate(groups)
    ]
    own = pltpu.make_async_copy(source.at[group], target.at[group], local)
    own.start()
    own.wait()
    for copy in copies:
        copy.wait()


def exchange_groups(value, collective):
    return pl.pallas_call(
        group_exchange_kernel,
        out_shape=jax.ShapeDtypeStruct(value.shape, value.dtype),
        in_specs=[ANY],
        out_specs=ANY,
        scratch_shapes=[
            pltpu.SemaphoreType.DMA((3,)),
            pltpu.SemaphoreType.DMA((3,)),
            pltpu.SemaphoreType.DMA,
        ],
        compiler_params=pltpu.CompilerParams(collective_id=collective, has_side_effects=True),
    )(value)


def gather_kernel(source, target, sends, arrivals, local):
    me = here()
    chip, core = me["y"] * 4 + me["x"], me["c"]
    chips = [moved(me, (7 * k) % 16 // 4, (7 * k) % 4, 0) for k in range(1, 16)]
    sibling = moved(me, 0, 0, 1)
    greet(chips + [sibling])
    copies = [
        remote(source, target.at[chip, core], sends, arrivals, k, place)
        for k, place in enumerate(chips)
    ]
    own = pltpu.make_async_copy(source, target.at[chip, core], local)
    own.start()
    own.wait()
    for copy in copies:
        copy.wait()
    remote(target.at[:, core], target.at[:, core], sends, arrivals, 15, sibling).wait()


def gather_plane(value, collective):
    rows, width = value.shape
    out = pl.pallas_call(
        gather_kernel,
        out_shape=jax.ShapeDtypeStruct((16, 2, rows, width), value.dtype),
        in_specs=[ANY],
        out_specs=ANY,
        scratch_shapes=[
            pltpu.SemaphoreType.DMA((16,)),
            pltpu.SemaphoreType.DMA((16,)),
            pltpu.SemaphoreType.DMA,
        ],
        compiler_params=pltpu.CompilerParams(collective_id=collective, has_side_effects=True),
    )(value)
    return out.reshape(32 * rows, width)


def update_kernel(seen, table_grad, rest_grad, *refs):
    masters, momenta, averages = refs[:7], refs[7:14], refs[14:21]
    loss_sum, count_out, clip_out = refs[21:24]
    outs = refs[24:]
    facts = jnp.sum(seen[...], 0)
    squares, loss, count = [jnp.sum(line) for line in (facts[:8], facts[8:9], facts[9:10])]
    clip = jnp.sqrt(jnp.full((8, 128), squares)) / count
    factor = (jnp.minimum(1.0, clip_limit / clip) / count)[0:1, 0:1]

    def step(k, grad):
        clipped = grad * factor
        moment = momentum_decay * momenta[k][...] + clipped
        weight = masters[k][...] - learn_rate * (clipped + momentum_decay * moment)
        outs[k][...] = weight
        outs[7 + k][...] = moment
        outs[14 + k][...] = average_decay * averages[k][...] + (1.0 - average_decay) * weight

    step(0, table_grad[...].astype(jnp.float32))

    @pl.when(pl.program_id(0) == 0)
    def _():
        loss_sum[0, 0] = loss
        count_out[0, 0] = count
        clip_out[...] = clip
        width = rest_grad.shape[1]
        at = 0
        for k in (2, 3, 4, 5):
            rows, columns = masters[k].shape
            blocks = []
            for _ in range(columns // width):
                blocks.append(rest_grad[at : at + rows].astype(jnp.float32))
                at += rows
            step(k, blocks[0] if len(blocks) == 1 else jnp.concatenate(blocks, axis=1))
        small = rest_grad[at : at + 16].astype(jnp.float32)
        step(1, small[:8])
        step(6, small[8 : 8 + masters[6].shape[0], : masters[6].shape[1]])


def update(seen, table_grad, rest_grad, masters, momenta, averages):
    steps = 5
    rows, width = table_grad.shape

    def whole(shape):
        return pl.BlockSpec(shape, lambda i: (0,) * len(shape))

    tall = pl.BlockSpec((rows // steps, width), lambda i: (i, 0))
    states = [tall] + [whole(m.shape) for m in masters[1:]]
    scalar = pl.BlockSpec(memory_space=pltpu.SMEM)
    one = jax.ShapeDtypeStruct((1, 1), jnp.float32)
    tile = jax.ShapeDtypeStruct((8, 128), jnp.float32)
    return pl.pallas_call(
        update_kernel,
        grid=(steps,),
        out_shape=[one, one, tile]
        + [jax.ShapeDtypeStruct(m.shape, m.dtype) for m in masters] * 3,
        in_specs=[whole(seen.shape), tall, whole(rest_grad.shape)] + states * 3,
        out_specs=[scalar, scalar, whole(tile.shape)] + states * 3,
        compiler_params=pltpu.CompilerParams(vmem_limit_bytes=WIDE),
    )(seen, table_grad, rest_grad, *masters, *momenta, *averages)


def normed(value, gain, shift):
    mean = jnp.mean(value, -1, keepdims=True)
    centred = value - mean
    var = jnp.mean(centred * centred, -1, keepdims=True)
    return centred * lax.rsqrt(var + norm_eps) * gain + shift


def teacher_kernel(
    lengths, slot, picks, got, extra, pos, norms, w_qkv, w_out, w_up, w_down, out, qkv, ctx
):
    f32, bf16 = jnp.float32, jnp.bfloat16
    span, width = pos.shape
    length = lengths[0, pl.program_id(0)]

    def pick(index, count):
        wide = lax.broadcasted_iota(jnp.int32, (index.shape[0], count), 1)
        return jnp.where(wide == index, 1.0, 0.0).astype(bf16)

    lines = norms[...].astype(f32)

    def scale(k):
        return lines[2 * k : 2 * k + 1], lines[2 * k + 1 : 2 * k + 2]

    emb = product(pick(slot[0], got.shape[0]), got[...])
    emb = emb + extra[0].astype(f32) + pos[...].astype(f32)
    first = normed(emb, *scale(0))
    qkv[...] = product(first.astype(bf16), w_qkv[...]).astype(bf16)
    lane = lax.broadcasted_iota(jnp.int32, (span, 2 * HD), 1)
    halves = [jnp.where(lane < HD, 1.0, 0.0), jnp.where(lane < HD, 0.0, 1.0)]
    valid = lax.broadcasted_iota(jnp.int32, (span, span), 1) < length

    def heads_at(at):
        query = qkv[:, pl.ds(at, 2 * HD)]
        keyed = qkv[:, pl.ds(width + at, 2 * HD)]
        valued = qkv[:, pl.ds(2 * width + at, 2 * HD)]
        total = jnp.zeros((span, 2 * HD), f32)
        for half in halves:
            scores = lax.dot_general(
                query * half.astype(bf16),
                keyed,
                (((1,), (1,)), ((), ())),
                preferred_element_type=f32,
            ) * HD ** (-0.5)
            scores = jnp.where(valid, scores, -1e30)
            spread = jnp.exp(scores - jnp.max(scores, -1, keepdims=True))
            probs = spread * (1.0 / jnp.sum(spread, -1, keepdims=True))
            total += half * product(probs.astype(bf16), valued)
        ctx[:, pl.ds(at, 2 * HD)] = total.astype(bf16)

    for at in range(0, width, 2 * HD):
        heads_at(at)

    second = normed(first + product(ctx[...], w_out[...]), *scale(1))
    low = second.astype(bf16)
    ffn = jnp.zeros((span, width), f32)
    for at in range(0, w_up.shape[1], width):
        pre = product(low, w_up[:, at : at + width])
        active = (0.5 * pre * (1.0 + lax.erf(pre * (0.5**0.5)))).astype(bf16)
        ffn += product(active, w_down[at : at + width, :])
    final = normed(second + ffn, *scale(2))
    out[0] = product(pick(picks[0], span), final.astype(bf16)).astype(bf16)


def teacher_rows(lengths, slot, picks, got, extra, pos, norms, w_qkv, w_out, w_up, w_down):
    count, picked = picks.shape
    span, width = pos.shape

    def whole(array, *shape):
        shape = shape or array.shape
        return pl.BlockSpec(shape, lambda i: (0,) * len(shape), pipeline_mode=pl.Buffered(1))

    def each(*shape):
        return pl.BlockSpec((1,) + shape, lambda i: (i, 0, 0))

    return pl.pallas_call(
        teacher_kernel,
        grid=(count,),
        out_shape=jax.ShapeDtypeStruct((count, picked, width), jnp.bfloat16),
        in_specs=[
            pl.BlockSpec(memory_space=pltpu.SMEM),
            each(span, 1),
            each(picked, 1),
            whole(got, got.shape[0], width),
            each(span, width),
            whole(pos),
            whole(norms),
            whole(w_qkv),
            whole(w_out),
            whole(w_up),
            whole(w_down),
        ],
        out_specs=each(picked, width),
        scratch_shapes=[
            pltpu.VMEM((span, 3 * width), jnp.bfloat16),
            pltpu.VMEM((span, width), jnp.bfloat16),
        ],
        compiler_params=pltpu.CompilerParams(vmem_limit_bytes=WIDE),
    )(
        lengths[None],
        slot.reshape(count, span, 1),
        picks[:, :, None],
        got,
        extra,
        pos,
        norms,
        w_qkv,
        w_out,
        w_up,
        w_down,
    )


DEEP = 64
WING = 256


def by_eight(value):
    return value.reshape(value.shape[0] // 8, 8, value.shape[1])


def logits_kernel(labels, rows, head, out, stats):
    f32 = jnp.float32
    taken = rows[...].reshape(-1, rows.shape[-1])
    vocab = out.shape[1]
    parts = []
    for at in range(0, taken.shape[0], WING):
        logits = lax.dot_general(
            head[0], taken[at : at + WING], (((1,), (1,)), ((), ())), preferred_element_type=f32
        )
        out[0, :, at : at + WING] = logits
        parts.append(logits)
    for k, logits in enumerate(parts):
        cols = slice(k * WING, (k + 1) * WING)
        top = jnp.max(jnp.max(by_eight(logits), 0), 0, keepdims=True)
        row = lax.broadcasted_iota(jnp.int32, (DEEP, WING), 0) - labels[:, cols]
        totals = [jnp.zeros((8, WING), f32)] * 3
        for deep in range(0, vocab, DEEP):
            part = logits[deep : deep + DEEP]
            spread = jnp.exp(part - top)
            hit = jnp.where(row == -deep, part, 0.0)
            totals = [
                total + jnp.sum(by_eight(more), 0)
                for total, more in zip(totals, (spread, spread * part, hit))
            ]
        lines = [top] + [jnp.sum(total, 0, keepdims=True) for total in totals]
        stats[0, :, cols] = jnp.concatenate(lines, axis=0)


def vocabulary_logits(labels, rows, heads):
    devices, count, picked, width = rows.shape
    vocab = heads.shape[1]
    block = 2 * WING // picked
    wide = block * picked
    return pl.pallas_call(
        logits_kernel,
        grid=(count, devices // block),
        out_shape=[
            jax.ShapeDtypeStruct((count, vocab, devices * picked), jnp.float32),
            jax.ShapeDtypeStruct((count, 4, devices * picked), jnp.float32),
        ],
        in_specs=[
            pl.BlockSpec((1, wide), lambda k, j: (0, j)),
            pl.BlockSpec((block, 1, picked, width), lambda k, j: (j, k, 0, 0)),
            pl.BlockSpec((1, vocab, width), lambda k, j: (k, 0, 0)),
        ],
        out_specs=[
            pl.BlockSpec((1, vocab, wide), lambda k, j: (k, 0, j)),
            pl.BlockSpec((1, 4, wide), lambda k, j: (k, 0, j)),
        ],
        compiler_params=pltpu.CompilerParams(vmem_limit_bytes=WIDE),
    )(labels, rows, heads)


def blend_kernel(stats, counted_ref, shift, loss, seen, sends, arrivals, local):
    f32, bf16 = jnp.float32, jnp.bfloat16
    me = here()
    greet([moved(me, *step) for step in AROUND])

    def columns(place):
        chip = place["y"] * 4 + place["x"]
        return stats.at[:, :, pl.ds(pl.multiple_of(chip * 128, 128), 128)]

    copies = []
    for k, step in enumerate(AROUND):
        place = moved(me, *step)
        copies.append(remote(columns(place), seen.at[number(me)], sends, arrivals, k, place))
    own = pltpu.make_async_copy(columns(me), seen.at[number(me)], local)
    own.start()
    own.wait()
    for copy in copies:
        copy.wait()

    def over_parts(k):
        tops = seen[:, k, 0, :]
        best = jnp.max(tops, 0, keepdims=True)
        scale = jnp.exp(tops - best)
        total = jnp.sum(seen[:, k, 1, :] * scale, 0, keepdims=True)
        return best + jnp.log(total), scale, total

    counted = counted_ref[...]
    lane = lax.broadcasted_iota(jnp.int32, (1, 128), 1)
    left = lane < 64
    totals, entropies, chances = [], [], []
    for k in range(4):
        lse, scale, total = over_parts(k)
        entropies.append(jnp.sum(seen[:, k, 2, :] * scale, 0, keepdims=True) / total - lse)
        chances.append(counted * (jnp.sum(seen[:, k, 3, :], 0, keepdims=True) - lse))
        totals.append(lse)
    student, _, _ = over_parts(4)

    def of_sequence(values):
        first = jnp.sum(jnp.where(left, values, 0.0), -1, keepdims=True)
        second = jnp.sum(jnp.where(left, 0.0, values), -1, keepdims=True)
        return jnp.where(left, first, second)

    hits = jnp.maximum(of_sequence(counted), 1.0)
    gains = [of_sequence(chance) / hits for chance in chances]
    best = functools.reduce(jnp.maximum, gains)
    powers = [jnp.exp(gain - best) for gain in gains]
    power = functools.reduce(jnp.add, powers)
    entropy = jnp.zeros((1, 128), f32)
    lines = []
    for k in range(4):
        lines.append(gains[k] - best - jnp.log(power) - totals[k])
        entropy += (powers[k] / power * entropies[k]).astype(bf16).astype(f32)
    lines += [student, counted, jnp.zeros((2, 128), f32)]
    chip = me["y"] * 4 + me["x"]
    shift[chip] = jnp.concatenate(lines, axis=0)
    ours = jnp.where(left, 0, 1) == me["c"]
    lines = [counted * (entropy + student), counted]
    lines = [jnp.where(ours, line, 0.0) for line in lines] + [jnp.zeros((6, 128), f32)]
    loss[...] = jnp.concatenate(lines, axis=0)
    copies = []
    for k in range(1, 16):
        place = moved(me, (7 * k) % 16 // 4, (7 * k) % 4, 0)
        copies.append(remote(shift.at[chip], shift.at[chip], sends, arrivals, 30 + k, place))
    for copy in copies:
        copy.wait()


def blend(stats, counted, collective):
    return pl.pallas_call(
        blend_kernel,
        out_shape=[
            jax.ShapeDtypeStruct((16, 8, 128), jnp.float32),
            jax.ShapeDtypeStruct((8, 128), jnp.float32),
        ],
        in_specs=[VMEM, VMEM],
        out_specs=[VMEM, VMEM],
        scratch_shapes=[
            pltpu.VMEM((32, 5, 4, 128), jnp.float32),
            pltpu.SemaphoreType.DMA((46,)),
            pltpu.SemaphoreType.DMA((46,)),
            pltpu.SemaphoreType.DMA,
        ],
        compiler_params=pltpu.CompilerParams(collective_id=collective, has_side_effects=True),
    )(stats, counted)


def head_grads_kernel(
    logits, z, shift, h, table, head_grad, head_low, grad_rows, crossed, low
):
    f32, bf16 = jnp.float32, jnp.bfloat16
    grad = jnp.zeros(head_grad.shape, f32)
    cross = jnp.zeros((1, WING), f32)
    for at in range(0, z.shape[2], WING):
        cols = slice(at, at + WING)
        lines = jnp.concatenate([shift[at // 128], shift[at // 128 + 1]], axis=1)
        lse, counted = lines[4:5], lines[5:6]
        total = jnp.zeros((8, WING), f32)
        for deep in range(0, z.shape[1], DEEP):
            rows = slice(deep, deep + DEEP)
            target = jnp.zeros((DEEP, WING), f32)
            for t in range(4):
                share = jnp.exp(logits[t, rows, cols] + lines[t : t + 1])
                target += share.astype(bf16).astype(f32)
            student = z[0, rows, cols]
            low[rows, cols] = (counted * (jnp.exp(student - lse) - target)).astype(bf16)
            total += jnp.sum(by_eight(target * student), 0)
        cross += counted * jnp.sum(total, 0, keepdims=True)
        grad_rows[cols] = lax.dot_general(
            low[:, cols], table[...], (((0,), (0,)), ((), ())), preferred_element_type=f32
        ).astype(bf16)
        grad += product(low[:, cols], h[cols])

    @pl.when(pl.program_id(0) == 0)
    def _():
        head_grad[...] = grad
        crossed[...] = cross

    @pl.when(pl.program_id(0) > 0)
    def _():
        head_grad[...] += grad
        crossed[...] += cross

    @pl.when(pl.program_id(0) == pl.num_programs(0) - 1)
    def _():
        head_low[...] = head_grad[...].astype(bf16)


def head_grads(logits, z, shift, h, table):
    teachers, vocab, rows = logits.shape
    width = table.shape[1]
    wide = 2 * WING
    return pl.pallas_call(
        head_grads_kernel,
        grid=(rows // wide,),
        out_shape=[
            jax.ShapeDtypeStruct((vocab, width), jnp.float32),
            jax.ShapeDtypeStruct((vocab, width), jnp.bfloat16),
            jax.ShapeDtypeStruct((rows, width), jnp.bfloat16),
            jax.ShapeDtypeStruct((1, WING), jnp.float32),
        ],
        in_specs=[
            pl.BlockSpec((teachers, vocab, wide), lambda j: (0, 0, j)),
            pl.BlockSpec((1, vocab, wide), lambda j: (0, 0, j)),
            pl.BlockSpec((wide // 128, 8, 128), lambda j: (j, 0, 0)),
            pl.BlockSpec((wide, width), lambda j: (j, 0)),
            pl.BlockSpec((vocab, width), lambda j: (0, 0)),
        ],
        out_specs=[
            pl.BlockSpec((vocab, width), lambda j: (0, 0)),
            pl.BlockSpec((vocab, width), lambda j: (0, 0)),
            pl.BlockSpec((wide, width), lambda j: (j, 0)),
            pl.BlockSpec((1, WING), lambda j: (0, 0)),
        ],
        scratch_shapes=[pltpu.VMEM((vocab, wide), jnp.bfloat16)],
        compiler_params=pltpu.CompilerParams(vmem_limit_bytes=40 * 2**20),
    )(logits, z, shift, h, table)


def quarter(group):
    return pl.ds(pl.multiple_of(group * 128, 128), 128)


def scatter_sum_kernel(plan, side, *refs):
    f32, bf16 = jnp.float32, jnp.bfloat16
    parts, refs = refs[: len(plan)], refs[len(plan) :]
    if side == "head":
        exact, sided, out, side_out, mine_exact, side_in, *refs = refs
    else:
        sided, out, side_out, side_in, *refs = refs
    own, other, both, in_a, in_b, mid_a, mid_b, end_a, end_b, sends, arrivals, local = refs
    me = here()
    group = lax.axis_index("grp")
    groups = [{"grp": lax.rem(group + d, 4)} for d in (1, 2, 3)]
    steps_x = [moved(me, 0, d, 0) for d in (1, 2, 3)]
    steps_y = [moved(me, d, 0, 0) for d in (1, 2, 3)]
    sibling = moved(me, 0, 0, 1)
    plane = [moved(me, *step) for step in AROUND]
    greet(groups + (plane if side == "rows" else [sibling] + steps_x + steps_y))
    copies, at, k = [], 0, 16
    width = own.shape[-1]
    for part, (rows, columns) in zip(parts, plan):
        for column in range(0, columns, width):
            span = (slice(None), pl.ds(at, rows))
            cols = pl.ds(column, width)
            copies.append(
                remote(
                    part.at[:, sibling["c"], :, cols],
                    other.at[span],
                    sends,
                    arrivals,
                    k,
                    sibling,
                )
            )
            mine = pltpu.make_async_copy(
                part.at[:, me["c"], :, cols], own.at[span], local.at[k - 15]
            )
            mine.start()
            copies.append(mine)
            at += rows
            k += 1
    over = [
        remote(
            sided.at[:, quarter(place["grp"])],
            side_in.at[group] if side == "rows" else side_in.at[d],
            sends,
            arrivals,
            13 + d,
            place,
        )
        for d, place in enumerate(groups)
    ]
    kept = pltpu.make_async_copy(
        (sided if side == "rows" else exact).at[:, quarter(group)],
        side_in.at[group] if side == "rows" else mine_exact,
        local.at[0],
    )
    kept.start()
    over.append(kept)
    for copy in copies:
        copy.wait()

    @pl.loop(0, 16)
    def _(k):
        both[k // 4, lax.rem(k, 4)] = (own[k].astype(f32) + other[k].astype(f32)).astype(bf16)

    cut = in_a.shape[-1]
    left, right = pl.ds(0, cut), pl.ds(cut, width - cut)
    copies = []
    for d in range(3):
        to_x, to_y = steps_x[d], steps_y[d]
        copies.append(
            remote(both.at[:, to_x["x"], :, left], in_a.at[d], sends, arrivals, 1 + d, to_x)
        )
        copies.append(
            remote(both.at[to_y["y"], :, :, right], in_b.at[d], sends, arrivals, 4 + d, to_y)
        )
    last = []
    if side == "rows":
        for copy in over:
            copy.wait()
        room = side_in.shape[1] // 32

        def of(place):
            return side_in.at[:, pl.ds(pl.multiple_of(number(place) * room, room), room)]

        for j, place in enumerate(plane):
            last.append(remote(of(place), side_out.at[number(me)], sends, arrivals, k + j, place))
        kept = pltpu.make_async_copy(of(me), side_out.at[number(me)], local.at[0])
        kept.start()
        last.append(kept)
    for copy in copies:
        copy.wait()

    @pl.loop(0, 4)
    def _(k):
        total_a = both[k, me["x"], :, left].astype(f32)
        total_b = both[me["y"], k, :, right].astype(f32)
        for d in range(3):
            total_a += in_a[d, k].astype(f32)
            total_b += in_b[d, k].astype(f32)
        mid_a[k] = total_a.astype(bf16)
        mid_b[k] = total_b.astype(bf16)

    copies = []
    for d in range(3):
        to_x, to_y = steps_x[d], steps_y[d]
        copies.append(remote(mid_a.at[to_y["y"]], end_a.at[d], sends, arrivals, 7 + d, to_y))
        copies.append(remote(mid_b.at[to_x["x"]], end_b.at[d], sends, arrivals, 10 + d, to_x))
    if side == "head":
        for copy in over:
            copy.wait()
        total = mine_exact[...]
        for d in range(3):
            total += side_in[d].astype(f32)
        side_out[...] = total
    for copy in copies:
        copy.wait()
    total_a = mid_a[me["y"]].astype(f32)
    total_b = mid_b[me["x"]].astype(f32)
    for d in range(3):
        total_a += end_a[d].astype(f32)
        total_b += end_b[d].astype(f32)
    out[:, left] = total_a.astype(out.dtype)
    out[:, right] = total_b.astype(out.dtype)
    for copy in last:
        copy.wait()


def sum_and_scatter(parts, width, dtype, side, sided, collective):
    plan = [part.shape[1:] for part in parts]
    rows = sum(r * (c // width) for r, c in plan)
    pieces = sum(c // width for _, c in plan)
    cut = width // 2
    rest = width - cut
    bf16 = jnp.bfloat16
    room = (12 if side == "head" else 36) * 2**20
    tall = sided[0].shape[0]
    if side == "head":
        side_out = jax.ShapeDtypeStruct((tall, 128), jnp.float32)
        side_scratch = [pltpu.VMEM((tall, 128), jnp.float32), pltpu.VMEM((3, tall, 128), bf16)]
    else:
        side_out = jax.ShapeDtypeStruct((32, 4, tall // 32, 128), bf16)
        side_scratch = [pltpu.VMEM((4, tall, 128), bf16)]
    semaphores = 16 + pieces + (len(AROUND) if side == "rows" else 0)
    return pl.pallas_call(
        partial(scatter_sum_kernel, plan, side),
        out_shape=[jax.ShapeDtypeStruct((rows, width), dtype), side_out],
        in_specs=[VMEM if side == "rows" else ANY] * (len(parts) + len(sided)),
        out_specs=[VMEM, VMEM],
        scratch_shapes=side_scratch
        + [
            pltpu.VMEM((16, rows, width), bf16),
            pltpu.VMEM((16, rows, width), bf16),
            pltpu.VMEM((4, 4, rows, width), bf16),
            pltpu.VMEM((3, 4, rows, cut), bf16),
            pltpu.VMEM((3, 4, rows, rest), bf16),
            pltpu.VMEM((4, rows, cut), bf16),
            pltpu.VMEM((4, rows, rest), bf16),
            pltpu.VMEM((3, rows, cut), bf16),
            pltpu.VMEM((3, rows, rest), bf16),
            pltpu.SemaphoreType.DMA((semaphores,)),
            pltpu.SemaphoreType.DMA((semaphores,)),
            pltpu.SemaphoreType.DMA((1 + pieces,)),
        ],
        compiler_params=pltpu.CompilerParams(
            collective_id=collective, has_side_effects=True, vmem_limit_bytes=room
        ),
    )(*[part.reshape(16, 2, *part.shape[1:]) for part in parts], *sided)


def group_sum_kernel(
    head, wants, given, rest, facts, crossed, table_out, rest_out, seen, total, rest_in, told, sends, arrivals
):
    f32, bf16 = jnp.float32, jnp.bfloat16
    me = here()
    group = lax.axis_index("grp")
    groups = [{"grp": lax.rem(group + d, 4)} for d in (1, 2, 3)]
    plane = [moved(me, *step) for step in AROUND]
    greet(groups + plane)
    mine = quarter(group)
    early = [
        remote(rest.at[:, quarter(groups[d]["grp"])], rest_in.at[d], sends, arrivals, d, groups[d])
        for d in range(3)
    ]
    total[...] = head[...]

    @pl.loop(0, wants.shape[0])
    def _(k):
        row = lax.broadcasted_iota(jnp.int32, (head.shape[0], wants.shape[1]), 0)
        hot = jnp.where(row == wants[pl.ds(k, 1), :], 1.0, 0.0).astype(bf16)
        total[...] += product(hot, given[k])

    rounded = total[...].astype(bf16)
    table_out[:, mine] = rounded
    rounded = rounded.astype(f32)
    squares = jnp.sum(by_eight(rounded * rounded), 0)
    wide = [
        remote(table_out.at[:, mine], table_out.at[:, mine], sends, arrivals, 3 + d, groups[d])
        for d in range(3)
    ]
    for copy in early:
        copy.wait()
    summed = rest[:, mine].astype(f32)
    for d in range(3):
        summed += rest_in[d].astype(f32)
    summed = summed.astype(bf16)
    rest_out[:, mine] = summed
    summed = summed.astype(f32)
    squares += jnp.sum(by_eight(summed * summed), 0)
    told[group, 0:8] = squares
    first = lax.broadcasted_iota(jnp.int32, (8, 128), 0) == 0
    cross = crossed[:, :128] + crossed[:, 128:]
    told[group, 8:16] = facts[...] - jnp.where(first, cross, 0.0)
    copies = []
    for d in range(3):
        copies.append(remote(told.at[group], told.at[group], sends, arrivals, 6 + d, groups[d]))
        wide.append(
            remote(rest_out.at[:, mine], rest_out.at[:, mine], sends, arrivals, 9 + d, groups[d])
        )
    for copy in copies:
        copy.wait()
    seen[number(me)] = told[0] + told[1] + told[2] + told[3]
    copies = []
    for k, place in enumerate(plane):
        copies.append(
            remote(seen.at[number(me)], seen.at[number(me)], sends, arrivals, 12 + k, place)
        )
    for copy in copies + wide:
        copy.wait()


def sum_of_groups(head, wants, given, rest, facts, crossed, collective):
    count = 12 + len(AROUND)
    bf16 = jnp.bfloat16
    return pl.pallas_call(
        group_sum_kernel,
        out_shape=[
            jax.ShapeDtypeStruct((head.shape[0], 512), bf16),
            jax.ShapeDtypeStruct(rest.shape, rest.dtype),
            jax.ShapeDtypeStruct((32, 16, 128), jnp.float32),
        ],
        in_specs=[VMEM] * 6,
        out_specs=[VMEM, VMEM, VMEM],
        scratch_shapes=[
            pltpu.VMEM(head.shape, jnp.float32),
            pltpu.VMEM((3, rest.shape[0], 128), rest.dtype),
            pltpu.VMEM((4, 16, 128), jnp.float32),
            pltpu.SemaphoreType.DMA((count,)),
            pltpu.SemaphoreType.DMA((count,)),
        ],
        compiler_params=pltpu.CompilerParams(
            collective_id=collective, has_side_effects=True, vmem_limit_bytes=40 * 2**20
        ),
    )(head, wants, given, rest, facts, crossed)


def slots(tokens, own_rows):
    count = tokens.shape[0]
    row, column = tokens[:, None], tokens[None, :]
    place = jnp.arange(count)
    repeated = jnp.any((row == column) & (place[:, None] < place[None, :]), axis=0)
    owner = tokens // own_rows
    counts = ~repeated[:, None] & (row >= (owner * own_rows)[None, :]) & (row < column)
    return owner, ~repeated, jnp.sum(counts.astype(jnp.int32), axis=0)


def slot_in_round(owner, rank, room, turn, apart=None):
    at = rank - turn * room
    return jnp.where((at >= 0) & (at < room), owner * (apart or room) + at, -1)


def wanted_rows(slot, first, local, places):
    hit = (jnp.where(first, slot, -1)[:, None] == jnp.arange(places)[None, :])
    return jnp.sum(jnp.where(hit, local[:, None] + 1, 0), axis=0) - 1


def one_hot(index, count):
    return (index[:, None] == jnp.arange(count)[None, :]).astype(jnp.bfloat16)


def product(left, right):
    return jnp.dot(left, right, preferred_element_type=jnp.float32)


def folded(rows):
    return jnp.concatenate(jnp.split(rows, 2, axis=2), axis=1)


def unfolded(rows):
    return jnp.concatenate(jnp.split(rows, 2, axis=1), axis=2)


def layer_norm(value, gain, shift):
    mean = jnp.mean(value, -1, keepdims=True)
    centred = value - mean
    var = jnp.mean(centred * centred, -1, keepdims=True)
    return centred * lax.rsqrt(var + norm_eps) * gain + shift


def project(left, right):
    return jnp.einsum("blk,kn->bln", left, right, preferred_element_type=jnp.float32)


def split_heads(packed, width):
    batch, span = (packed.shape[0], packed.shape[1])
    return [
        packed[:, :, piece * width : (piece + 1) * width].reshape(batch, span, width // HD, HD)
        for piece in range(3)
    ]


def masked_scores(query, keyed, lengths):
    scores = jnp.einsum(
        "bqhd,bkhd->bhqk", query, keyed, preferred_element_type=jnp.float32
    ) * HD ** (-0.5)
    valid = jnp.arange(query.shape[1])[None, :] < lengths[:, None]
    return jnp.where(valid[:, None, None, :], scores, -1e30)


def forward(embedded, lengths, weights):
    w_qkv, w_out, w_up, w_down, norms = weights
    norms = norms.astype(jnp.float32)
    width = w_out.shape[1]
    first = layer_norm(embedded, norms[:, 0], norms[:, 1])
    first_low = first.astype(jnp.bfloat16)
    packed = project(first_low, w_qkv).astype(jnp.bfloat16)
    query, keyed, valued = split_heads(packed, width)
    scores = masked_scores(query, keyed, lengths)
    top = jnp.max(scores, -1, keepdims=True)
    total = jnp.sum(jnp.exp(scores - top), -1, keepdims=True)
    probs = (jnp.exp(scores - top) / total).astype(jnp.bfloat16)
    context = jnp.einsum("bhqk,bkhd->bqhd", probs, valued, preferred_element_type=jnp.float32)
    context = context.reshape(first.shape).astype(jnp.bfloat16)
    joined = first + project(context, w_out)
    second = layer_norm(joined, norms[:, 2], norms[:, 3])
    second_low = second.astype(jnp.bfloat16)
    hidden_pre = project(second_low, w_up)
    active = jax.nn.gelu(hidden_pre, approximate=False).astype(jnp.bfloat16)
    summed = second + project(active, w_down)
    final = layer_norm(summed, norms[:, 4], norms[:, 5])
    saved = (
        embedded,
        first_low,
        packed,
        context,
        joined,
        second_low,
        hidden_pre,
        active,
        summed,
    )
    return (final, saved)


def norm_back(value, gain, grad):
    mean = jnp.mean(value, -1, keepdims=True)
    centred = value - mean
    scale = lax.rsqrt(jnp.mean(centred * centred, -1, keepdims=True) + norm_eps)
    unit = centred * scale
    scaled = grad * gain
    back = scaled - jnp.mean(scaled, -1, keepdims=True)
    back = scale * (back - unit * jnp.mean(scaled * unit, -1, keepdims=True))
    return back, jnp.sum(grad * unit, 0, keepdims=True), jnp.sum(grad, 0, keepdims=True)


def product_of(left, right, dims):
    return lax.dot_general(left, right, (dims, ((), ())), preferred_element_type=jnp.float32)


def backward_kernel(
    lengths,
    picks,
    slot,
    grad_rows,
    embedded,
    first_low,
    packed,
    context,
    joined,
    second_low,
    hidden_pre,
    active,
    summed,
    norms,
    w_qkv,
    w_out,
    w_up,
    w_down,
    g_qkv,
    g_out,
    g_up,
    g_down,
    g_emb,
    g_norms,
    given,
    d_packed,
    d_context,
    carried,
):
    f32, bf16 = jnp.float32, jnp.bfloat16
    span, width = embedded.shape
    rows, columns, both = ((0,), (0,)), ((1,), (1,)), ((1,), (0,))
    row = lax.broadcasted_iota(jnp.int32, (span, picks.shape[1]), 0)
    hot = jnp.where(row == picks[...], 1.0, 0.0)
    d_final = jnp.dot(
        hot, grad_rows[...], preferred_element_type=f32, precision=lax.Precision.HIGHEST
    )
    d_summed, gain_c, shift_c = norm_back(summed[...], norms[4:5], d_final)
    d_ffn = d_summed.astype(bf16)
    carried[...] = d_summed

    @pl.loop(0, w_up.shape[1] // width)
    def _(k):
        cols = pl.ds(pl.multiple_of(k * width, width), width)
        g_down[cols] = product_of(active[:, cols], d_ffn, rows).astype(bf16)
        pre = hidden_pre[:, cols]
        slope = 0.5 * (1.0 + lax.erf(pre * (0.5**0.5)))
        slope += pre * (jnp.exp(-0.5 * pre * pre) * (0.5 / math.pi) ** 0.5)
        d_up = (slope * product_of(d_ffn, w_down[cols], columns)).astype(bf16)
        g_up[:, cols] = product_of(second_low[...], d_up, rows).astype(bf16)
        carried[...] += product_of(d_up, w_up[:, cols], columns)

    d_joined, gain_b, shift_b = norm_back(joined[...], norms[2:3], carried[...])
    d_attn = d_joined.astype(bf16)
    g_out[...] = product_of(context[...], d_attn, rows).astype(bf16)
    d_context[...] = product_of(d_attn, w_out[...], columns).astype(bf16)
    lane = lax.broadcasted_iota(jnp.int32, (span, 2 * HD), 1)
    halves = [jnp.where(lane < HD, 1.0, 0.0), jnp.where(lane < HD, 0.0, 1.0)]
    valid = lax.broadcasted_iota(jnp.int32, (span, span), 1) < lengths[0, 0]

    @pl.loop(0, width // (2 * HD))
    def _(k):
        at = pl.multiple_of(k * 2 * HD, 2 * HD)
        query, keyed, valued = [
            packed[:, pl.ds(piece * width + at, 2 * HD)] for piece in range(3)
        ]
        d_heads = d_context[:, pl.ds(at, 2 * HD)]
        d_query, d_keyed, d_valued = [jnp.zeros((span, 2 * HD), f32)] * 3
        for half in halves:
            low = half.astype(bf16)
            scores = product_of(query * low, keyed, columns) * HD ** (-0.5)
            scores = jnp.where(valid, scores, -1e30)
            spread = jnp.exp(scores - jnp.max(scores, -1, keepdims=True))
            probs = spread * (1.0 / jnp.sum(spread, -1, keepdims=True))
            d_valued += half * product_of(probs.astype(bf16), d_heads, rows)
            d_probs = product_of(d_heads * low, valued, columns)
            d_scores = probs * (d_probs - jnp.sum(probs * d_probs, -1, keepdims=True))
            d_scores = d_scores.astype(bf16)
            d_query += half * product_of(d_scores, keyed, both)
            d_keyed += half * product_of(d_scores, query, rows)
        for piece, value in enumerate((d_query * HD ** (-0.5), d_keyed * HD ** (-0.5), d_valued)):
            d_packed[:, pl.ds(piece * width + at, 2 * HD)] = value.astype(bf16)

    carried[...] = d_joined

    @pl.loop(0, 3)
    def _(k):
        cols = pl.ds(pl.multiple_of(k * width, width), width)
        g_qkv[:, cols] = product_of(first_low[...], d_packed[:, cols], rows).astype(bf16)
        carried[...] += product_of(d_packed[:, cols], w_qkv[:, cols], columns)

    d_emb, gain_a, shift_a = norm_back(embedded[...], norms[0:1], carried[...])
    g_emb[...] = d_emb
    lines = [gain_a, shift_a, gain_b, shift_b, gain_c, shift_c, jnp.zeros((2, width), f32)]
    g_norms[...] = jnp.concatenate(lines, axis=0)
    low = d_emb.astype(bf16)

    @pl.loop(0, given.shape[0] // span)
    def _(k):
        place = lax.broadcasted_iota(jnp.int32, (span, span), 0) + k * span
        place = jnp.where(place == slot[...], 1.0, 0.0).astype(bf16)
        given[pl.ds(pl.multiple_of(k * span, span), span)] = product(place, low).astype(bf16)


def backward(lengths, picks, slot, places, weights, saved, grad_rows):
    w_qkv, w_out, w_up, w_down, norms = weights
    span, width = saved[0].shape[1:]
    f32, bf16 = jnp.float32, jnp.bfloat16
    return pl.pallas_call(
        backward_kernel,
        out_shape=[
            jax.ShapeDtypeStruct(w_qkv.shape, bf16),
            jax.ShapeDtypeStruct(w_out.shape, bf16),
            jax.ShapeDtypeStruct(w_up.shape, bf16),
            jax.ShapeDtypeStruct(w_down.shape, bf16),
            jax.ShapeDtypeStruct((span, width), f32),
            jax.ShapeDtypeStruct((8, width), f32),
            jax.ShapeDtypeStruct((places, width), bf16),
        ],
        in_specs=[pl.BlockSpec(memory_space=pltpu.SMEM)] + [VMEM] * 17,
        out_specs=[VMEM] * 7,
        scratch_shapes=[
            pltpu.VMEM((span, 3 * width), bf16),
            pltpu.VMEM((span, width), bf16),
            pltpu.VMEM((span, width), f32),
        ],
        compiler_params=pltpu.CompilerParams(vmem_limit_bytes=32 * 2**20),
    )(
        lengths[None],
        picks,
        slot[None],
        grad_rows,
        *[value[0] for value in saved],
        norms.astype(f32).T,
        w_qkv,
        w_out,
        w_up,
        w_down,
    )


def per_device(
    ids,
    lengths,
    picks,
    labels,
    s_table,
    s_pos,
    s_qkv,
    s_out,
    s_up,
    s_down,
    s_norms,
    m_table,
    m_pos,
    m_qkv,
    m_out,
    m_up,
    m_down,
    m_norms,
    a_table,
    a_pos,
    a_qkv,
    a_out,
    a_up,
    a_down,
    a_norms,
    t_table,
    t_pos,
    t_qkv,
    t_out,
    t_up,
    t_down,
    t_norms,
):
    masters = (s_table, s_pos, s_qkv, s_out, s_up, s_down, s_norms)
    momenta = (m_table, m_pos, m_qkv, m_out, m_up, m_down, m_norms)
    averages = (a_table, a_pos, a_qkv, a_out, a_up, a_down, a_norms)
    f32, bf16 = jnp.float32, jnp.bfloat16
    fsdp = lax.axis_size(FSDP)
    width, t_width = s_table.shape[1], t_table.shape[2]
    vocab_own = s_table.shape[0]
    picked = picks.shape[1]
    span = ids.shape[1]

    facts = jnp.concatenate([ids, picks, jnp.broadcast_to(lengths[:, None], (1, 64))], axis=1)
    facts = jnp.pad(facts.reshape(3, 128), ((0, 5), (0, 0)))
    facts = exchange_groups(jnp.broadcast_to(facts, (4, 8, 128)), 9)[:, :3].reshape(4, -1)
    group_ids, group_picks = facts[:, :span], facts[:, span : span + picked]
    group_lengths = facts[:, span + picked]
    own_table = s_table.astype(bf16)
    t_owner, t_first, t_rank = slots(group_ids.reshape(-1), vocab_own)
    s_owners, s_firsts, s_ranks = jax.vmap(lambda one: slots(one, vocab_own))(group_ids)
    my_group = lax.axis_index("grp")
    s_owner, s_rank = (
        lax.dynamic_index_in_dim(v, my_group, 0, keepdims=False) for v in (s_owners, s_ranks)
    )
    most = jnp.maximum(jnp.max(t_rank) // T_ROOM, jnp.max(s_ranks) // S_ROOM) + 1
    t_local = group_ids.reshape(-1) - t_owner * vocab_own
    s_locals = group_ids - s_owners * vocab_own

    def asked(turn):
        t_slot = slot_in_round(t_owner, t_rank, T_ROOM, turn)
        s_slot = slot_in_round(s_owner, s_rank, S_ROOM, turn)
        t_ask = wanted_rows(t_slot, t_first, t_local, fsdp * T_ROOM).reshape(fsdp, T_ROOM)
        s_asks = jax.vmap(partial(wanted_rows, places=fsdp * S_APART))(
            slot_in_round(s_owners, s_ranks, S_ROOM, turn, S_APART), s_firsts, s_locals
        ).reshape(-1, fsdp, S_APART)
        s_ask = lax.dynamic_index_in_dim(s_asks, my_group, 0, keepdims=False)[:, :S_ROOM]
        s_asks = jnp.moveaxis(s_asks, 0, 1).reshape(fsdp, -1)
        return t_slot, s_slot, t_ask, s_ask, s_asks

    def answer(t_want, s_want):
        t_sent = product(one_hot(t_want.reshape(-1), vocab_own), t_table[0]).astype(bf16)
        s_sent = product(one_hot(s_want.reshape(-1), vocab_own), own_table).astype(bf16)
        return jnp.concatenate(
            [t_sent.reshape(fsdp, T_ROOM, t_width), folded(s_sent.reshape(fsdp, S_ROOM, width))],
            axis=2,
        )

    def placed(got, t_slot, s_slot):
        t_got = got[:, :, :t_width].reshape(-1, t_width)
        s_got = unfolded(got[:, :, t_width:]).reshape(-1, width)
        return (
            product(one_hot(t_slot, fsdp * T_ROOM), t_got),
            product(one_hot(s_slot, fsdp * S_ROOM), s_got),
        )

    def swap(value):
        return lax.all_to_all(value, FSDP, split_axis=0, concat_axis=0, tiled=True)

    def ask_again(turn):
        t_slot, s_slot, t_ask, s_ask, s_asks = asked(turn)
        wants = swap(jnp.concatenate([t_ask, s_ask, s_asks], axis=1))
        both = T_ROOM + S_ROOM
        return t_slot, s_slot, wants[:, :T_ROOM], wants[:, T_ROOM:both], wants[:, both:]

    def more_rows(state):
        turn, t_emb, s_emb = state
        t_slot, s_slot, t_want, s_want, _ = ask_again(turn)
        t_more, s_more = placed(swap(answer(t_want, s_want)), t_slot, s_slot)
        return turn + 1, t_emb + t_more.astype(bf16), s_emb + s_more.astype(bf16)

    t_slot, s_slot, t_ask, s_ask, s_asks = asked(0)
    line = jnp.concatenate(
        [t_ask, s_ask, jnp.broadcast_to(most, (fsdp, 128 - T_ROOM - S_ROOM))], axis=1
    )
    lines = [
        line,
        jnp.broadcast_to(jnp.concatenate([picks, labels], axis=1), (fsdp, 2 * picked)),
        jnp.broadcast_to(lengths[:, None], (fsdp, 128)),
        s_asks,
    ]
    notes = jnp.stack(lines + [jnp.zeros((fsdp, 128), jnp.int32)] * 4, axis=1)
    notes, got = route(notes, t_table[0], own_table, 1)
    wants = notes[:, 3]
    rounds = jnp.max(notes[:, 0, T_ROOM + S_ROOM])
    plane_picks, plane_labels = notes[:, 1, :picked], notes[:, 1, picked : 2 * picked]
    plane_lengths = notes[:, 2, 0]
    nothing = (jnp.zeros((t_slot.shape[0], t_width), bf16), jnp.zeros((span, width), bf16))
    _, t_extra, s_extra = lax.while_loop(
        lambda state: state[0] < rounds, more_rows, (jnp.int32(1), *nothing)
    )

    def pieces(blocks, qkv, out, up, down, pos, norms):
        lines = norms.shape[0]
        tail = jnp.moveaxis(norms.astype(f32).reshape(lines, blocks, -1), 1, 0)
        tail = jnp.pad(tail, ((0, 0), (0, 8 - lines), (0, width - tail.shape[2])))
        small = jnp.concatenate([pos.reshape(blocks, -1, width).astype(f32), tail], axis=1)
        big = [part.astype(bf16).reshape(blocks, -1, part.shape[1]) for part in (qkv, out, up, down)]
        return big + [lax.optimization_barrier(small.astype(bf16))]

    def pack(parts):
        columns = [
            part[:, :, at : at + width] for part in parts for at in range(0, part.shape[2], width)
        ]
        return jnp.concatenate(columns, axis=1)

    def unpack(packed):
        blocks, lead = packed.shape[0], s_qkv.shape[0]

        def across(at, count):
            return jnp.concatenate(
                [
                    packed[:, at + k * lead : at + (k + 1) * lead].reshape(-1, width)
                    for k in range(count)
                ],
                axis=1,
            )

        at_out = s_qkv.shape[1] // width * lead
        at_up = at_out + lead
        at_down = at_up + s_up.shape[1] // width * lead
        at_pos = at_down + s_down.shape[0]
        at_norms = at_pos + s_pos.shape[0]
        return (
            across(0, s_qkv.shape[1] // width),
            across(at_out, 1),
            across(at_up, s_up.shape[1] // width),
            packed[:, at_down:at_pos].reshape(-1, width),
            packed[:, at_pos:at_norms].reshape(-1, width),
            jnp.moveaxis(
                packed[:, at_norms : at_norms + s_norms.shape[1], :lead], 1, 0
            ).reshape(s_norms.shape[1], -1),
        )

    own_packed = pack(pieces(1, s_qkv, s_out, s_up, s_down, s_pos, s_norms.T))
    w_qkv, w_out, w_up, w_down, positions, norms = unpack(
        lax.all_gather(own_packed, FSDP, axis=0, tiled=True)
    )
    student = (w_qkv, w_out, w_up, w_down, norms.T)
    heads = lax.all_gather(t_table[0], "grp", axis=0, tiled=False)

    taken = teacher_rows(
        group_lengths,
        t_slot,
        group_picks,
        got.reshape(-1, got.shape[2]),
        t_extra.reshape(-1, span, t_width),
        t_pos[0],
        t_norms[0].T,
        t_qkv[0],
        t_out[0],
        t_up[0],
        t_down[0],
    )
    taken, heads = lax.optimization_barrier((taken, heads))
    rows = exchange_groups(taken, 10)
    s_extra, got, rows = lax.optimization_barrier((s_extra, got, rows))
    rows = lax.all_gather(rows, FSDP, axis=0, tiled=False)

    s_got = unfolded(got[:, :, t_width:]).reshape(-1, width)
    s_emb = product(one_hot(s_slot, fsdp * S_ROOM), s_got) + s_extra.astype(f32)
    embedded = s_emb[None] + positions.astype(f32)[None]
    final, saved = forward(embedded, lengths, student)
    own_rows = jnp.take_along_axis(final, picks[:, :, None], axis=1).astype(bf16)[0]
    h = gather_plane(own_rows, 11)
    base = lax.axis_index(FSDP) * vocab_own
    labels_here = plane_labels.reshape(1, -1) - base
    z, z_stats = vocabulary_logits(labels_here, h.reshape(fsdp, 1, picked, width), own_table[None])
    logits, stats = vocabulary_logits(labels_here, rows, heads)
    stats = jnp.concatenate([stats, z_stats], axis=0)
    plane_counted = (plane_picks < plane_lengths[:, None]).astype(f32).reshape(-1, 1, 2 * picked)
    chip = lax.axis_index(("y", "x"))
    chip_counted = lax.dynamic_index_in_dim(plane_counted, chip, 0, keepdims=False)
    shift, own_loss = blend(stats, chip_counted, 3)
    head_grad, head_low, grad_rows, crossed = head_grads(logits, z, shift, h, own_table)
    grad_rows, head_grad = sum_and_scatter(
        [grad_rows.reshape(fsdp, picked, width)], width, f32, "head", [head_grad, head_low], 5
    )

    g_slot = slot_in_round(s_owner, s_rank, S_ROOM, 0, S_APART)
    g_qkv, g_out, g_up, g_down, g_pos, g_norms, given_rows = backward(
        lengths, picks, g_slot, fsdp * S_APART, student, saved, grad_rows
    )
    low_embedded = g_pos.astype(bf16)

    def given(turn):
        slot = slot_in_round(s_owner, s_rank, S_ROOM, turn, S_APART)
        hot = (jnp.arange(fsdp * S_APART)[:, None] == slot[None, :]).astype(bf16)
        return product(hot, low_embedded).astype(bf16)

    def more_grads(state):
        turn, total = state
        wants = ask_again(turn)[4]
        rows = jnp.stack(jnp.split(given(turn), 4, axis=1))
        rows = lax.all_to_all(rows, "grp", split_axis=0, concat_axis=0, tiled=True)
        rows = swap(jnp.moveaxis(rows.reshape(4, fsdp, S_APART, -1), 0, 1))
        hot = one_hot(wants.reshape(-1), vocab_own).T
        return turn + 1, total + product(hot, rows.reshape(-1, rows.shape[3]))

    _, head_grad = lax.while_loop(
        lambda state: state[0] < rounds, more_grads, (jnp.int32(1), head_grad)
    )
    parts = pieces(fsdp, g_qkv, g_out, g_up, g_down, g_pos, g_norms)
    rest, got = sum_and_scatter(parts, width, bf16, "rows", [given_rows], 7)
    table_sum, rest_sum, seen = sum_of_groups(
        head_grad, wants.reshape(4, -1), got.reshape(4, -1, got.shape[3]), rest, own_loss, crossed, 8
    )
    turned = [group[:6] + (group[6].T,) for group in (masters, momenta, averages)]
    loss_sum, count, clip_norm, *outs = update(seen, table_sum, rest_sum, *turned)
    outs = tuple(out.T if k % 7 == 6 else out for k, out in enumerate(outs))
    return (loss_sum.reshape(()), count.reshape(()), clip_norm[0, 0]) + outs


def solution(mesh):
    finer = Mesh(
        mesh.devices.reshape(mesh.shape["grp"], 4, 4, 2), ("grp", "y", "x", "c")
    )
    return jax.shard_map(
        per_device,
        mesh=finer,
        in_specs=(
            P(GRP_FSDP, None),
            P(GRP_FSDP),
            P(GRP_FSDP, None),
            P(GRP_FSDP, None),
            P(FSDP, None),
            P(FSDP, None),
            P(FSDP, None),
            P(FSDP, None),
            P(FSDP, None),
            P(FSDP, None),
            P(FSDP, None),
            P(FSDP, None),
            P(FSDP, None),
            P(FSDP, None),
            P(FSDP, None),
            P(FSDP, None),
            P(FSDP, None),
            P(FSDP, None),
            P(FSDP, None),
            P(FSDP, None),
            P(FSDP, None),
            P(FSDP, None),
            P(FSDP, None),
            P(FSDP, None),
            P(FSDP, None),
            P("grp", FSDP, None),
            P("grp", None, None),
            P("grp", None, None),
            P("grp", None, None),
            P("grp", None, None),
            P("grp", None, None),
            P("grp", None, None),
        ),
        out_specs=(
            P(),
            P(),
            P(),
            P(FSDP, None),
            P(FSDP, None),
            P(FSDP, None),
            P(FSDP, None),
            P(FSDP, None),
            P(FSDP, None),
            P(FSDP, None),
            P(FSDP, None),
            P(FSDP, None),
            P(FSDP, None),
            P(FSDP, None),
            P(FSDP, None),
            P(FSDP, None),
            P(FSDP, None),
            P(FSDP, None),
            P(FSDP, None),
            P(FSDP, None),
            P(FSDP, None),
            P(FSDP, None),
            P(FSDP, None),
            P(FSDP, None),
        ),
        check_vma=False,
    )
```

```python
import functools
import math
from functools import partial

import jax
import jax.numpy as jnp
from jax import lax
from jax.experimental import pallas as pl
from jax.experimental.pallas import tpu as pltpu
from jax.sharding import Mesh
from jax.sharding import PartitionSpec as P

HD = 64
FSDP = ("y", "x", "c")
GRP_FSDP = ("grp", "y", "x", "c")
T_ROOM = 48
S_ROOM = 24
S_APART = 32
WIDE = 56 * 2**20

norm_eps = 1e-12
clip_limit = 0.001
learn_rate = 100000.0
momentum_decay = 0.9
average_decay = 0.9


SIZES = {"y": 4, "x": 4, "c": 2}
MESH = pl.DeviceIdType.MESH
ANY = pl.BlockSpec(memory_space=pl.ANY)
VMEM = pl.BlockSpec(memory_space=pltpu.VMEM)
AROUND = [((11 * k) % 32 // 8, (11 * k) % 8 // 2, (11 * k) % 2) for k in range(1, 32)]


def here():
    return {axis: lax.axis_index(axis) for axis in SIZES}


def moved(me, dy, dx, dc):
    return {
        "y": lax.rem(me["y"] + dy, 4),
        "x": lax.rem(me["x"] + dx, 4),
        "c": lax.rem(me["c"] + dc, 2),
    }


def number(place):
    return (place["y"] * 4 + place["x"]) * 2 + place["c"]


def greet(places, work=None):
    barrier = pltpu.get_barrier_semaphore()
    for place in places:
        pl.semaphore_signal(barrier, inc=1, device_id=place, device_id_type=MESH)
    if work:
        work()
    pl.semaphore_wait(barrier, len(places))


def remote(source, target, sends, arrivals, at, place):
    copy = pltpu.make_async_remote_copy(
        src_ref=source,
        dst_ref=target,
        send_sem=sends.at[at],
        recv_sem=arrivals.at[at],
        device_id=place,
        device_id_type=MESH,
    )
    copy.start()
    return copy


def route_kernel(notes, t_table, s_table, heard, got, sent, wants, sends, arrivals, local):
    f32, bf16 = jnp.float32, jnp.bfloat16
    me = here()
    greet([moved(me, *step) for step in AROUND])
    copies = []
    for k, step in enumerate(AROUND):
        place = moved(me, *step)
        copies.append(
            remote(notes.at[number(place)], heard.at[number(me)], sends, arrivals, k, place)
        )
    heard[number(me)] = notes[number(me)]
    for copy in copies:
        copy.wait()
    all_wants = heard[:, 0, :].astype(f32).T
    vocab, t_width = t_table.shape
    half = s_table.shape[1] // 2
    batch = wants.shape[2]
    for k in range(wants.shape[0]):
        wants[k] = all_wants[:, k * batch : (k + 1) * batch]

    def rows_of(k, at, room, table):
        index = jnp.concatenate(
            [wants[k, at : at + room, p : p + 1] for p in range(batch)], axis=0
        )
        entry = lax.broadcasted_iota(jnp.int32, (index.shape[0], vocab), 1).astype(f32)
        hot = jnp.where(entry == index, 1.0, 0.0).astype(bf16)
        return product(hot, table[...])

    @pl.loop(0, wants.shape[0])
    def _(k):
        t_rows = rows_of(k, 0, T_ROOM, t_table)
        s_rows = rows_of(k, T_ROOM, S_ROOM, s_table)
        for j in range(batch):
            p = k * batch + j
            sent[p, :, :t_width] = t_rows[j * T_ROOM : (j + 1) * T_ROOM].astype(bf16)
            own = s_rows[j * S_ROOM : (j + 1) * S_ROOM]
            own = jnp.concatenate([own[:, :half], own[:, half:]], axis=0)
            sent[p, :, t_width:] = own.astype(bf16)

    copies = []
    for k, step in enumerate(AROUND):
        place = moved(me, *step)
        copies.append(
            remote(
                sent.at[number(place)], got.at[number(me)], sends, arrivals, len(AROUND) + k, place
            )
        )
    mine = pltpu.make_async_copy(sent.at[number(me)], got.at[number(me)], local)
    mine.start()
    mine.wait()
    for copy in copies:
        copy.wait()


def route(notes, t_table, s_table, collective):
    width = t_table.shape[1] + s_table.shape[1] // 2
    return pl.pallas_call(
        route_kernel,
        out_shape=[
            jax.ShapeDtypeStruct(notes.shape, notes.dtype),
            jax.ShapeDtypeStruct((32, T_ROOM, width), jnp.bfloat16),
        ],
        in_specs=[VMEM, VMEM, VMEM],
        out_specs=[VMEM, ANY],
        scratch_shapes=[
            pltpu.VMEM((32, T_ROOM, width), jnp.bfloat16),
            pltpu.VMEM((4, 128, 8), jnp.float32),
            pltpu.SemaphoreType.DMA((2 * len(AROUND),)),
            pltpu.SemaphoreType.DMA((2 * len(AROUND),)),
            pltpu.SemaphoreType.DMA,
        ],
        compiler_params=pltpu.CompilerParams(
            collective_id=collective, has_side_effects=True, vmem_limit_bytes=40 * 2**20
        ),
    )(notes, t_table, s_table)


def group_exchange_kernel(source, target, sends, arrivals, local):
    group = lax.axis_index("grp")
    groups = [lax.rem(group + d, 4) for d in (1, 2, 3)]
    greet([{"grp": g} for g in groups])
    copies = [
        remote(source.at[g], target.at[group], sends, arrivals, d, {"grp": g})
        for d, g in enumerate(groups)
    ]
    own = pltpu.make_async_copy(source.at[group], target.at[group], local)
    own.start()
    own.wait()
    for copy in copies:
        copy.wait()


def exchange_groups(value, collective):
    return pl.pallas_call(
        group_exchange_kernel,
        out_shape=jax.ShapeDtypeStruct(value.shape, value.dtype),
        in_specs=[ANY],
        out_specs=ANY,
        scratch_shapes=[
            pltpu.SemaphoreType.DMA((3,)),
            pltpu.SemaphoreType.DMA((3,)),
            pltpu.SemaphoreType.DMA,
        ],
        compiler_params=pltpu.CompilerParams(collective_id=collective, has_side_effects=True),
    )(value)


def gather_kernel(source, target, sends, arrivals, local):
    me = here()
    chip, core = me["y"] * 4 + me["x"], me["c"]
    chips = [moved(me, (7 * k) % 16 // 4, (7 * k) % 4, 0) for k in range(1, 16)]
    sibling = moved(me, 0, 0, 1)
    greet(chips + [sibling])
    copies = [
        remote(source, target.at[chip, core], sends, arrivals, k, place)
        for k, place in enumerate(chips)
    ]
    own = pltpu.make_async_copy(source, target.at[chip, core], local)
    own.start()
    own.wait()
    for copy in copies:
        copy.wait()
    remote(target.at[:, core], target.at[:, core], sends, arrivals, 15, sibling).wait()


def gather_plane(value, collective):
    rows, width = value.shape
    out = pl.pallas_call(
        gather_kernel,
        out_shape=jax.ShapeDtypeStruct((16, 2, rows, width), value.dtype),
        in_specs=[ANY],
        out_specs=ANY,
        scratch_shapes=[
            pltpu.SemaphoreType.DMA((16,)),
            pltpu.SemaphoreType.DMA((16,)),
            pltpu.SemaphoreType.DMA,
        ],
        compiler_params=pltpu.CompilerParams(collective_id=collective, has_side_effects=True),
    )(value)
    return out.reshape(32 * rows, width)


def update_kernel(seen, table_grad, rest_grad, *refs):
    masters, momenta, averages = refs[:7], refs[7:14], refs[14:21]
    loss_sum, count_out, clip_out = refs[21:24]
    outs = refs[24:]
    facts = jnp.sum(seen[...], 0)
    squares, loss, count = [jnp.sum(line) for line in (facts[:8], facts[8:9], facts[9:10])]
    clip = jnp.sqrt(jnp.full((8, 128), squares)) / count
    factor = (jnp.minimum(1.0, clip_limit / clip) / count)[0:1, 0:1]

    def step(k, grad):
        clipped = grad * factor
        moment = momentum_decay * momenta[k][...] + clipped
        weight = masters[k][...] - learn_rate * (clipped + momentum_decay * moment)
        outs[k][...] = weight
        outs[7 + k][...] = moment
        outs[14 + k][...] = average_decay * averages[k][...] + (1.0 - average_decay) * weight

    step(0, table_grad[...].astype(jnp.float32))

    @pl.when(pl.program_id(0) == 0)
    def _():
        loss_sum[0, 0] = loss
        count_out[0, 0] = count
        clip_out[...] = clip
        width = rest_grad.shape[1]
        at = 0
        for k in (2, 3, 4, 5):
            rows, columns = masters[k].shape
            blocks = []
            for _ in range(columns // width):
                blocks.append(rest_grad[at : at + rows].astype(jnp.float32))
                at += rows
            step(k, blocks[0] if len(blocks) == 1 else jnp.concatenate(blocks, axis=1))
        small = rest_grad[at : at + 16].astype(jnp.float32)
        step(1, small[:8])
        lines, columns = masters[6].shape
        at = ((lax.axis_index("y") * 4 + lax.axis_index("x")) * 2 + lax.axis_index("c")) * columns
        row = lax.broadcasted_iota(jnp.int32, (width, columns), 0) - at
        own = lax.broadcasted_iota(jnp.int32, (width, columns), 1) == row
        own = jnp.where(own, 1.0, 0.0).astype(jnp.bfloat16)
        step(6, product(small.astype(jnp.bfloat16), own)[8 : 8 + lines])


def update(seen, table_grad, rest_grad, masters, momenta, averages):
    steps = 5
    rows, width = table_grad.shape

    def whole(shape):
        return pl.BlockSpec(shape, lambda i: (0,) * len(shape))

    tall = pl.BlockSpec((rows // steps, width), lambda i: (i, 0))
    states = [tall] + [whole(m.shape) for m in masters[1:]]
    scalar = pl.BlockSpec(memory_space=pltpu.SMEM)
    one = jax.ShapeDtypeStruct((1, 1), jnp.float32)
    tile = jax.ShapeDtypeStruct((8, 128), jnp.float32)
    return pl.pallas_call(
        update_kernel,
        grid=(steps,),
        out_shape=[one, one, tile]
        + [jax.ShapeDtypeStruct(m.shape, m.dtype) for m in masters] * 3,
        in_specs=[whole(seen.shape), tall, whole(rest_grad.shape)] + states * 3,
        out_specs=[scalar, scalar, whole(tile.shape)] + states * 3,
        compiler_params=pltpu.CompilerParams(vmem_limit_bytes=WIDE),
    )(seen, table_grad, rest_grad, *masters, *momenta, *averages)


def normed(value, gain, shift):
    mean = jnp.mean(value, -1, keepdims=True)
    centred = value - mean
    var = jnp.mean(centred * centred, -1, keepdims=True)
    return centred * lax.rsqrt(var + norm_eps) * gain + shift


def teacher_kernel(
    lengths, slot, picks, got, extra, pos, norms, w_qkv, w_out, w_up, w_down, out, qkv, ctx
):
    f32, bf16 = jnp.float32, jnp.bfloat16
    span, width = pos.shape
    length = lengths[0, pl.program_id(0)]

    def pick(index, count):
        wide = lax.broadcasted_iota(jnp.int32, (index.shape[0], count), 1)
        return jnp.where(wide == index, 1.0, 0.0).astype(bf16)

    lines = norms[...].astype(f32)

    def scale(k):
        return lines[2 * k : 2 * k + 1], lines[2 * k + 1 : 2 * k + 2]

    emb = product(pick(slot[0], got.shape[0]), got[...])
    emb = emb + extra[0].astype(f32) + pos[...].astype(f32)
    first = normed(emb, *scale(0))
    qkv[...] = product(first.astype(bf16), w_qkv[...]).astype(bf16)
    lane = lax.broadcasted_iota(jnp.int32, (span, 2 * HD), 1)
    halves = [jnp.where(lane < HD, 1.0, 0.0), jnp.where(lane < HD, 0.0, 1.0)]
    valid = lax.broadcasted_iota(jnp.int32, (span, span), 1) < length

    def heads_at(at):
        query = qkv[:, pl.ds(at, 2 * HD)]
        keyed = qkv[:, pl.ds(width + at, 2 * HD)]
        valued = qkv[:, pl.ds(2 * width + at, 2 * HD)]
        total = jnp.zeros((span, 2 * HD), f32)
        for half in halves:
            scores = lax.dot_general(
                query * half.astype(bf16),
                keyed,
                (((1,), (1,)), ((), ())),
                preferred_element_type=f32,
            ) * HD ** (-0.5)
            scores = jnp.where(valid, scores, -1e30)
            spread = jnp.exp(scores - jnp.max(scores, -1, keepdims=True))
            probs = spread * (1.0 / jnp.sum(spread, -1, keepdims=True))
            total += half * product(probs.astype(bf16), valued)
        ctx[:, pl.ds(at, 2 * HD)] = total.astype(bf16)

    for at in range(0, width, 2 * HD):
        heads_at(at)

    second = normed(first + product(ctx[...], w_out[...]), *scale(1))
    low = second.astype(bf16)
    ffn = jnp.zeros((span, width), f32)
    for at in range(0, w_up.shape[1], width):
        pre = product(low, w_up[:, at : at + width])
        active = (0.5 * pre * (1.0 + lax.erf(pre * (0.5**0.5)))).astype(bf16)
        ffn += product(active, w_down[at : at + width, :])
    final = normed(second + ffn, *scale(2))
    out[0] = product(pick(picks[0], span), final.astype(bf16)).astype(bf16)


def teacher_rows(lengths, slot, picks, got, extra, pos, norms, w_qkv, w_out, w_up, w_down):
    count, picked = picks.shape
    span, width = pos.shape

    def whole(array, *shape):
        shape = shape or array.shape
        return pl.BlockSpec(shape, lambda i: (0,) * len(shape), pipeline_mode=pl.Buffered(1))

    def each(*shape):
        return pl.BlockSpec((1,) + shape, lambda i: (i, 0, 0))

    return pl.pallas_call(
        teacher_kernel,
        grid=(count,),
        out_shape=jax.ShapeDtypeStruct((count, picked, width), jnp.bfloat16),
        in_specs=[
            pl.BlockSpec(memory_space=pltpu.SMEM),
            each(span, 1),
            each(picked, 1),
            whole(got, got.shape[0], width),
            each(span, width),
            whole(pos),
            whole(norms),
            whole(w_qkv),
            whole(w_out),
            whole(w_up),
            whole(w_down),
        ],
        out_specs=each(picked, width),
        scratch_shapes=[
            pltpu.VMEM((span, 3 * width), jnp.bfloat16),
            pltpu.VMEM((span, width), jnp.bfloat16),
        ],
        compiler_params=pltpu.CompilerParams(vmem_limit_bytes=WIDE),
    )(
        lengths[None],
        slot.reshape(count, span, 1),
        picks[:, :, None],
        got,
        extra,
        pos,
        norms,
        w_qkv,
        w_out,
        w_up,
        w_down,
    )


DEEP = 64
WING = 256


def by_eight(value):
    return value.reshape(value.shape[0] // 8, 8, value.shape[1])


def logits_kernel(labels, rows, head, out, stats):
    f32 = jnp.float32
    taken = rows[...].reshape(-1, rows.shape[-1])
    vocab = out.shape[1]
    parts = []
    for at in range(0, taken.shape[0], WING):
        logits = lax.dot_general(
            head[0], taken[at : at + WING], (((1,), (1,)), ((), ())), preferred_element_type=f32
        )
        out[0, :, at : at + WING] = logits
        parts.append(logits)
    for k, logits in enumerate(parts):
        cols = slice(k * WING, (k + 1) * WING)
        top = jnp.max(jnp.max(by_eight(logits), 0), 0, keepdims=True)
        row = lax.broadcasted_iota(jnp.int32, (DEEP, WING), 0) - labels[:, cols]
        totals = [jnp.zeros((8, WING), f32)] * 3
        for deep in range(0, vocab, DEEP):
            part = logits[deep : deep + DEEP]
            spread = jnp.exp(part - top)
            hit = jnp.where(row == -deep, part, 0.0)
            totals = [
                total + jnp.sum(by_eight(more), 0)
                for total, more in zip(totals, (spread, spread * part, hit))
            ]
        lines = [top] + [jnp.sum(total, 0, keepdims=True) for total in totals]
        stats[0, :, cols] = jnp.concatenate(lines, axis=0)


def vocabulary_logits(labels, rows, heads):
    devices, count, picked, width = rows.shape
    vocab = heads.shape[1]
    block = 2 * WING // picked
    wide = block * picked
    return pl.pallas_call(
        logits_kernel,
        grid=(count, devices // block),
        out_shape=[
            jax.ShapeDtypeStruct((count, vocab, devices * picked), jnp.float32),
            jax.ShapeDtypeStruct((count, 4, devices * picked), jnp.float32),
        ],
        in_specs=[
            pl.BlockSpec((1, wide), lambda k, j: (0, j)),
            pl.BlockSpec((block, 1, picked, width), lambda k, j: (j, k, 0, 0)),
            pl.BlockSpec((1, vocab, width), lambda k, j: (k, 0, 0)),
        ],
        out_specs=[
            pl.BlockSpec((1, vocab, wide), lambda k, j: (k, 0, j)),
            pl.BlockSpec((1, 4, wide), lambda k, j: (k, 0, j)),
        ],
        compiler_params=pltpu.CompilerParams(vmem_limit_bytes=WIDE),
    )(labels, rows, heads)


def blend_kernel(stats, counted_ref, shift, loss, seen, sends, arrivals, local):
    f32, bf16 = jnp.float32, jnp.bfloat16
    me = here()
    greet([moved(me, *step) for step in AROUND])

    def columns(place):
        chip = place["y"] * 4 + place["x"]
        return stats.at[:, :, pl.ds(pl.multiple_of(chip * 128, 128), 128)]

    copies = []
    for k, step in enumerate(AROUND):
        place = moved(me, *step)
        copies.append(remote(columns(place), seen.at[number(me)], sends, arrivals, k, place))
    own = pltpu.make_async_copy(columns(me), seen.at[number(me)], local)
    own.start()
    own.wait()
    for copy in copies:
        copy.wait()

    def over_parts(k):
        tops = seen[:, k, 0, :]
        best = jnp.max(tops, 0, keepdims=True)
        scale = jnp.exp(tops - best)
        total = jnp.sum(seen[:, k, 1, :] * scale, 0, keepdims=True)
        return best + jnp.log(total), scale, total

    counted = counted_ref[...]
    lane = lax.broadcasted_iota(jnp.int32, (1, 128), 1)
    left = lane < 64
    totals, entropies, chances = [], [], []
    for k in range(4):
        lse, scale, total = over_parts(k)
        entropies.append(jnp.sum(seen[:, k, 2, :] * scale, 0, keepdims=True) / total - lse)
        chances.append(counted * (jnp.sum(seen[:, k, 3, :], 0, keepdims=True) - lse))
        totals.append(lse)
    student, _, _ = over_parts(4)

    def of_sequence(values):
        first = jnp.sum(jnp.where(left, values, 0.0), -1, keepdims=True)
        second = jnp.sum(jnp.where(left, 0.0, values), -1, keepdims=True)
        return jnp.where(left, first, second)

    hits = jnp.maximum(of_sequence(counted), 1.0)
    gains = [of_sequence(chance) / hits for chance in chances]
    best = functools.reduce(jnp.maximum, gains)
    powers = [jnp.exp(gain - best) for gain in gains]
    power = functools.reduce(jnp.add, powers)
    entropy = jnp.zeros((1, 128), f32)
    lines = []
    for k in range(4):
        lines.append(gains[k] - best - jnp.log(power) - totals[k])
        entropy += (powers[k] / power * entropies[k]).astype(bf16).astype(f32)
    lines += [student, counted, jnp.zeros((2, 128), f32)]
    chip = me["y"] * 4 + me["x"]
    shift[chip] = jnp.concatenate(lines, axis=0)
    ours = jnp.where(left, 0, 1) == me["c"]
    lines = [counted * (entropy + student), counted]
    lines = [jnp.where(ours, line, 0.0) for line in lines] + [jnp.zeros((6, 128), f32)]
    loss[...] = jnp.concatenate(lines, axis=0)
    copies = []
    for k in range(1, 16):
        place = moved(me, (7 * k) % 16 // 4, (7 * k) % 4, 0)
        copies.append(remote(shift.at[chip], shift.at[chip], sends, arrivals, 30 + k, place))
    for copy in copies:
        copy.wait()


def blend(stats, counted, collective):
    return pl.pallas_call(
        blend_kernel,
        out_shape=[
            jax.ShapeDtypeStruct((16, 8, 128), jnp.float32),
            jax.ShapeDtypeStruct((8, 128), jnp.float32),
        ],
        in_specs=[VMEM, VMEM],
        out_specs=[VMEM, VMEM],
        scratch_shapes=[
            pltpu.VMEM((32, 5, 4, 128), jnp.float32),
            pltpu.SemaphoreType.DMA((46,)),
            pltpu.SemaphoreType.DMA((46,)),
            pltpu.SemaphoreType.DMA,
        ],
        compiler_params=pltpu.CompilerParams(collective_id=collective, has_side_effects=True),
    )(stats, counted)


def head_grads_kernel(
    logits, z, shift, h, table, head_grad, head_low, grad_rows, crossed, low
):
    f32, bf16 = jnp.float32, jnp.bfloat16
    grad = jnp.zeros(head_grad.shape, f32)
    cross = jnp.zeros((1, WING), f32)
    for at in range(0, z.shape[2], WING):
        cols = slice(at, at + WING)
        lines = jnp.concatenate([shift[at // 128], shift[at // 128 + 1]], axis=1)
        lse, counted = lines[4:5], lines[5:6]
        total = jnp.zeros((8, WING), f32)
        for deep in range(0, z.shape[1], DEEP):
            rows = slice(deep, deep + DEEP)
            target = jnp.zeros((DEEP, WING), f32)
            for t in range(4):
                share = jnp.exp(logits[t, rows, cols] + lines[t : t + 1])
                target += share.astype(bf16).astype(f32)
            student = z[0, rows, cols]
            low[rows, cols] = (counted * (jnp.exp(student - lse) - target)).astype(bf16)
            total += jnp.sum(by_eight(target * student), 0)
        cross += counted * jnp.sum(total, 0, keepdims=True)
        grad_rows[cols] = lax.dot_general(
            low[:, cols], table[...], (((0,), (0,)), ((), ())), preferred_element_type=f32
        ).astype(bf16)
        grad += product(low[:, cols], h[cols])

    @pl.when(pl.program_id(0) == 0)
    def _():
        head_grad[...] = grad
        crossed[...] = cross

    @pl.when(pl.program_id(0) > 0)
    def _():
        head_grad[...] += grad
        crossed[...] += cross

    @pl.when(pl.program_id(0) == pl.num_programs(0) - 1)
    def _():
        head_low[...] = head_grad[...].astype(bf16)


def head_grads(logits, z, shift, h, table):
    teachers, vocab, rows = logits.shape
    width = table.shape[1]
    wide = 2 * WING
    return pl.pallas_call(
        head_grads_kernel,
        grid=(rows // wide,),
        out_shape=[
            jax.ShapeDtypeStruct((vocab, width), jnp.float32),
            jax.ShapeDtypeStruct((vocab, width), jnp.bfloat16),
            jax.ShapeDtypeStruct((rows, width), jnp.bfloat16),
            jax.ShapeDtypeStruct((1, WING), jnp.float32),
        ],
        in_specs=[
            pl.BlockSpec((teachers, vocab, wide), lambda j: (0, 0, j)),
            pl.BlockSpec((1, vocab, wide), lambda j: (0, 0, j)),
            pl.BlockSpec((wide // 128, 8, 128), lambda j: (j, 0, 0)),
            pl.BlockSpec((wide, width), lambda j: (j, 0)),
            pl.BlockSpec((vocab, width), lambda j: (0, 0)),
        ],
        out_specs=[
            pl.BlockSpec((vocab, width), lambda j: (0, 0)),
            pl.BlockSpec((vocab, width), lambda j: (0, 0)),
            pl.BlockSpec((wide, width), lambda j: (j, 0)),
            pl.BlockSpec((1, WING), lambda j: (0, 0)),
        ],
        scratch_shapes=[pltpu.VMEM((vocab, wide), jnp.bfloat16)],
        compiler_params=pltpu.CompilerParams(vmem_limit_bytes=40 * 2**20),
    )(logits, z, shift, h, table)


def quarter(group):
    return pl.ds(pl.multiple_of(group * 128, 128), 128)


def scatter_sum_kernel(plan, side, *refs, work=None):
    f32, bf16 = jnp.float32, jnp.bfloat16
    parts, refs = refs[: len(plan)], refs[len(plan) :]
    if side == "head":
        exact, sided, out, side_out, mine_exact, side_in, *refs = refs
    else:
        sided, out, side_out, side_in, *refs = refs
    own, other, both, in_a, in_b, mid_a, mid_b, end_a, end_b, sends, arrivals, local = refs
    me = here()
    group = lax.axis_index("grp")
    groups = [{"grp": lax.rem(group + d, 4)} for d in (1, 2, 3)]
    steps_x = [moved(me, 0, d, 0) for d in (1, 2, 3)]
    steps_y = [moved(me, d, 0, 0) for d in (1, 2, 3)]
    sibling = moved(me, 0, 0, 1)
    plane = [moved(me, *step) for step in AROUND]
    greet(groups + (plane if side == "rows" else [sibling] + steps_x + steps_y), work)
    copies, at, k = [], 0, 16
    width = own.shape[-1]
    for part, (rows, columns) in zip(parts, plan):
        for column in range(0, columns, width):
            span = (slice(None), pl.ds(at, rows))
            cols = pl.ds(column, width)
            copies.append(
                remote(
                    part.at[:, sibling["c"], :, cols],
                    other.at[span],
                    sends,
                    arrivals,
                    k,
                    sibling,
                )
            )
            mine = pltpu.make_async_copy(
                part.at[:, me["c"], :, cols], own.at[span], local.at[k - 15]
            )
            mine.start()
            copies.append(mine)
            at += rows
            k += 1
    over = [
        remote(
            sided.at[:, quarter(place["grp"])],
            side_in.at[group] if side == "rows" else side_in.at[d],
            sends,
            arrivals,
            13 + d,
            place,
        )
        for d, place in enumerate(groups)
    ]
    kept = pltpu.make_async_copy(
        (sided if side == "rows" else exact).at[:, quarter(group)],
        side_in.at[group] if side == "rows" else mine_exact,
        local.at[0],
    )
    kept.start()
    over.append(kept)
    for copy in copies:
        copy.wait()

    @pl.loop(0, 16)
    def _(k):
        both[k // 4, lax.rem(k, 4)] = (own[k].astype(f32) + other[k].astype(f32)).astype(bf16)

    cut = in_a.shape[-1]
    left, right = pl.ds(0, cut), pl.ds(cut, width - cut)
    copies = []
    for d in range(3):
        to_x, to_y = steps_x[d], steps_y[d]
        copies.append(
            remote(both.at[:, to_x["x"], :, left], in_a.at[d], sends, arrivals, 1 + d, to_x)
        )
        copies.append(
            remote(both.at[to_y["y"], :, :, right], in_b.at[d], sends, arrivals, 4 + d, to_y)
        )
    last = []
    if side == "rows":
        for copy in over:
            copy.wait()
        room = side_in.shape[1] // 32

        def of(place):
            return side_in.at[:, pl.ds(pl.multiple_of(number(place) * room, room), room)]

        for j, place in enumerate(plane):
            last.append(remote(of(place), side_out.at[number(me)], sends, arrivals, k + j, place))
        kept = pltpu.make_async_copy(of(me), side_out.at[number(me)], local.at[0])
        kept.start()
        last.append(kept)
    for copy in copies:
        copy.wait()

    @pl.loop(0, 4)
    def _(k):
        total_a = both[k, me["x"], :, left].astype(f32)
        total_b = both[me["y"], k, :, right].astype(f32)
        for d in range(3):
            total_a += in_a[d, k].astype(f32)
            total_b += in_b[d, k].astype(f32)
        mid_a[k] = total_a.astype(bf16)
        mid_b[k] = total_b.astype(bf16)

    copies = []
    for d in range(3):
        to_x, to_y = steps_x[d], steps_y[d]
        copies.append(remote(mid_a.at[to_y["y"]], end_a.at[d], sends, arrivals, 7 + d, to_y))
        copies.append(remote(mid_b.at[to_x["x"]], end_b.at[d], sends, arrivals, 10 + d, to_x))
    if side == "head":
        for copy in over:
            copy.wait()
        total = mine_exact[...]
        for d in range(3):
            total += side_in[d].astype(f32)
        side_out[...] = total
    for copy in copies:
        copy.wait()
    total_a = mid_a[me["y"]].astype(f32)
    total_b = mid_b[me["x"]].astype(f32)
    for d in range(3):
        total_a += end_a[d].astype(f32)
        total_b += end_b[d].astype(f32)
    out[:, left] = total_a.astype(out.dtype)
    out[:, right] = total_b.astype(out.dtype)
    for copy in last:
        copy.wait()


def scatter_scratch(rows, width, pieces, more):
    cut = width // 2
    rest = width - cut
    bf16 = jnp.bfloat16
    semaphores = 16 + pieces + more
    return [
        pltpu.VMEM((16, rows, width), bf16),
        pltpu.VMEM((16, rows, width), bf16),
        pltpu.VMEM((4, 4, rows, width), bf16),
        pltpu.VMEM((3, 4, rows, cut), bf16),
        pltpu.VMEM((3, 4, rows, rest), bf16),
        pltpu.VMEM((4, rows, cut), bf16),
        pltpu.VMEM((4, rows, rest), bf16),
        pltpu.VMEM((3, rows, cut), bf16),
        pltpu.VMEM((3, rows, rest), bf16),
        pltpu.SemaphoreType.DMA((semaphores,)),
        pltpu.SemaphoreType.DMA((semaphores,)),
        pltpu.SemaphoreType.DMA((1 + pieces,)),
    ]


def scatter_head(part, exact, low, collective):
    _, rows, width = part.shape
    tall = low.shape[0]
    f32, bf16 = jnp.float32, jnp.bfloat16
    return pl.pallas_call(
        partial(scatter_sum_kernel, [(rows, width)], "head"),
        out_shape=[
            jax.ShapeDtypeStruct((rows, width), f32),
            jax.ShapeDtypeStruct((tall, 128), f32),
        ],
        in_specs=[ANY] * 3,
        out_specs=[VMEM, VMEM],
        scratch_shapes=[pltpu.VMEM((tall, 128), f32), pltpu.VMEM((3, tall, 128), bf16)]
        + scatter_scratch(rows, width, 1, 0),
        compiler_params=pltpu.CompilerParams(
            collective_id=collective, has_side_effects=True, vmem_limit_bytes=12 * 2**20
        ),
    )(part.reshape(16, 2, rows, width), exact, low)


def group_sum_kernel(
    head, wants, given, rest, facts, crossed, table_out, rest_out, seen, total, rest_in, told, sends, arrivals
):
    f32, bf16 = jnp.float32, jnp.bfloat16
    me = here()
    group = lax.axis_index("grp")
    groups = [{"grp": lax.rem(group + d, 4)} for d in (1, 2, 3)]
    plane = [moved(me, *step) for step in AROUND]
    greet(groups + plane)
    mine = quarter(group)
    early = [
        remote(rest.at[:, quarter(groups[d]["grp"])], rest_in.at[d], sends, arrivals, d, groups[d])
        for d in range(3)
    ]
    total[...] = head[...]

    @pl.loop(0, wants.shape[0])
    def _(k):
        row = lax.broadcasted_iota(jnp.int32, (head.shape[0], wants.shape[1]), 0)
        hot = jnp.where(row == wants[pl.ds(k, 1), :], 1.0, 0.0).astype(bf16)
        total[...] += product(hot, given[k])

    rounded = total[...].astype(bf16)
    table_out[:, mine] = rounded
    rounded = rounded.astype(f32)
    squares = jnp.sum(by_eight(rounded * rounded), 0)
    wide = [
        remote(table_out.at[:, mine], table_out.at[:, mine], sends, arrivals, 3 + d, groups[d])
        for d in range(3)
    ]
    for copy in early:
        copy.wait()
    summed = rest[:, mine].astype(f32)
    for d in range(3):
        summed += rest_in[d].astype(f32)
    summed = summed.astype(bf16)
    rest_out[:, mine] = summed
    summed = summed.astype(f32)
    squares += jnp.sum(by_eight(summed * summed), 0)
    told[group, 0:8] = squares
    first = lax.broadcasted_iota(jnp.int32, (8, 128), 0) == 0
    cross = crossed[:, :128] + crossed[:, 128:]
    told[group, 8:16] = facts[...] - jnp.where(first, cross, 0.0)
    copies = []
    for d in range(3):
        copies.append(remote(told.at[group], told.at[group], sends, arrivals, 6 + d, groups[d]))
        wide.append(
            remote(rest_out.at[:, mine], rest_out.at[:, mine], sends, arrivals, 9 + d, groups[d])
        )
    for copy in copies:
        copy.wait()
    seen[number(me)] = told[0] + told[1] + told[2] + told[3]
    copies = []
    for k, place in enumerate(plane):
        copies.append(
            remote(seen.at[number(me)], seen.at[number(me)], sends, arrivals, 12 + k, place)
        )
    for copy in copies + wide:
        copy.wait()


def sum_of_groups(head, wants, given, rest, facts, crossed, collective):
    count = 12 + len(AROUND)
    bf16 = jnp.bfloat16
    return pl.pallas_call(
        group_sum_kernel,
        out_shape=[
            jax.ShapeDtypeStruct((head.shape[0], 512), bf16),
            jax.ShapeDtypeStruct(rest.shape, rest.dtype),
            jax.ShapeDtypeStruct((32, 16, 128), jnp.float32),
        ],
        in_specs=[VMEM] * 6,
        out_specs=[VMEM, VMEM, VMEM],
        scratch_shapes=[
            pltpu.VMEM(head.shape, jnp.float32),
            pltpu.VMEM((3, rest.shape[0], 128), rest.dtype),
            pltpu.VMEM((4, 16, 128), jnp.float32),
            pltpu.SemaphoreType.DMA((count,)),
            pltpu.SemaphoreType.DMA((count,)),
        ],
        compiler_params=pltpu.CompilerParams(
            collective_id=collective, has_side_effects=True, vmem_limit_bytes=40 * 2**20
        ),
    )(head, wants, given, rest, facts, crossed)


def slots(tokens, own_rows):
    count = tokens.shape[0]
    row, column = tokens[:, None], tokens[None, :]
    place = jnp.arange(count)
    repeated = jnp.any((row == column) & (place[:, None] < place[None, :]), axis=0)
    owner = tokens // own_rows
    counts = ~repeated[:, None] & (row >= (owner * own_rows)[None, :]) & (row < column)
    return owner, ~repeated, jnp.sum(counts.astype(jnp.int32), axis=0)


def slot_in_round(owner, rank, room, turn, apart=None):
    at = rank - turn * room
    return jnp.where((at >= 0) & (at < room), owner * (apart or room) + at, -1)


def wanted_rows(slot, first, local, places):
    hit = (jnp.where(first, slot, -1)[:, None] == jnp.arange(places)[None, :])
    return jnp.sum(jnp.where(hit, local[:, None] + 1, 0), axis=0) - 1


def one_hot(index, count):
    return (index[:, None] == jnp.arange(count)[None, :]).astype(jnp.bfloat16)


def product(left, right):
    return jnp.dot(left, right, preferred_element_type=jnp.float32)


def folded(rows):
    return jnp.concatenate(jnp.split(rows, 2, axis=2), axis=1)


def unfolded(rows):
    return jnp.concatenate(jnp.split(rows, 2, axis=1), axis=2)


def layer_norm(value, gain, shift):
    mean = jnp.mean(value, -1, keepdims=True)
    centred = value - mean
    var = jnp.mean(centred * centred, -1, keepdims=True)
    return centred * lax.rsqrt(var + norm_eps) * gain + shift


def project(left, right):
    return jnp.einsum("blk,kn->bln", left, right, preferred_element_type=jnp.float32)


def split_heads(packed, width):
    batch, span = (packed.shape[0], packed.shape[1])
    return [
        packed[:, :, piece * width : (piece + 1) * width].reshape(batch, span, width // HD, HD)
        for piece in range(3)
    ]


def masked_scores(query, keyed, lengths):
    scores = jnp.einsum(
        "bqhd,bkhd->bhqk", query, keyed, preferred_element_type=jnp.float32
    ) * HD ** (-0.5)
    valid = jnp.arange(query.shape[1])[None, :] < lengths[:, None]
    return jnp.where(valid[:, None, None, :], scores, -1e30)


def forward(embedded, lengths, weights):
    w_qkv, w_out, w_up, w_down, norms = weights
    norms = norms.astype(jnp.float32)
    width = w_out.shape[1]
    first = layer_norm(embedded, norms[:, 0], norms[:, 1])
    first_low = first.astype(jnp.bfloat16)
    packed = project(first_low, w_qkv).astype(jnp.bfloat16)
    query, keyed, valued = split_heads(packed, width)
    scores = masked_scores(query, keyed, lengths)
    top = jnp.max(scores, -1, keepdims=True)
    total = jnp.sum(jnp.exp(scores - top), -1, keepdims=True)
    probs = (jnp.exp(scores - top) / total).astype(jnp.bfloat16)
    context = jnp.einsum("bhqk,bkhd->bqhd", probs, valued, preferred_element_type=jnp.float32)
    context = context.reshape(first.shape).astype(jnp.bfloat16)
    joined = first + project(context, w_out)
    second = layer_norm(joined, norms[:, 2], norms[:, 3])
    second_low = second.astype(jnp.bfloat16)
    hidden_pre = project(second_low, w_up)
    active = jax.nn.gelu(hidden_pre, approximate=False).astype(jnp.bfloat16)
    summed = second + project(active, w_down)
    final = layer_norm(summed, norms[:, 4], norms[:, 5])
    saved = (
        embedded,
        first_low,
        packed,
        context,
        joined,
        second_low,
        hidden_pre,
        active,
        summed,
    )
    return (final, saved)


def norm_back(value, gain, grad):
    mean = jnp.mean(value, -1, keepdims=True)
    centred = value - mean
    scale = lax.rsqrt(jnp.mean(centred * centred, -1, keepdims=True) + norm_eps)
    unit = centred * scale
    scaled = grad * gain
    back = scaled - jnp.mean(scaled, -1, keepdims=True)
    back = scale * (back - unit * jnp.mean(scaled * unit, -1, keepdims=True))
    return back, jnp.sum(grad * unit, 0, keepdims=True), jnp.sum(grad, 0, keepdims=True)


def product_of(left, right, dims):
    return lax.dot_general(left, right, (dims, ((), ())), preferred_element_type=jnp.float32)


def backward_kernel(
    lengths,
    picks,
    slot,
    grad_rows,
    embedded,
    first_low,
    packed,
    context,
    joined,
    second_low,
    hidden_pre,
    active,
    summed,
    norms,
    w_qkv,
    w_out,
    w_up,
    w_down,
    g_qkv,
    g_out,
    g_up,
    g_down,
    small,
    low_emb,
    given,
    d_packed,
    d_context,
    carried,
):
    f32, bf16 = jnp.float32, jnp.bfloat16
    span, width = embedded.shape
    rows, columns, both = ((0,), (0,)), ((1,), (1,)), ((1,), (0,))
    row = lax.broadcasted_iota(jnp.int32, (span, picks.shape[1]), 0)
    hot = jnp.where(row == picks[...], 1.0, 0.0)
    d_final = jnp.dot(
        hot, grad_rows[...], preferred_element_type=f32, precision=lax.Precision.HIGHEST
    )
    d_summed, gain_c, shift_c = norm_back(summed[...], norms[4:5], d_final)
    d_ffn = d_summed.astype(bf16)
    carried[...] = d_summed

    @pl.loop(0, w_up.shape[1] // width)
    def _(k):
        cols = pl.ds(pl.multiple_of(k * width, width), width)
        blocks = g_down.shape[0] * width // w_up.shape[1]
        piece = product_of(active[:, cols], d_ffn, rows)
        g_down[pl.ds(k * blocks, blocks)] = piece.reshape(blocks, *g_down.shape[1:]).astype(bf16)
        pre = hidden_pre[:, cols]
        slope = 0.5 * (1.0 + lax.erf(pre * (0.5**0.5)))
        slope += pre * (jnp.exp(-0.5 * pre * pre) * (0.5 / math.pi) ** 0.5)
        d_up = (slope * product_of(d_ffn, w_down[cols], columns)).astype(bf16)
        piece = product_of(second_low[...], d_up, rows)
        g_up[:, :, :, cols] = piece.reshape(*g_up.shape[:3], width).astype(bf16)
        carried[...] += product_of(d_up, w_up[:, cols], columns)

    d_joined, gain_b, shift_b = norm_back(joined[...], norms[2:3], carried[...])
    d_attn = d_joined.astype(bf16)
    g_out[...] = product_of(context[...], d_attn, rows).reshape(g_out.shape).astype(bf16)
    d_context[...] = product_of(d_attn, w_out[...], columns).astype(bf16)
    lane = lax.broadcasted_iota(jnp.int32, (span, 2 * HD), 1)
    halves = [jnp.where(lane < HD, 1.0, 0.0), jnp.where(lane < HD, 0.0, 1.0)]
    valid = lax.broadcasted_iota(jnp.int32, (span, span), 1) < lengths[0, 0]

    @pl.loop(0, width // (2 * HD))
    def _(k):
        at = pl.multiple_of(k * 2 * HD, 2 * HD)
        query, keyed, valued = [
            packed[:, pl.ds(piece * width + at, 2 * HD)] for piece in range(3)
        ]
        d_heads = d_context[:, pl.ds(at, 2 * HD)]
        d_query, d_keyed, d_valued = [jnp.zeros((span, 2 * HD), f32)] * 3
        for half in halves:
            low = half.astype(bf16)
            scores = product_of(query * low, keyed, columns) * HD ** (-0.5)
            scores = jnp.where(valid, scores, -1e30)
            spread = jnp.exp(scores - jnp.max(scores, -1, keepdims=True))
            probs = spread * (1.0 / jnp.sum(spread, -1, keepdims=True))
            d_valued += half * product_of(probs.astype(bf16), d_heads, rows)
            d_probs = product_of(d_heads * low, valued, columns)
            d_scores = probs * (d_probs - jnp.sum(probs * d_probs, -1, keepdims=True))
            d_scores = d_scores.astype(bf16)
            d_query += half * product_of(d_scores, keyed, both)
            d_keyed += half * product_of(d_scores, query, rows)
        for piece, value in enumerate((d_query * HD ** (-0.5), d_keyed * HD ** (-0.5), d_valued)):
            d_packed[:, pl.ds(piece * width + at, 2 * HD)] = value.astype(bf16)

    carried[...] = d_joined

    @pl.loop(0, 3)
    def _(k):
        cols = pl.ds(pl.multiple_of(k * width, width), width)
        piece = product_of(first_low[...], d_packed[:, cols], rows)
        g_qkv[:, :, :, cols] = piece.reshape(*g_qkv.shape[:3], width).astype(bf16)
        carried[...] += product_of(d_packed[:, cols], w_qkv[:, cols], columns)

    d_emb, gain_a, shift_a = norm_back(embedded[...], norms[0:1], carried[...])
    carried[...] = d_emb
    lines = [gain_a, shift_a, gain_b, shift_b, gain_c, shift_c, jnp.zeros((2, width), f32)]
    lines = jnp.concatenate(lines, axis=0)
    owner = lax.broadcasted_iota(jnp.int32, lines.shape, 1)

    @pl.loop(0, 32)
    def _(k):
        mine = (owner >= k * (width // 32)) & (owner < (k + 1) * (width // 32))
        block = [carried[pl.ds(pl.multiple_of(k * 8, 8), 8)], jnp.where(mine, lines, 0.0)]
        small[k // 2, lax.rem(k, 2)] = jnp.concatenate(block, axis=0).astype(bf16)

    low = d_emb.astype(bf16)
    low_emb[...] = low

    @pl.loop(0, given.shape[0] // span)
    def _(k):
        place = lax.broadcasted_iota(jnp.int32, (span, span), 0) + k * span
        place = jnp.where(place == slot[...], 1.0, 0.0).astype(bf16)
        given[pl.ds(pl.multiple_of(k * span, span), span)] = product(place, low).astype(bf16)


def finish_kernel(plan, *refs):
    inputs, (out, side_out, low_emb), refs = refs[:18], refs[18:21], refs[21:]
    parts, (given, d_packed, d_context, carried), refs = refs[:5], refs[5:9], refs[9:]
    g_qkv, g_out, g_up, g_down, small = parts
    work = partial(
        backward_kernel,
        *inputs,
        g_qkv,
        g_out,
        g_up,
        g_down,
        small,
        low_emb,
        given,
        d_packed,
        d_context,
        carried,
    )
    scatter_sum_kernel(plan, "rows", *parts, given, out, side_out, *refs, work=work)


def backward(lengths, picks, slot, places, weights, saved, grad_rows, collective):
    w_qkv, w_out, w_up, w_down, norms = weights
    span, width = saved[0].shape[1:]
    f32, bf16 = jnp.float32, jnp.bfloat16
    plan = [(w.shape[0] // 32, w.shape[1]) for w in (w_qkv, w_out, w_up, w_down)] + [(16, width)]
    rows = sum(r * (c // width) for r, c in plan)
    pieces = sum(c // width for _, c in plan)
    return pl.pallas_call(
        partial(finish_kernel, plan),
        out_shape=[
            jax.ShapeDtypeStruct((rows, width), bf16),
            jax.ShapeDtypeStruct((32, 4, places // 32, 128), bf16),
            jax.ShapeDtypeStruct((span, width), bf16),
        ],
        in_specs=[pl.BlockSpec(memory_space=pltpu.SMEM)] + [VMEM] * 17,
        out_specs=[VMEM] * 3,
        scratch_shapes=[pltpu.VMEM((16, 2, *size), bf16) for size in plan]
        + [
            pltpu.VMEM((places, width), bf16),
            pltpu.VMEM((span, 3 * width), bf16),
            pltpu.VMEM((span, width), bf16),
            pltpu.VMEM((span, width), f32),
            pltpu.VMEM((4, places, 128), bf16),
        ]
        + scatter_scratch(rows, width, pieces, len(AROUND)),
        compiler_params=pltpu.CompilerParams(
            collective_id=collective, has_side_effects=True, vmem_limit_bytes=36 * 2**20
        ),
    )(
        lengths[None],
        picks,
        slot[None],
        grad_rows,
        *[value[0] for value in saved],
        norms.astype(f32).T,
        w_qkv,
        w_out,
        w_up,
        w_down,
    )


def per_device(
    ids,
    lengths,
    picks,
    labels,
    s_table,
    s_pos,
    s_qkv,
    s_out,
    s_up,
    s_down,
    s_norms,
    m_table,
    m_pos,
    m_qkv,
    m_out,
    m_up,
    m_down,
    m_norms,
    a_table,
    a_pos,
    a_qkv,
    a_out,
    a_up,
    a_down,
    a_norms,
    t_table,
    t_pos,
    t_qkv,
    t_out,
    t_up,
    t_down,
    t_norms,
):
    masters = (s_table, s_pos, s_qkv, s_out, s_up, s_down, s_norms)
    momenta = (m_table, m_pos, m_qkv, m_out, m_up, m_down, m_norms)
    averages = (a_table, a_pos, a_qkv, a_out, a_up, a_down, a_norms)
    f32, bf16 = jnp.float32, jnp.bfloat16
    fsdp = lax.axis_size(FSDP)
    width, t_width = s_table.shape[1], t_table.shape[2]
    vocab_own = s_table.shape[0]
    picked = picks.shape[1]
    span = ids.shape[1]

    facts = jnp.concatenate([ids, picks, jnp.broadcast_to(lengths[:, None], (1, 64))], axis=1)
    facts = jnp.pad(facts.reshape(3, 128), ((0, 5), (0, 0)))
    facts = exchange_groups(jnp.broadcast_to(facts, (4, 8, 128)), 9)[:, :3].reshape(4, -1)
    group_ids, group_picks = facts[:, :span], facts[:, span : span + picked]
    group_lengths = facts[:, span + picked]
    own_table = s_table.astype(bf16)
    t_owner, t_first, t_rank = slots(group_ids.reshape(-1), vocab_own)
    s_owners, s_firsts, s_ranks = jax.vmap(lambda one: slots(one, vocab_own))(group_ids)
    my_group = lax.axis_index("grp")
    s_owner, s_rank = (
        lax.dynamic_index_in_dim(v, my_group, 0, keepdims=False) for v in (s_owners, s_ranks)
    )
    most = jnp.maximum(jnp.max(t_rank) // T_ROOM, jnp.max(s_ranks) // S_ROOM) + 1
    t_local = group_ids.reshape(-1) - t_owner * vocab_own
    s_locals = group_ids - s_owners * vocab_own

    def asked(turn):
        t_slot = slot_in_round(t_owner, t_rank, T_ROOM, turn)
        s_slot = slot_in_round(s_owner, s_rank, S_ROOM, turn)
        t_ask = wanted_rows(t_slot, t_first, t_local, fsdp * T_ROOM).reshape(fsdp, T_ROOM)
        s_asks = jax.vmap(partial(wanted_rows, places=fsdp * S_APART))(
            slot_in_round(s_owners, s_ranks, S_ROOM, turn, S_APART), s_firsts, s_locals
        ).reshape(-1, fsdp, S_APART)
        s_ask = lax.dynamic_index_in_dim(s_asks, my_group, 0, keepdims=False)[:, :S_ROOM]
        s_asks = jnp.moveaxis(s_asks, 0, 1).reshape(fsdp, -1)
        return t_slot, s_slot, t_ask, s_ask, s_asks

    def answer(t_want, s_want):
        t_sent = product(one_hot(t_want.reshape(-1), vocab_own), t_table[0]).astype(bf16)
        s_sent = product(one_hot(s_want.reshape(-1), vocab_own), own_table).astype(bf16)
        return jnp.concatenate(
            [t_sent.reshape(fsdp, T_ROOM, t_width), folded(s_sent.reshape(fsdp, S_ROOM, width))],
            axis=2,
        )

    def placed(got, t_slot, s_slot):
        t_got = got[:, :, :t_width].reshape(-1, t_width)
        s_got = unfolded(got[:, :, t_width:]).reshape(-1, width)
        return (
            product(one_hot(t_slot, fsdp * T_ROOM), t_got),
            product(one_hot(s_slot, fsdp * S_ROOM), s_got),
        )

    def swap(value):
        return lax.all_to_all(value, FSDP, split_axis=0, concat_axis=0, tiled=True)

    def ask_again(turn):
        t_slot, s_slot, t_ask, s_ask, s_asks = asked(turn)
        wants = swap(jnp.concatenate([t_ask, s_ask, s_asks], axis=1))
        both = T_ROOM + S_ROOM
        return t_slot, s_slot, wants[:, :T_ROOM], wants[:, T_ROOM:both], wants[:, both:]

    def more_rows(state):
        turn, t_emb, s_emb = state
        t_slot, s_slot, t_want, s_want, _ = ask_again(turn)
        t_more, s_more = placed(swap(answer(t_want, s_want)), t_slot, s_slot)
        return turn + 1, t_emb + t_more.astype(bf16), s_emb + s_more.astype(bf16)

    t_slot, s_slot, t_ask, s_ask, s_asks = asked(0)
    line = jnp.concatenate(
        [t_ask, s_ask, jnp.broadcast_to(most, (fsdp, 128 - T_ROOM - S_ROOM))], axis=1
    )
    lines = [
        line,
        jnp.broadcast_to(jnp.concatenate([picks, labels], axis=1), (fsdp, 2 * picked)),
        jnp.broadcast_to(lengths[:, None], (fsdp, 128)),
        s_asks,
    ]
    notes = jnp.stack(lines + [jnp.zeros((fsdp, 128), jnp.int32)] * 4, axis=1)
    notes, got = route(notes, t_table[0], own_table, 1)
    wants = notes[:, 3]
    rounds = jnp.max(notes[:, 0, T_ROOM + S_ROOM])
    plane_picks, plane_labels = notes[:, 1, :picked], notes[:, 1, picked : 2 * picked]
    plane_lengths = notes[:, 2, 0]
    nothing = (jnp.zeros((t_slot.shape[0], t_width), bf16), jnp.zeros((span, width), bf16))
    _, t_extra, s_extra = lax.while_loop(
        lambda state: state[0] < rounds, more_rows, (jnp.int32(1), *nothing)
    )

    def pieces(blocks, qkv, out, up, down, pos, norms):
        lines = norms.shape[0]
        tail = jnp.moveaxis(norms.astype(f32).reshape(lines, blocks, -1), 1, 0)
        tail = jnp.pad(tail, ((0, 0), (0, 8 - lines), (0, width - tail.shape[2])))
        small = jnp.concatenate([pos.reshape(blocks, -1, width).astype(f32), tail], axis=1)
        big = [part.astype(bf16).reshape(blocks, -1, part.shape[1]) for part in (qkv, out, up, down)]
        return big + [lax.optimization_barrier(small.astype(bf16))]

    def pack(parts):
        columns = [
            part[:, :, at : at + width] for part in parts for at in range(0, part.shape[2], width)
        ]
        return jnp.concatenate(columns, axis=1)

    def unpack(packed):
        blocks, lead = packed.shape[0], s_qkv.shape[0]

        def across(at, count):
            return jnp.concatenate(
                [
                    packed[:, at + k * lead : at + (k + 1) * lead].reshape(-1, width)
                    for k in range(count)
                ],
                axis=1,
            )

        at_out = s_qkv.shape[1] // width * lead
        at_up = at_out + lead
        at_down = at_up + s_up.shape[1] // width * lead
        at_pos = at_down + s_down.shape[0]
        at_norms = at_pos + s_pos.shape[0]
        return (
            across(0, s_qkv.shape[1] // width),
            across(at_out, 1),
            across(at_up, s_up.shape[1] // width),
            packed[:, at_down:at_pos].reshape(-1, width),
            packed[:, at_pos:at_norms].reshape(-1, width),
            jnp.moveaxis(
                packed[:, at_norms : at_norms + s_norms.shape[1], :lead], 1, 0
            ).reshape(s_norms.shape[1], -1),
        )

    own_packed = pack(pieces(1, s_qkv, s_out, s_up, s_down, s_pos, s_norms.T))
    w_qkv, w_out, w_up, w_down, positions, norms = unpack(
        lax.all_gather(own_packed, FSDP, axis=0, tiled=True)
    )
    student = (w_qkv, w_out, w_up, w_down, norms.T)
    heads = lax.all_gather(t_table[0], "grp", axis=0, tiled=False)

    taken = teacher_rows(
        group_lengths,
        t_slot,
        group_picks,
        got.reshape(-1, got.shape[2]),
        t_extra.reshape(-1, span, t_width),
        t_pos[0],
        t_norms[0].T,
        t_qkv[0],
        t_out[0],
        t_up[0],
        t_down[0],
    )
    taken, heads = lax.optimization_barrier((taken, heads))
    rows = exchange_groups(taken, 10)
    s_extra, got, rows = lax.optimization_barrier((s_extra, got, rows))
    rows = lax.all_gather(rows, FSDP, axis=0, tiled=False)

    s_got = unfolded(got[:, :, t_width:]).reshape(-1, width)
    s_emb = product(one_hot(s_slot, fsdp * S_ROOM), s_got) + s_extra.astype(f32)
    embedded = s_emb[None] + positions.astype(f32)[None]
    final, saved = forward(embedded, lengths, student)
    own_rows = jnp.take_along_axis(final, picks[:, :, None], axis=1).astype(bf16)[0]
    h = gather_plane(own_rows, 11)
    base = lax.axis_index(FSDP) * vocab_own
    labels_here = plane_labels.reshape(1, -1) - base
    z, z_stats = vocabulary_logits(labels_here, h.reshape(fsdp, 1, picked, width), own_table[None])
    logits, stats = vocabulary_logits(labels_here, rows, heads)
    stats = jnp.concatenate([stats, z_stats], axis=0)
    plane_counted = (plane_picks < plane_lengths[:, None]).astype(f32).reshape(-1, 1, 2 * picked)
    chip = lax.axis_index(("y", "x"))
    chip_counted = lax.dynamic_index_in_dim(plane_counted, chip, 0, keepdims=False)
    shift, own_loss = blend(stats, chip_counted, 3)
    head_grad, head_low, grad_rows, crossed = head_grads(logits, z, shift, h, own_table)
    grad_rows, head_grad = scatter_head(
        grad_rows.reshape(fsdp, picked, width), head_grad, head_low, 5
    )

    g_slot = slot_in_round(s_owner, s_rank, S_ROOM, 0, S_APART)
    rest, got, low_embedded = backward(
        lengths, picks, g_slot, fsdp * S_APART, student, saved, grad_rows, 7
    )

    def given(turn):
        slot = slot_in_round(s_owner, s_rank, S_ROOM, turn, S_APART)
        hot = (jnp.arange(fsdp * S_APART)[:, None] == slot[None, :]).astype(bf16)
        return product(hot, low_embedded).astype(bf16)

    def more_grads(state):
        turn, total = state
        wants = ask_again(turn)[4]
        rows = jnp.stack(jnp.split(given(turn), 4, axis=1))
        rows = lax.all_to_all(rows, "grp", split_axis=0, concat_axis=0, tiled=True)
        rows = swap(jnp.moveaxis(rows.reshape(4, fsdp, S_APART, -1), 0, 1))
        hot = one_hot(wants.reshape(-1), vocab_own).T
        return turn + 1, total + product(hot, rows.reshape(-1, rows.shape[3]))

    _, head_grad = lax.while_loop(
        lambda state: state[0] < rounds, more_grads, (jnp.int32(1), head_grad)
    )
    table_sum, rest_sum, seen = sum_of_groups(
        head_grad, wants.reshape(4, -1), got.reshape(4, -1, got.shape[3]), rest, own_loss, crossed, 8
    )
    turned = [group[:6] + (group[6].T,) for group in (masters, momenta, averages)]
    loss_sum, count, clip_norm, *outs = update(seen, table_sum, rest_sum, *turned)
    outs = tuple(out.T if k % 7 == 6 else out for k, out in enumerate(outs))
    return (loss_sum.reshape(()), count.reshape(()), clip_norm[0, 0]) + outs


def solution(mesh):
    finer = Mesh(
        mesh.devices.reshape(mesh.shape["grp"], 4, 4, 2), ("grp", "y", "x", "c")
    )
    return jax.shard_map(
        per_device,
        mesh=finer,
        in_specs=(
            P(GRP_FSDP, None),
            P(GRP_FSDP),
            P(GRP_FSDP, None),
            P(GRP_FSDP, None),
            P(FSDP, None),
            P(FSDP, None),
            P(FSDP, None),
            P(FSDP, None),
            P(FSDP, None),
            P(FSDP, None),
            P(FSDP, None),
            P(FSDP, None),
            P(FSDP, None),
            P(FSDP, None),
            P(FSDP, None),
            P(FSDP, None),
            P(FSDP, None),
            P(FSDP, None),
            P(FSDP, None),
            P(FSDP, None),
            P(FSDP, None),
            P(FSDP, None),
            P(FSDP, None),
            P(FSDP, None),
            P(FSDP, None),
            P("grp", FSDP, None),
            P("grp", None, None),
            P("grp", None, None),
            P("grp", None, None),
            P("grp", None, None),
            P("grp", None, None),
            P("grp", None, None),
        ),
        out_specs=(
            P(),
            P(),
            P(),
            P(FSDP, None),
            P(FSDP, None),
            P(FSDP, None),
            P(FSDP, None),
            P(FSDP, None),
            P(FSDP, None),
            P(FSDP, None),
            P(FSDP, None),
            P(FSDP, None),
            P(FSDP, None),
            P(FSDP, None),
            P(FSDP, None),
            P(FSDP, None),
            P(FSDP, None),
            P(FSDP, None),
            P(FSDP, None),
            P(FSDP, None),
            P(FSDP, None),
            P(FSDP, None),
            P(FSDP, None),
            P(FSDP, None),
        ),
        check_vma=False,
    )
```

```python
import functools
import math
from functools import partial

import jax
import jax.numpy as jnp
from jax import lax
from jax.experimental import pallas as pl
from jax.experimental.pallas import tpu as pltpu
from jax.sharding import Mesh
from jax.sharding import PartitionSpec as P

HD = 64
FSDP = ("y", "x", "c")
GRP_FSDP = ("grp", "y", "x", "c")
T_ROOM = 48
S_ROOM = 24
S_APART = 32
WIDE = 56 * 2**20

norm_eps = 1e-12
clip_limit = 0.001
learn_rate = 100000.0
momentum_decay = 0.9
average_decay = 0.9


SIZES = {"y": 4, "x": 4, "c": 2}
MESH = pl.DeviceIdType.MESH
ANY = pl.BlockSpec(memory_space=pl.ANY)
VMEM = pl.BlockSpec(memory_space=pltpu.VMEM)
AROUND = [((11 * k) % 32 // 8, (11 * k) % 8 // 2, (11 * k) % 2) for k in range(1, 32)]


def here():
    return {axis: lax.axis_index(axis) for axis in SIZES}


def moved(me, dy, dx, dc):
    return {
        "y": lax.rem(me["y"] + dy, 4),
        "x": lax.rem(me["x"] + dx, 4),
        "c": lax.rem(me["c"] + dc, 2),
    }


def number(place):
    return (place["y"] * 4 + place["x"]) * 2 + place["c"]


def greet(places, work=None):
    barrier = pltpu.get_barrier_semaphore()
    for place in places:
        pl.semaphore_signal(barrier, inc=1, device_id=place, device_id_type=MESH)
    if work:
        work()
    pl.semaphore_wait(barrier, len(places))


def remote(source, target, sends, arrivals, at, place):
    copy = pltpu.make_async_remote_copy(
        src_ref=source,
        dst_ref=target,
        send_sem=sends.at[at],
        recv_sem=arrivals.at[at],
        device_id=place,
        device_id_type=MESH,
    )
    copy.start()
    return copy


def route_kernel(notes, t_table, s_table, heard, got, sent, wants, sends, arrivals, local):
    f32, bf16 = jnp.float32, jnp.bfloat16
    me = here()
    greet([moved(me, *step) for step in AROUND])
    copies = []
    for k, step in enumerate(AROUND):
        place = moved(me, *step)
        copies.append(
            remote(notes.at[number(place)], heard.at[number(me)], sends, arrivals, k, place)
        )
    heard[number(me)] = notes[number(me)]
    for copy in copies:
        copy.wait()
    all_wants = heard[:, 0, :].astype(f32).T
    vocab, t_width = t_table.shape
    half = s_table.shape[1] // 2
    batch = wants.shape[2]
    for k in range(wants.shape[0]):
        wants[k] = all_wants[:, k * batch : (k + 1) * batch]

    def rows_of(k, at, room, table):
        index = jnp.concatenate(
            [wants[k, at : at + room, p : p + 1] for p in range(batch)], axis=0
        )
        entry = lax.broadcasted_iota(jnp.int32, (index.shape[0], vocab), 1).astype(f32)
        hot = jnp.where(entry == index, 1.0, 0.0).astype(bf16)
        return product(hot, table[...])

    @pl.loop(0, wants.shape[0])
    def _(k):
        t_rows = rows_of(k, 0, T_ROOM, t_table)
        s_rows = rows_of(k, T_ROOM, S_ROOM, s_table)
        for j in range(batch):
            p = k * batch + j
            sent[p, :, :t_width] = t_rows[j * T_ROOM : (j + 1) * T_ROOM].astype(bf16)
            own = s_rows[j * S_ROOM : (j + 1) * S_ROOM]
            own = jnp.concatenate([own[:, :half], own[:, half:]], axis=0)
            sent[p, :, t_width:] = own.astype(bf16)

    copies = []
    for k, step in enumerate(AROUND):
        place = moved(me, *step)
        copies.append(
            remote(
                sent.at[number(place)], got.at[number(me)], sends, arrivals, len(AROUND) + k, place
            )
        )
    mine = pltpu.make_async_copy(sent.at[number(me)], got.at[number(me)], local)
    mine.start()
    mine.wait()
    for copy in copies:
        copy.wait()


def route(notes, t_table, s_table, collective):
    width = t_table.shape[1] + s_table.shape[1] // 2
    return pl.pallas_call(
        route_kernel,
        out_shape=[
            jax.ShapeDtypeStruct(notes.shape, notes.dtype),
            jax.ShapeDtypeStruct((32, T_ROOM, width), jnp.bfloat16),
        ],
        in_specs=[VMEM, VMEM, VMEM],
        out_specs=[VMEM, ANY],
        scratch_shapes=[
            pltpu.VMEM((32, T_ROOM, width), jnp.bfloat16),
            pltpu.VMEM((4, 128, 8), jnp.float32),
            pltpu.SemaphoreType.DMA((2 * len(AROUND),)),
            pltpu.SemaphoreType.DMA((2 * len(AROUND),)),
            pltpu.SemaphoreType.DMA,
        ],
        compiler_params=pltpu.CompilerParams(
            collective_id=collective, has_side_effects=True, vmem_limit_bytes=WIDE
        ),
    )(notes, t_table, s_table)


def group_exchange_kernel(source, target, sends, arrivals, local):
    group = lax.axis_index("grp")
    groups = [lax.rem(group + d, 4) for d in (1, 2, 3)]
    greet([{"grp": g} for g in groups])
    copies = [
        remote(source.at[g], target.at[group], sends, arrivals, d, {"grp": g})
        for d, g in enumerate(groups)
    ]
    own = pltpu.make_async_copy(source.at[group], target.at[group], local)
    own.start()
    own.wait()
    for copy in copies:
        copy.wait()


def exchange_groups(value, collective):
    return pl.pallas_call(
        group_exchange_kernel,
        out_shape=jax.ShapeDtypeStruct(value.shape, value.dtype),
        in_specs=[ANY],
        out_specs=ANY,
        scratch_shapes=[
            pltpu.SemaphoreType.DMA((3,)),
            pltpu.SemaphoreType.DMA((3,)),
            pltpu.SemaphoreType.DMA,
        ],
        compiler_params=pltpu.CompilerParams(collective_id=collective, has_side_effects=True),
    )(value)


def gather_kernel(source, target, sends, arrivals, local):
    me = here()
    chip, core = me["y"] * 4 + me["x"], me["c"]
    chips = [moved(me, (7 * k) % 16 // 4, (7 * k) % 4, 0) for k in range(1, 16)]
    sibling = moved(me, 0, 0, 1)
    greet(chips + [sibling])
    copies = [
        remote(source, target.at[chip, core], sends, arrivals, k, place)
        for k, place in enumerate(chips)
    ]
    own = pltpu.make_async_copy(source, target.at[chip, core], local)
    own.start()
    own.wait()
    for copy in copies:
        copy.wait()
    remote(target.at[:, core], target.at[:, core], sends, arrivals, 15, sibling).wait()


def gather_plane(value, collective):
    rows, width = value.shape
    out = pl.pallas_call(
        gather_kernel,
        out_shape=jax.ShapeDtypeStruct((16, 2, rows, width), value.dtype),
        in_specs=[ANY],
        out_specs=ANY,
        scratch_shapes=[
            pltpu.SemaphoreType.DMA((16,)),
            pltpu.SemaphoreType.DMA((16,)),
            pltpu.SemaphoreType.DMA,
        ],
        compiler_params=pltpu.CompilerParams(collective_id=collective, has_side_effects=True),
    )(value)
    return out.reshape(32 * rows, width)


def update_kernel(seen, table_grad, rest_grad, *refs):
    masters, momenta, averages = refs[:7], refs[7:14], refs[14:21]
    loss_sum, count_out, clip_out = refs[21:24]
    outs = refs[24:]
    facts = jnp.sum(seen[...], 0)
    squares, loss, count = [jnp.sum(line) for line in (facts[:8], facts[8:9], facts[9:10])]
    clip = jnp.sqrt(jnp.full((8, 128), squares)) / count
    factor = (jnp.minimum(1.0, clip_limit / clip) / count)[0:1, 0:1]

    def step(k, grad):
        clipped = grad * factor
        moment = momentum_decay * momenta[k][...] + clipped
        weight = masters[k][...] - learn_rate * (clipped + momentum_decay * moment)
        outs[k][...] = weight
        outs[7 + k][...] = moment
        outs[14 + k][...] = average_decay * averages[k][...] + (1.0 - average_decay) * weight

    step(0, table_grad[...].astype(jnp.float32))

    @pl.when(pl.program_id(0) == 0)
    def _():
        loss_sum[0, 0] = loss
        count_out[0, 0] = count
        clip_out[...] = clip
        width = rest_grad.shape[1]
        at = 0
        for k in (2, 3, 4, 5):
            rows, columns = masters[k].shape
            blocks = []
            for _ in range(columns // width):
                blocks.append(rest_grad[at : at + rows].astype(jnp.float32))
                at += rows
            step(k, blocks[0] if len(blocks) == 1 else jnp.concatenate(blocks, axis=1))
        small = rest_grad[at : at + 16].astype(jnp.float32)
        step(1, small[:8])
        lines, columns = masters[6].shape
        at = ((lax.axis_index("y") * 4 + lax.axis_index("x")) * 2 + lax.axis_index("c")) * columns
        row = lax.broadcasted_iota(jnp.int32, (width, columns), 0) - at
        own = lax.broadcasted_iota(jnp.int32, (width, columns), 1) == row
        own = jnp.where(own, 1.0, 0.0).astype(jnp.bfloat16)
        step(6, product(small.astype(jnp.bfloat16), own)[8 : 8 + lines])


def update(seen, table_grad, rest_grad, masters, momenta, averages):
    steps = 5
    rows, width = table_grad.shape

    def whole(shape):
        return pl.BlockSpec(shape, lambda i: (0,) * len(shape))

    tall = pl.BlockSpec((rows // steps, width), lambda i: (i, 0))
    states = [tall] + [whole(m.shape) for m in masters[1:]]
    scalar = pl.BlockSpec(memory_space=pltpu.SMEM)
    one = jax.ShapeDtypeStruct((1, 1), jnp.float32)
    tile = jax.ShapeDtypeStruct((8, 128), jnp.float32)
    return pl.pallas_call(
        update_kernel,
        grid=(steps,),
        out_shape=[one, one, tile]
        + [jax.ShapeDtypeStruct(m.shape, m.dtype) for m in masters] * 3,
        in_specs=[whole(seen.shape), tall, whole(rest_grad.shape)] + states * 3,
        out_specs=[scalar, scalar, whole(tile.shape)] + states * 3,
        compiler_params=pltpu.CompilerParams(vmem_limit_bytes=WIDE),
    )(seen, table_grad, rest_grad, *masters, *momenta, *averages)


def normed(value, gain, shift):
    mean = jnp.mean(value, -1, keepdims=True)
    centred = value - mean
    var = jnp.mean(centred * centred, -1, keepdims=True)
    return centred * lax.rsqrt(var + norm_eps) * gain + shift


def teacher_kernel(
    lengths, slot, picks, got, extra, pos, norms, w_qkv, w_out, w_up, w_down, out, qkv, ctx
):
    f32, bf16 = jnp.float32, jnp.bfloat16
    span, width = pos.shape
    length = lengths[0, pl.program_id(0)]

    def pick(index, count):
        wide = lax.broadcasted_iota(jnp.int32, (index.shape[0], count), 1)
        return jnp.where(wide == index, 1.0, 0.0).astype(bf16)

    lines = norms[...].astype(f32)

    def scale(k):
        return lines[2 * k : 2 * k + 1], lines[2 * k + 1 : 2 * k + 2]

    emb = product(pick(slot[0], got.shape[0]), got[...])
    emb = emb + extra[0].astype(f32) + pos[...].astype(f32)
    first = normed(emb, *scale(0))
    qkv[...] = product(first.astype(bf16), w_qkv[...]).astype(bf16)
    lane = lax.broadcasted_iota(jnp.int32, (span, 2 * HD), 1)
    halves = [jnp.where(lane < HD, 1.0, 0.0), jnp.where(lane < HD, 0.0, 1.0)]
    valid = lax.broadcasted_iota(jnp.int32, (span, span), 1) < length

    def heads_at(at):
        query = qkv[:, pl.ds(at, 2 * HD)]
        keyed = qkv[:, pl.ds(width + at, 2 * HD)]
        valued = qkv[:, pl.ds(2 * width + at, 2 * HD)]
        total = jnp.zeros((span, 2 * HD), f32)
        for half in halves:
            scores = lax.dot_general(
                query * half.astype(bf16),
                keyed,
                (((1,), (1,)), ((), ())),
                preferred_element_type=f32,
            ) * HD ** (-0.5)
            scores = jnp.where(valid, scores, -1e30)
            spread = jnp.exp(scores - jnp.max(scores, -1, keepdims=True))
            probs = spread * (1.0 / jnp.sum(spread, -1, keepdims=True))
            total += half * product(probs.astype(bf16), valued)
        ctx[:, pl.ds(at, 2 * HD)] = total.astype(bf16)

    for at in range(0, width, 2 * HD):
        heads_at(at)

    second = normed(first + product(ctx[...], w_out[...]), *scale(1))
    low = second.astype(bf16)
    ffn = jnp.zeros((span, width), f32)
    for at in range(0, w_up.shape[1], width):
        pre = product(low, w_up[:, at : at + width])
        active = (0.5 * pre * (1.0 + lax.erf(pre * (0.5**0.5)))).astype(bf16)
        ffn += product(active, w_down[at : at + width, :])
    final = normed(second + ffn, *scale(2))
    out[0] = product(pick(picks[0], span), final.astype(bf16)).astype(bf16)


def teacher_rows(lengths, slot, picks, got, extra, pos, norms, w_qkv, w_out, w_up, w_down):
    count, picked = picks.shape
    span, width = pos.shape

    def whole(array, *shape):
        shape = shape or array.shape
        return pl.BlockSpec(shape, lambda i: (0,) * len(shape), pipeline_mode=pl.Buffered(1))

    def each(*shape):
        return pl.BlockSpec((1,) + shape, lambda i: (i, 0, 0))

    return pl.pallas_call(
        teacher_kernel,
        grid=(count,),
        out_shape=jax.ShapeDtypeStruct((count, picked, width), jnp.bfloat16),
        in_specs=[
            pl.BlockSpec(memory_space=pltpu.SMEM),
            each(span, 1),
            each(picked, 1),
            whole(got, got.shape[0], width),
            each(span, width),
            whole(pos),
            whole(norms),
            whole(w_qkv),
            whole(w_out),
            whole(w_up),
            whole(w_down),
        ],
        out_specs=each(picked, width),
        scratch_shapes=[
            pltpu.VMEM((span, 3 * width), jnp.bfloat16),
            pltpu.VMEM((span, width), jnp.bfloat16),
        ],
        compiler_params=pltpu.CompilerParams(vmem_limit_bytes=WIDE),
    )(
        lengths[None],
        slot.reshape(count, span, 1),
        picks[:, :, None],
        got,
        extra,
        pos,
        norms,
        w_qkv,
        w_out,
        w_up,
        w_down,
    )


DEEP = 64
WING = 256


def by_eight(value):
    return value.reshape(value.shape[0] // 8, 8, value.shape[1])


def logits_kernel(labels, rows, head, out, stats):
    f32 = jnp.float32
    taken = rows[...].reshape(-1, rows.shape[-1])
    vocab = out.shape[1]
    parts = []
    for at in range(0, taken.shape[0], WING):
        logits = lax.dot_general(
            head[0], taken[at : at + WING], (((1,), (1,)), ((), ())), preferred_element_type=f32
        )
        out[0, :, at : at + WING] = logits
        parts.append(logits)
    for k, logits in enumerate(parts):
        cols = slice(k * WING, (k + 1) * WING)
        top = jnp.max(jnp.max(by_eight(logits), 0), 0, keepdims=True)
        row = lax.broadcasted_iota(jnp.int32, (DEEP, WING), 0) - labels[:, cols]
        totals = [jnp.zeros((8, WING), f32)] * 3
        for deep in range(0, vocab, DEEP):
            part = logits[deep : deep + DEEP]
            spread = jnp.exp(part - top)
            hit = jnp.where(row == -deep, part, 0.0)
            totals = [
                total + jnp.sum(by_eight(more), 0)
                for total, more in zip(totals, (spread, spread * part, hit))
            ]
        lines = [top] + [jnp.sum(total, 0, keepdims=True) for total in totals]
        stats[0, :, cols] = jnp.concatenate(lines, axis=0)


def vocabulary_logits(labels, rows, heads):
    devices, count, picked, width = rows.shape
    vocab = heads.shape[1]
    block = 2 * WING // picked
    wide = block * picked
    return pl.pallas_call(
        logits_kernel,
        grid=(count, devices // block),
        out_shape=[
            jax.ShapeDtypeStruct((count, vocab, devices * picked), jnp.float32),
            jax.ShapeDtypeStruct((count, 4, devices * picked), jnp.float32),
        ],
        in_specs=[
            pl.BlockSpec((1, wide), lambda k, j: (0, j)),
            pl.BlockSpec((block, 1, picked, width), lambda k, j: (j, k, 0, 0)),
            pl.BlockSpec((1, vocab, width), lambda k, j: (k, 0, 0)),
        ],
        out_specs=[
            pl.BlockSpec((1, vocab, wide), lambda k, j: (k, 0, j)),
            pl.BlockSpec((1, 4, wide), lambda k, j: (k, 0, j)),
        ],
        compiler_params=pltpu.CompilerParams(vmem_limit_bytes=WIDE),
    )(labels, rows, heads)


def blend_kernel(stats, counted_ref, shift, loss, seen, sends, arrivals, local):
    f32, bf16 = jnp.float32, jnp.bfloat16
    me = here()
    greet([moved(me, *step) for step in AROUND])

    def columns(place):
        chip = place["y"] * 4 + place["x"]
        return stats.at[:, :, pl.ds(pl.multiple_of(chip * 128, 128), 128)]

    copies = []
    for k, step in enumerate(AROUND):
        place = moved(me, *step)
        copies.append(remote(columns(place), seen.at[number(me)], sends, arrivals, k, place))
    own = pltpu.make_async_copy(columns(me), seen.at[number(me)], local)
    own.start()
    own.wait()
    for copy in copies:
        copy.wait()

    def over_parts(k):
        tops = seen[:, k, 0, :]
        best = jnp.max(tops, 0, keepdims=True)
        scale = jnp.exp(tops - best)
        total = jnp.sum(seen[:, k, 1, :] * scale, 0, keepdims=True)
        return best + jnp.log(total), scale, total

    counted = counted_ref[...]
    lane = lax.broadcasted_iota(jnp.int32, (1, 128), 1)
    left = lane < 64
    totals, entropies, chances = [], [], []
    for k in range(4):
        lse, scale, total = over_parts(k)
        entropies.append(jnp.sum(seen[:, k, 2, :] * scale, 0, keepdims=True) / total - lse)
        chances.append(counted * (jnp.sum(seen[:, k, 3, :], 0, keepdims=True) - lse))
        totals.append(lse)
    student, _, _ = over_parts(4)

    def of_sequence(values):
        first = jnp.sum(jnp.where(left, values, 0.0), -1, keepdims=True)
        second = jnp.sum(jnp.where(left, 0.0, values), -1, keepdims=True)
        return jnp.where(left, first, second)

    hits = jnp.maximum(of_sequence(counted), 1.0)
    gains = [of_sequence(chance) / hits for chance in chances]
    best = functools.reduce(jnp.maximum, gains)
    powers = [jnp.exp(gain - best) for gain in gains]
    power = functools.reduce(jnp.add, powers)
    entropy = jnp.zeros((1, 128), f32)
    lines = []
    for k in range(4):
        lines.append(gains[k] - best - jnp.log(power) - totals[k])
        entropy += (powers[k] / power * entropies[k]).astype(bf16).astype(f32)
    lines += [student, counted, jnp.zeros((2, 128), f32)]
    chip = me["y"] * 4 + me["x"]
    shift[chip] = jnp.concatenate(lines, axis=0)
    ours = jnp.where(left, 0, 1) == me["c"]
    lines = [counted * (entropy + student), counted]
    lines = [jnp.where(ours, line, 0.0) for line in lines] + [jnp.zeros((6, 128), f32)]
    loss[...] = jnp.concatenate(lines, axis=0)
    copies = []
    for k in range(1, 16):
        place = moved(me, (7 * k) % 16 // 4, (7 * k) % 4, 0)
        copies.append(remote(shift.at[chip], shift.at[chip], sends, arrivals, 30 + k, place))
    for copy in copies:
        copy.wait()


def blend(stats, counted, collective):
    return pl.pallas_call(
        blend_kernel,
        out_shape=[
            jax.ShapeDtypeStruct((16, 8, 128), jnp.float32),
            jax.ShapeDtypeStruct((8, 128), jnp.float32),
        ],
        in_specs=[VMEM, VMEM],
        out_specs=[VMEM, VMEM],
        scratch_shapes=[
            pltpu.VMEM((32, 5, 4, 128), jnp.float32),
            pltpu.SemaphoreType.DMA((46,)),
            pltpu.SemaphoreType.DMA((46,)),
            pltpu.SemaphoreType.DMA,
        ],
        compiler_params=pltpu.CompilerParams(collective_id=collective, has_side_effects=True),
    )(stats, counted)


def head_grads_kernel(
    logits, z, shift, h, table, head_grad, head_low, grad_rows, crossed, low
):
    f32, bf16 = jnp.float32, jnp.bfloat16
    grad = jnp.zeros(head_grad.shape, f32)
    cross = jnp.zeros((1, WING), f32)
    for at in range(0, z.shape[2], WING):
        cols = slice(at, at + WING)
        lines = jnp.concatenate([shift[at // 128], shift[at // 128 + 1]], axis=1)
        lse, counted = lines[4:5], lines[5:6]
        total = jnp.zeros((8, WING), f32)
        for deep in range(0, z.shape[1], DEEP):
            rows = slice(deep, deep + DEEP)
            target = jnp.zeros((DEEP, WING), f32)
            for t in range(4):
                share = jnp.exp(logits[t, rows, cols] + lines[t : t + 1])
                target += share.astype(bf16).astype(f32)
            student = z[0, rows, cols]
            low[rows, cols] = (counted * (jnp.exp(student - lse) - target)).astype(bf16)
            total += jnp.sum(by_eight(target * student), 0)
        cross += counted * jnp.sum(total, 0, keepdims=True)
        grad_rows[cols] = lax.dot_general(
            low[:, cols], table[...], (((0,), (0,)), ((), ())), preferred_element_type=f32
        ).astype(bf16)
        grad += product(low[:, cols], h[cols])

    @pl.when(pl.program_id(0) == 0)
    def _():
        head_grad[...] = grad
        crossed[...] = cross

    @pl.when(pl.program_id(0) > 0)
    def _():
        head_grad[...] += grad
        crossed[...] += cross

    @pl.when(pl.program_id(0) == pl.num_programs(0) - 1)
    def _():
        head_low[...] = head_grad[...].astype(bf16)


def head_grads(logits, z, shift, h, table):
    teachers, vocab, rows = logits.shape
    width = table.shape[1]
    wide = 2 * WING
    return pl.pallas_call(
        head_grads_kernel,
        grid=(rows // wide,),
        out_shape=[
            jax.ShapeDtypeStruct((vocab, width), jnp.float32),
            jax.ShapeDtypeStruct((vocab, width), jnp.bfloat16),
            jax.ShapeDtypeStruct((rows, width), jnp.bfloat16),
            jax.ShapeDtypeStruct((1, WING), jnp.float32),
        ],
        in_specs=[
            pl.BlockSpec((teachers, vocab, wide), lambda j: (0, 0, j)),
            pl.BlockSpec((1, vocab, wide), lambda j: (0, 0, j)),
            pl.BlockSpec((wide // 128, 8, 128), lambda j: (j, 0, 0)),
            pl.BlockSpec((wide, width), lambda j: (j, 0)),
            pl.BlockSpec((vocab, width), lambda j: (0, 0)),
        ],
        out_specs=[
            pl.BlockSpec((vocab, width), lambda j: (0, 0)),
            pl.BlockSpec((vocab, width), lambda j: (0, 0)),
            pl.BlockSpec((wide, width), lambda j: (j, 0)),
            pl.BlockSpec((1, WING), lambda j: (0, 0)),
        ],
        scratch_shapes=[pltpu.VMEM((vocab, wide), jnp.bfloat16)],
        compiler_params=pltpu.CompilerParams(vmem_limit_bytes=40 * 2**20),
    )(logits, z, shift, h, table)


def quarter(group):
    return pl.ds(pl.multiple_of(group * 128, 128), 128)


def scatter_sum_kernel(plan, side, *refs, work=None):
    f32, bf16 = jnp.float32, jnp.bfloat16
    parts, refs = refs[: len(plan)], refs[len(plan) :]
    if side == "head":
        exact, sided, out, side_out, mine_exact, side_in, *refs = refs
    else:
        sided, out, side_out, side_in, *refs = refs
    own, other, both, in_a, in_b, mid_a, mid_b, end_a, end_b, sends, arrivals, local = refs
    me = here()
    group = lax.axis_index("grp")
    groups = [{"grp": lax.rem(group + d, 4)} for d in (1, 2, 3)]
    steps_x = [moved(me, 0, d, 0) for d in (1, 2, 3)]
    steps_y = [moved(me, d, 0, 0) for d in (1, 2, 3)]
    sibling = moved(me, 0, 0, 1)
    plane = [moved(me, *step) for step in AROUND]
    greet(groups + (plane if side == "rows" else [sibling] + steps_x + steps_y), work)
    copies, at, k = [], 0, 16
    width = own.shape[-1]
    for part, (rows, columns) in zip(parts, plan):
        for column in range(0, columns, width):
            span = (slice(None), pl.ds(at, rows))
            cols = pl.ds(column, width)
            copies.append(
                remote(
                    part.at[:, sibling["c"], :, cols],
                    other.at[span],
                    sends,
                    arrivals,
                    k,
                    sibling,
                )
            )
            mine = pltpu.make_async_copy(
                part.at[:, me["c"], :, cols], own.at[span], local.at[k - 15]
            )
            mine.start()
            copies.append(mine)
            at += rows
            k += 1
    over = [
        remote(
            sided.at[:, quarter(place["grp"])],
            side_in.at[group] if side == "rows" else side_in.at[d],
            sends,
            arrivals,
            13 + d,
            place,
        )
        for d, place in enumerate(groups)
    ]
    kept = pltpu.make_async_copy(
        (sided if side == "rows" else exact).at[:, quarter(group)],
        side_in.at[group] if side == "rows" else mine_exact,
        local.at[0],
    )
    kept.start()
    over.append(kept)
    for copy in copies:
        copy.wait()

    @pl.loop(0, 16)
    def _(k):
        both[k // 4, lax.rem(k, 4)] = (own[k].astype(f32) + other[k].astype(f32)).astype(bf16)

    cut = in_a.shape[-1]
    left, right = pl.ds(0, cut), pl.ds(cut, width - cut)
    copies = []
    for d in range(3):
        to_x, to_y = steps_x[d], steps_y[d]
        copies.append(
            remote(both.at[:, to_x["x"], :, left], in_a.at[d], sends, arrivals, 1 + d, to_x)
        )
        copies.append(
            remote(both.at[to_y["y"], :, :, right], in_b.at[d], sends, arrivals, 4 + d, to_y)
        )
    last = []
    if side == "rows":
        for copy in over:
            copy.wait()
        room = side_in.shape[1] // 32

        def of(place):
            return side_in.at[:, pl.ds(pl.multiple_of(number(place) * room, room), room)]

        for j, place in enumerate(plane):
            last.append(remote(of(place), side_out.at[number(me)], sends, arrivals, k + j, place))
        kept = pltpu.make_async_copy(of(me), side_out.at[number(me)], local.at[0])
        kept.start()
        last.append(kept)
    for copy in copies:
        copy.wait()

    @pl.loop(0, 4)
    def _(k):
        total_a = both[k, me["x"], :, left].astype(f32)
        total_b = both[me["y"], k, :, right].astype(f32)
        for d in range(3):
            total_a += in_a[d, k].astype(f32)
            total_b += in_b[d, k].astype(f32)
        mid_a[k] = total_a.astype(bf16)
        mid_b[k] = total_b.astype(bf16)

    copies = []
    for d in range(3):
        to_x, to_y = steps_x[d], steps_y[d]
        copies.append(remote(mid_a.at[to_y["y"]], end_a.at[d], sends, arrivals, 7 + d, to_y))
        copies.append(remote(mid_b.at[to_x["x"]], end_b.at[d], sends, arrivals, 10 + d, to_x))
    if side == "head":
        for copy in over:
            copy.wait()
        total = mine_exact[...]
        for d in range(3):
            total += side_in[d].astype(f32)
        side_out[...] = total
    for copy in copies:
        copy.wait()
    total_a = mid_a[me["y"]].astype(f32)
    total_b = mid_b[me["x"]].astype(f32)
    for d in range(3):
        total_a += end_a[d].astype(f32)
        total_b += end_b[d].astype(f32)
    out[:, left] = total_a.astype(out.dtype)
    out[:, right] = total_b.astype(out.dtype)
    for copy in last:
        copy.wait()


def scatter_scratch(rows, width, pieces, more):
    cut = width // 2
    rest = width - cut
    bf16 = jnp.bfloat16
    semaphores = 16 + pieces + more
    return [
        pltpu.VMEM((16, rows, width), bf16),
        pltpu.VMEM((16, rows, width), bf16),
        pltpu.VMEM((4, 4, rows, width), bf16),
        pltpu.VMEM((3, 4, rows, cut), bf16),
        pltpu.VMEM((3, 4, rows, rest), bf16),
        pltpu.VMEM((4, rows, cut), bf16),
        pltpu.VMEM((4, rows, rest), bf16),
        pltpu.VMEM((3, rows, cut), bf16),
        pltpu.VMEM((3, rows, rest), bf16),
        pltpu.SemaphoreType.DMA((semaphores,)),
        pltpu.SemaphoreType.DMA((semaphores,)),
        pltpu.SemaphoreType.DMA((1 + pieces,)),
    ]


def scatter_head(part, exact, low, collective):
    _, rows, width = part.shape
    tall = low.shape[0]
    f32, bf16 = jnp.float32, jnp.bfloat16
    return pl.pallas_call(
        partial(scatter_sum_kernel, [(rows, width)], "head"),
        out_shape=[
            jax.ShapeDtypeStruct((rows, width), f32),
            jax.ShapeDtypeStruct((tall, 128), f32),
        ],
        in_specs=[ANY] * 3,
        out_specs=[VMEM, VMEM],
        scratch_shapes=[pltpu.VMEM((tall, 128), f32), pltpu.VMEM((3, tall, 128), bf16)]
        + scatter_scratch(rows, width, 1, 0),
        compiler_params=pltpu.CompilerParams(
            collective_id=collective, has_side_effects=True, vmem_limit_bytes=12 * 2**20
        ),
    )(part.reshape(16, 2, rows, width), exact, low)


def group_sum_kernel(
    head, wants, given, rest, facts, crossed, table_out, rest_out, seen, total, rest_in, told, sends, arrivals
):
    f32, bf16 = jnp.float32, jnp.bfloat16
    me = here()
    group = lax.axis_index("grp")
    groups = [{"grp": lax.rem(group + d, 4)} for d in (1, 2, 3)]
    plane = [moved(me, *step) for step in AROUND]
    greet(groups + plane)
    mine = quarter(group)
    early = [
        remote(rest.at[:, quarter(groups[d]["grp"])], rest_in.at[d], sends, arrivals, d, groups[d])
        for d in range(3)
    ]
    total[...] = head[...]

    @pl.loop(0, wants.shape[0])
    def _(k):
        row = lax.broadcasted_iota(jnp.int32, (head.shape[0], wants.shape[1]), 0)
        hot = jnp.where(row == wants[pl.ds(k, 1), :], 1.0, 0.0).astype(bf16)
        total[...] += product(hot, given[k])

    rounded = total[...].astype(bf16)
    table_out[:, mine] = rounded
    rounded = rounded.astype(f32)
    squares = jnp.sum(by_eight(rounded * rounded), 0)
    wide = [
        remote(table_out.at[:, mine], table_out.at[:, mine], sends, arrivals, 3 + d, groups[d])
        for d in range(3)
    ]
    for copy in early:
        copy.wait()
    summed = rest[:, mine].astype(f32)
    for d in range(3):
        summed += rest_in[d].astype(f32)
    summed = summed.astype(bf16)
    rest_out[:, mine] = summed
    summed = summed.astype(f32)
    squares += jnp.sum(by_eight(summed * summed), 0)
    told[group, 0:8] = squares
    first = lax.broadcasted_iota(jnp.int32, (8, 128), 0) == 0
    cross = crossed[:, :128] + crossed[:, 128:]
    told[group, 8:16] = facts[...] - jnp.where(first, cross, 0.0)
    copies = []
    for d in range(3):
        copies.append(remote(told.at[group], told.at[group], sends, arrivals, 6 + d, groups[d]))
        wide.append(
            remote(rest_out.at[:, mine], rest_out.at[:, mine], sends, arrivals, 9 + d, groups[d])
        )
    for copy in copies:
        copy.wait()
    seen[number(me)] = told[0] + told[1] + told[2] + told[3]
    copies = []
    for k, place in enumerate(plane):
        copies.append(
            remote(seen.at[number(me)], seen.at[number(me)], sends, arrivals, 12 + k, place)
        )
    for copy in copies + wide:
        copy.wait()


def sum_of_groups(head, wants, given, rest, facts, crossed, collective):
    count = 12 + len(AROUND)
    bf16 = jnp.bfloat16
    return pl.pallas_call(
        group_sum_kernel,
        out_shape=[
            jax.ShapeDtypeStruct((head.shape[0], 512), bf16),
            jax.ShapeDtypeStruct(rest.shape, rest.dtype),
            jax.ShapeDtypeStruct((32, 16, 128), jnp.float32),
        ],
        in_specs=[VMEM] * 6,
        out_specs=[VMEM, VMEM, VMEM],
        scratch_shapes=[
            pltpu.VMEM(head.shape, jnp.float32),
            pltpu.VMEM((3, rest.shape[0], 128), rest.dtype),
            pltpu.VMEM((4, 16, 128), jnp.float32),
            pltpu.SemaphoreType.DMA((count,)),
            pltpu.SemaphoreType.DMA((count,)),
        ],
        compiler_params=pltpu.CompilerParams(
            collective_id=collective, has_side_effects=True, vmem_limit_bytes=40 * 2**20
        ),
    )(head, wants, given, rest, facts, crossed)


def slots(tokens, own_rows):
    count = tokens.shape[0]
    row, column = tokens[:, None], tokens[None, :]
    place = jnp.arange(count)
    repeated = jnp.any((row == column) & (place[:, None] < place[None, :]), axis=0)
    owner = tokens // own_rows
    counts = ~repeated[:, None] & (row >= (owner * own_rows)[None, :]) & (row < column)
    return owner, ~repeated, jnp.sum(counts.astype(jnp.int32), axis=0)


def slot_in_round(owner, rank, room, turn, apart=None):
    at = rank - turn * room
    return jnp.where((at >= 0) & (at < room), owner * (apart or room) + at, -1)


def wanted_rows(slot, first, local, places):
    hit = (jnp.where(first, slot, -1)[:, None] == jnp.arange(places)[None, :])
    return jnp.sum(jnp.where(hit, local[:, None] + 1, 0), axis=0) - 1


def one_hot(index, count):
    return (index[:, None] == jnp.arange(count)[None, :]).astype(jnp.bfloat16)


def product(left, right):
    return jnp.dot(left, right, preferred_element_type=jnp.float32)


def folded(rows):
    return jnp.concatenate(jnp.split(rows, 2, axis=2), axis=1)


def unfolded(rows):
    return jnp.concatenate(jnp.split(rows, 2, axis=1), axis=2)


def layer_norm(value, gain, shift):
    mean = jnp.mean(value, -1, keepdims=True)
    centred = value - mean
    var = jnp.mean(centred * centred, -1, keepdims=True)
    return centred * lax.rsqrt(var + norm_eps) * gain + shift


def project(left, right):
    return jnp.einsum("blk,kn->bln", left, right, preferred_element_type=jnp.float32)


def split_heads(packed, width):
    batch, span = (packed.shape[0], packed.shape[1])
    return [
        packed[:, :, piece * width : (piece + 1) * width].reshape(batch, span, width // HD, HD)
        for piece in range(3)
    ]


def masked_scores(query, keyed, lengths):
    scores = jnp.einsum(
        "bqhd,bkhd->bhqk", query, keyed, preferred_element_type=jnp.float32
    ) * HD ** (-0.5)
    valid = jnp.arange(query.shape[1])[None, :] < lengths[:, None]
    return jnp.where(valid[:, None, None, :], scores, -1e30)


def forward(embedded, lengths, weights):
    w_qkv, w_out, w_up, w_down, norms = weights
    norms = norms.astype(jnp.float32)
    width = w_out.shape[1]
    first = layer_norm(embedded, norms[:, 0], norms[:, 1])
    first_low = first.astype(jnp.bfloat16)
    packed = project(first_low, w_qkv).astype(jnp.bfloat16)
    query, keyed, valued = split_heads(packed, width)
    scores = masked_scores(query, keyed, lengths)
    top = jnp.max(scores, -1, keepdims=True)
    total = jnp.sum(jnp.exp(scores - top), -1, keepdims=True)
    probs = (jnp.exp(scores - top) / total).astype(jnp.bfloat16)
    context = jnp.einsum("bhqk,bkhd->bqhd", probs, valued, preferred_element_type=jnp.float32)
    context = context.reshape(first.shape).astype(jnp.bfloat16)
    joined = first + project(context, w_out)
    second = layer_norm(joined, norms[:, 2], norms[:, 3])
    second_low = second.astype(jnp.bfloat16)
    hidden_pre = project(second_low, w_up)
    active = jax.nn.gelu(hidden_pre, approximate=False).astype(jnp.bfloat16)
    summed = second + project(active, w_down)
    final = layer_norm(summed, norms[:, 4], norms[:, 5])
    saved = (
        embedded,
        first_low,
        packed,
        context,
        joined,
        second_low,
        hidden_pre,
        active,
        summed,
    )
    return (final, saved)


def norm_back(value, gain, grad):
    mean = jnp.mean(value, -1, keepdims=True)
    centred = value - mean
    scale = lax.rsqrt(jnp.mean(centred * centred, -1, keepdims=True) + norm_eps)
    unit = centred * scale
    scaled = grad * gain
    back = scaled - jnp.mean(scaled, -1, keepdims=True)
    back = scale * (back - unit * jnp.mean(scaled * unit, -1, keepdims=True))
    return back, jnp.sum(grad * unit, 0, keepdims=True), jnp.sum(grad, 0, keepdims=True)


def product_of(left, right, dims):
    return lax.dot_general(left, right, (dims, ((), ())), preferred_element_type=jnp.float32)


def backward_kernel(
    lengths,
    picks,
    slot,
    grad_rows,
    embedded,
    first_low,
    packed,
    context,
    joined,
    second_low,
    hidden_pre,
    active,
    summed,
    norms,
    w_qkv,
    w_out,
    w_up,
    w_down,
    g_qkv,
    g_out,
    g_up,
    g_down,
    small,
    low_emb,
    given,
    d_packed,
    d_context,
    carried,
):
    f32, bf16 = jnp.float32, jnp.bfloat16
    span, width = embedded.shape
    rows, columns, both = ((0,), (0,)), ((1,), (1,)), ((1,), (0,))
    row = lax.broadcasted_iota(jnp.int32, (span, picks.shape[1]), 0)
    hot = jnp.where(row == picks[...], 1.0, 0.0)
    d_final = jnp.dot(
        hot, grad_rows[...], preferred_element_type=f32, precision=lax.Precision.HIGHEST
    )
    d_summed, gain_c, shift_c = norm_back(summed[...], norms[4:5], d_final)
    d_ffn = d_summed.astype(bf16)
    carried[...] = d_summed

    @pl.loop(0, w_up.shape[1] // width)
    def _(k):
        cols = pl.ds(pl.multiple_of(k * width, width), width)
        blocks = g_down.shape[0] * width // w_up.shape[1]
        piece = product_of(active[:, cols], d_ffn, rows)
        g_down[pl.ds(k * blocks, blocks)] = piece.reshape(blocks, *g_down.shape[1:]).astype(bf16)
        pre = hidden_pre[:, cols]
        slope = 0.5 * (1.0 + lax.erf(pre * (0.5**0.5)))
        slope += pre * (jnp.exp(-0.5 * pre * pre) * (0.5 / math.pi) ** 0.5)
        d_up = (slope * product_of(d_ffn, w_down[cols], columns)).astype(bf16)
        piece = product_of(second_low[...], d_up, rows)
        g_up[:, :, :, cols] = piece.reshape(*g_up.shape[:3], width).astype(bf16)
        carried[...] += product_of(d_up, w_up[:, cols], columns)

    d_joined, gain_b, shift_b = norm_back(joined[...], norms[2:3], carried[...])
    d_attn = d_joined.astype(bf16)
    g_out[...] = product_of(context[...], d_attn, rows).reshape(g_out.shape).astype(bf16)
    d_context[...] = product_of(d_attn, w_out[...], columns).astype(bf16)
    lane = lax.broadcasted_iota(jnp.int32, (span, 2 * HD), 1)
    halves = [jnp.where(lane < HD, 1.0, 0.0), jnp.where(lane < HD, 0.0, 1.0)]
    valid = lax.broadcasted_iota(jnp.int32, (span, span), 1) < lengths[0, 0]

    @pl.loop(0, width // (2 * HD))
    def _(k):
        at = pl.multiple_of(k * 2 * HD, 2 * HD)
        query, keyed, valued = [
            packed[:, pl.ds(piece * width + at, 2 * HD)] for piece in range(3)
        ]
        d_heads = d_context[:, pl.ds(at, 2 * HD)]
        d_query, d_keyed, d_valued = [jnp.zeros((span, 2 * HD), f32)] * 3
        for half in halves:
            low = half.astype(bf16)
            scores = product_of(query * low, keyed, columns) * HD ** (-0.5)
            scores = jnp.where(valid, scores, -1e30)
            spread = jnp.exp(scores - jnp.max(scores, -1, keepdims=True))
            probs = spread * (1.0 / jnp.sum(spread, -1, keepdims=True))
            d_valued += half * product_of(probs.astype(bf16), d_heads, rows)
            d_probs = product_of(d_heads * low, valued, columns)
            d_scores = probs * (d_probs - jnp.sum(probs * d_probs, -1, keepdims=True))
            d_scores = d_scores.astype(bf16)
            d_query += half * product_of(d_scores, keyed, both)
            d_keyed += half * product_of(d_scores, query, rows)
        for piece, value in enumerate((d_query * HD ** (-0.5), d_keyed * HD ** (-0.5), d_valued)):
            d_packed[:, pl.ds(piece * width + at, 2 * HD)] = value.astype(bf16)

    carried[...] = d_joined

    @pl.loop(0, 3)
    def _(k):
        cols = pl.ds(pl.multiple_of(k * width, width), width)
        piece = product_of(first_low[...], d_packed[:, cols], rows)
        g_qkv[:, :, :, cols] = piece.reshape(*g_qkv.shape[:3], width).astype(bf16)
        carried[...] += product_of(d_packed[:, cols], w_qkv[:, cols], columns)

    d_emb, gain_a, shift_a = norm_back(embedded[...], norms[0:1], carried[...])
    carried[...] = d_emb
    lines = [gain_a, shift_a, gain_b, shift_b, gain_c, shift_c, jnp.zeros((2, width), f32)]
    lines = jnp.concatenate(lines, axis=0)
    owner = lax.broadcasted_iota(jnp.int32, lines.shape, 1)

    @pl.loop(0, 32)
    def _(k):
        mine = (owner >= k * (width // 32)) & (owner < (k + 1) * (width // 32))
        block = [carried[pl.ds(pl.multiple_of(k * 8, 8), 8)], jnp.where(mine, lines, 0.0)]
        small[k // 2, lax.rem(k, 2)] = jnp.concatenate(block, axis=0).astype(bf16)

    low = d_emb.astype(bf16)
    low_emb[...] = low

    @pl.loop(0, given.shape[0] // span)
    def _(k):
        place = lax.broadcasted_iota(jnp.int32, (span, span), 0) + k * span
        place = jnp.where(place == slot[...], 1.0, 0.0).astype(bf16)
        given[pl.ds(pl.multiple_of(k * span, span), span)] = product(place, low).astype(bf16)


def finish_kernel(plan, *refs):
    inputs, (out, side_out, low_emb), refs = refs[:18], refs[18:21], refs[21:]
    parts, (given, d_packed, d_context, carried), refs = refs[:5], refs[5:9], refs[9:]
    g_qkv, g_out, g_up, g_down, small = parts
    work = partial(
        backward_kernel,
        *inputs,
        g_qkv,
        g_out,
        g_up,
        g_down,
        small,
        low_emb,
        given,
        d_packed,
        d_context,
        carried,
    )
    scatter_sum_kernel(plan, "rows", *parts, given, out, side_out, *refs, work=work)


def backward(lengths, picks, slot, places, weights, saved, grad_rows, collective):
    w_qkv, w_out, w_up, w_down, norms = weights
    span, width = saved[0].shape[1:]
    f32, bf16 = jnp.float32, jnp.bfloat16
    plan = [(w.shape[0] // 32, w.shape[1]) for w in (w_qkv, w_out, w_up, w_down)] + [(16, width)]
    rows = sum(r * (c // width) for r, c in plan)
    pieces = sum(c // width for _, c in plan)
    return pl.pallas_call(
        partial(finish_kernel, plan),
        out_shape=[
            jax.ShapeDtypeStruct((rows, width), bf16),
            jax.ShapeDtypeStruct((32, 4, places // 32, 128), bf16),
            jax.ShapeDtypeStruct((span, width), bf16),
        ],
        in_specs=[pl.BlockSpec(memory_space=pltpu.SMEM)] + [VMEM] * 17,
        out_specs=[VMEM] * 3,
        scratch_shapes=[pltpu.VMEM((16, 2, *size), bf16) for size in plan]
        + [
            pltpu.VMEM((places, width), bf16),
            pltpu.VMEM((span, 3 * width), bf16),
            pltpu.VMEM((span, width), bf16),
            pltpu.VMEM((span, width), f32),
            pltpu.VMEM((4, places, 128), bf16),
        ]
        + scatter_scratch(rows, width, pieces, len(AROUND)),
        compiler_params=pltpu.CompilerParams(
            collective_id=collective, has_side_effects=True, vmem_limit_bytes=36 * 2**20
        ),
    )(
        lengths[None],
        picks,
        slot[None],
        grad_rows,
        *[value[0] for value in saved],
        norms.astype(f32).T,
        w_qkv,
        w_out,
        w_up,
        w_down,
    )


def per_device(
    ids,
    lengths,
    picks,
    labels,
    s_table,
    s_pos,
    s_qkv,
    s_out,
    s_up,
    s_down,
    s_norms,
    m_table,
    m_pos,
    m_qkv,
    m_out,
    m_up,
    m_down,
    m_norms,
    a_table,
    a_pos,
    a_qkv,
    a_out,
    a_up,
    a_down,
    a_norms,
    t_table,
    t_pos,
    t_qkv,
    t_out,
    t_up,
    t_down,
    t_norms,
):
    masters = (s_table, s_pos, s_qkv, s_out, s_up, s_down, s_norms)
    momenta = (m_table, m_pos, m_qkv, m_out, m_up, m_down, m_norms)
    averages = (a_table, a_pos, a_qkv, a_out, a_up, a_down, a_norms)
    f32, bf16 = jnp.float32, jnp.bfloat16
    fsdp = lax.axis_size(FSDP)
    width, t_width = s_table.shape[1], t_table.shape[2]
    vocab_own = s_table.shape[0]
    picked = picks.shape[1]
    span = ids.shape[1]

    facts = jnp.concatenate([ids, picks, jnp.broadcast_to(lengths[:, None], (1, 64))], axis=1)
    facts = jnp.pad(facts.reshape(3, 128), ((0, 5), (0, 0)))
    facts = exchange_groups(jnp.broadcast_to(facts, (4, 8, 128)), 9)[:, :3].reshape(4, -1)
    group_ids, group_picks = facts[:, :span], facts[:, span : span + picked]
    group_lengths = facts[:, span + picked]
    own_table = s_table.astype(bf16)
    t_owner, t_first, t_rank = slots(group_ids.reshape(-1), vocab_own)
    s_owners, s_firsts, s_ranks = jax.vmap(lambda one: slots(one, vocab_own))(group_ids)
    my_group = lax.axis_index("grp")
    s_owner, s_rank = (
        lax.dynamic_index_in_dim(v, my_group, 0, keepdims=False) for v in (s_owners, s_ranks)
    )
    most = jnp.maximum(jnp.max(t_rank) // T_ROOM, jnp.max(s_ranks) // S_ROOM) + 1
    t_local = group_ids.reshape(-1) - t_owner * vocab_own
    s_locals = group_ids - s_owners * vocab_own

    def asked(turn):
        t_slot = slot_in_round(t_owner, t_rank, T_ROOM, turn)
        s_slot = slot_in_round(s_owner, s_rank, S_ROOM, turn)
        t_ask = wanted_rows(t_slot, t_first, t_local, fsdp * T_ROOM).reshape(fsdp, T_ROOM)
        s_asks = jax.vmap(partial(wanted_rows, places=fsdp * S_APART))(
            slot_in_round(s_owners, s_ranks, S_ROOM, turn, S_APART), s_firsts, s_locals
        ).reshape(-1, fsdp, S_APART)
        s_ask = lax.dynamic_index_in_dim(s_asks, my_group, 0, keepdims=False)[:, :S_ROOM]
        s_asks = jnp.moveaxis(s_asks, 0, 1).reshape(fsdp, -1)
        return t_slot, s_slot, t_ask, s_ask, s_asks

    def answer(t_want, s_want):
        t_sent = product(one_hot(t_want.reshape(-1), vocab_own), t_table[0]).astype(bf16)
        s_sent = product(one_hot(s_want.reshape(-1), vocab_own), own_table).astype(bf16)
        return jnp.concatenate(
            [t_sent.reshape(fsdp, T_ROOM, t_width), folded(s_sent.reshape(fsdp, S_ROOM, width))],
            axis=2,
        )

    def placed(got, t_slot, s_slot):
        t_got = got[:, :, :t_width].reshape(-1, t_width)
        s_got = unfolded(got[:, :, t_width:]).reshape(-1, width)
        return (
            product(one_hot(t_slot, fsdp * T_ROOM), t_got),
            product(one_hot(s_slot, fsdp * S_ROOM), s_got),
        )

    def swap(value):
        return lax.all_to_all(value, FSDP, split_axis=0, concat_axis=0, tiled=True)

    def ask_again(turn):
        t_slot, s_slot, t_ask, s_ask, s_asks = asked(turn)
        wants = swap(jnp.concatenate([t_ask, s_ask, s_asks], axis=1))
        both = T_ROOM + S_ROOM
        return t_slot, s_slot, wants[:, :T_ROOM], wants[:, T_ROOM:both], wants[:, both:]

    def more_rows(state):
        turn, t_emb, s_emb = state
        t_slot, s_slot, t_want, s_want, _ = ask_again(turn)
        t_more, s_more = placed(swap(answer(t_want, s_want)), t_slot, s_slot)
        return turn + 1, t_emb + t_more.astype(bf16), s_emb + s_more.astype(bf16)

    t_slot, s_slot, t_ask, s_ask, s_asks = asked(0)
    line = jnp.concatenate(
        [t_ask, s_ask, jnp.broadcast_to(most, (fsdp, 128 - T_ROOM - S_ROOM))], axis=1
    )
    lines = [
        line,
        jnp.broadcast_to(jnp.concatenate([picks, labels], axis=1), (fsdp, 2 * picked)),
        jnp.broadcast_to(lengths[:, None], (fsdp, 128)),
        s_asks,
    ]
    notes = jnp.stack(lines + [jnp.zeros((fsdp, 128), jnp.int32)] * 4, axis=1)
    notes, got = route(notes, t_table[0], own_table, 1)
    wants = notes[:, 3]
    rounds = jnp.max(notes[:, 0, T_ROOM + S_ROOM])
    plane_picks, plane_labels = notes[:, 1, :picked], notes[:, 1, picked : 2 * picked]
    plane_lengths = notes[:, 2, 0]
    nothing = (jnp.zeros((t_slot.shape[0], t_width), bf16), jnp.zeros((span, width), bf16))
    _, t_extra, s_extra = lax.while_loop(
        lambda state: state[0] < rounds, more_rows, (jnp.int32(1), *nothing)
    )

    def pieces(blocks, qkv, out, up, down, pos, norms):
        lines = norms.shape[0]
        tail = jnp.moveaxis(norms.astype(f32).reshape(lines, blocks, -1), 1, 0)
        tail = jnp.pad(tail, ((0, 0), (0, 8 - lines), (0, width - tail.shape[2])))
        small = jnp.concatenate([pos.reshape(blocks, -1, width).astype(f32), tail], axis=1)
        big = [part.astype(bf16).reshape(blocks, -1, part.shape[1]) for part in (qkv, out, up, down)]
        return big + [lax.optimization_barrier(small.astype(bf16))]

    def pack(parts):
        columns = [
            part[:, :, at : at + width] for part in parts for at in range(0, part.shape[2], width)
        ]
        return jnp.concatenate(columns, axis=1)

    def unpack(packed):
        blocks, lead = packed.shape[0], s_qkv.shape[0]

        def across(at, count):
            return jnp.concatenate(
                [
                    packed[:, at + k * lead : at + (k + 1) * lead].reshape(-1, width)
                    for k in range(count)
                ],
                axis=1,
            )

        at_out = s_qkv.shape[1] // width * lead
        at_up = at_out + lead
        at_down = at_up + s_up.shape[1] // width * lead
        at_pos = at_down + s_down.shape[0]
        at_norms = at_pos + s_pos.shape[0]
        return (
            across(0, s_qkv.shape[1] // width),
            across(at_out, 1),
            across(at_up, s_up.shape[1] // width),
            packed[:, at_down:at_pos].reshape(-1, width),
            packed[:, at_pos:at_norms].reshape(-1, width),
            jnp.moveaxis(
                packed[:, at_norms : at_norms + s_norms.shape[1], :lead], 1, 0
            ).reshape(s_norms.shape[1], -1),
        )

    own_packed = pack(pieces(1, s_qkv, s_out, s_up, s_down, s_pos, s_norms.T))
    w_qkv, w_out, w_up, w_down, positions, norms = unpack(
        lax.all_gather(own_packed, FSDP, axis=0, tiled=True)
    )
    student = (w_qkv, w_out, w_up, w_down, norms.T)
    heads = lax.all_gather(t_table[0], "grp", axis=0, tiled=False)

    taken = teacher_rows(
        group_lengths,
        t_slot,
        group_picks,
        got.reshape(-1, got.shape[2]),
        t_extra.reshape(-1, span, t_width),
        t_pos[0],
        t_norms[0].T,
        t_qkv[0],
        t_out[0],
        t_up[0],
        t_down[0],
    )
    taken, heads = lax.optimization_barrier((taken, heads))
    rows = exchange_groups(taken, 10)
    s_extra, got, rows = lax.optimization_barrier((s_extra, got, rows))
    rows = lax.all_gather(rows, FSDP, axis=0, tiled=False)

    s_got = unfolded(got[:, :, t_width:]).reshape(-1, width)
    s_emb = product(one_hot(s_slot, fsdp * S_ROOM), s_got) + s_extra.astype(f32)
    embedded = s_emb[None] + positions.astype(f32)[None]
    final, saved = forward(embedded, lengths, student)
    own_rows = jnp.take_along_axis(final, picks[:, :, None], axis=1).astype(bf16)[0]
    h = gather_plane(own_rows, 11)
    base = lax.axis_index(FSDP) * vocab_own
    labels_here = plane_labels.reshape(1, -1) - base
    z, z_stats = vocabulary_logits(labels_here, h.reshape(fsdp, 1, picked, width), own_table[None])
    logits, stats = vocabulary_logits(labels_here, rows, heads)
    stats = jnp.concatenate([stats, z_stats], axis=0)
    plane_counted = (plane_picks < plane_lengths[:, None]).astype(f32).reshape(-1, 1, 2 * picked)
    chip = lax.axis_index(("y", "x"))
    chip_counted = lax.dynamic_index_in_dim(plane_counted, chip, 0, keepdims=False)
    shift, own_loss = blend(stats, chip_counted, 3)
    head_grad, head_low, grad_rows, crossed = head_grads(logits, z, shift, h, own_table)
    grad_rows, head_grad = scatter_head(
        grad_rows.reshape(fsdp, picked, width), head_grad, head_low, 5
    )

    g_slot = slot_in_round(s_owner, s_rank, S_ROOM, 0, S_APART)
    rest, got, low_embedded = backward(
        lengths, picks, g_slot, fsdp * S_APART, student, saved, grad_rows, 7
    )

    def given(turn):
        slot = slot_in_round(s_owner, s_rank, S_ROOM, turn, S_APART)
        hot = (jnp.arange(fsdp * S_APART)[:, None] == slot[None, :]).astype(bf16)
        return product(hot, low_embedded).astype(bf16)

    def more_grads(state):
        turn, total = state
        wants = ask_again(turn)[4]
        rows = jnp.stack(jnp.split(given(turn), 4, axis=1))
        rows = lax.all_to_all(rows, "grp", split_axis=0, concat_axis=0, tiled=True)
        rows = swap(jnp.moveaxis(rows.reshape(4, fsdp, S_APART, -1), 0, 1))
        hot = one_hot(wants.reshape(-1), vocab_own).T
        return turn + 1, total + product(hot, rows.reshape(-1, rows.shape[3]))

    _, head_grad = lax.while_loop(
        lambda state: state[0] < rounds, more_grads, (jnp.int32(1), head_grad)
    )
    table_sum, rest_sum, seen = sum_of_groups(
        head_grad, wants.reshape(4, -1), got.reshape(4, -1, got.shape[3]), rest, own_loss, crossed, 8
    )
    turned = [group[:6] + (group[6].T,) for group in (masters, momenta, averages)]
    loss_sum, count, clip_norm, *outs = update(seen, table_sum, rest_sum, *turned)
    outs = tuple(out.T if k % 7 == 6 else out for k, out in enumerate(outs))
    return (loss_sum.reshape(()), count.reshape(()), clip_norm[0, 0]) + outs


def solution(mesh):
    finer = Mesh(
        mesh.devices.reshape(mesh.shape["grp"], 4, 4, 2), ("grp", "y", "x", "c")
    )
    return jax.shard_map(
        per_device,
        mesh=finer,
        in_specs=(
            P(GRP_FSDP, None),
            P(GRP_FSDP),
            P(GRP_FSDP, None),
            P(GRP_FSDP, None),
            P(FSDP, None),
            P(FSDP, None),
            P(FSDP, None),
            P(FSDP, None),
            P(FSDP, None),
            P(FSDP, None),
            P(FSDP, None),
            P(FSDP, None),
            P(FSDP, None),
            P(FSDP, None),
            P(FSDP, None),
            P(FSDP, None),
            P(FSDP, None),
            P(FSDP, None),
            P(FSDP, None),
            P(FSDP, None),
            P(FSDP, None),
            P(FSDP, None),
            P(FSDP, None),
            P(FSDP, None),
            P(FSDP, None),
            P("grp", FSDP, None),
            P("grp", None, None),
            P("grp", None, None),
            P("grp", None, None),
            P("grp", None, None),
            P("grp", None, None),
            P("grp", None, None),
        ),
        out_specs=(
            P(),
            P(),
            P(),
            P(FSDP, None),
            P(FSDP, None),
            P(FSDP, None),
            P(FSDP, None),
            P(FSDP, None),
            P(FSDP, None),
            P(FSDP, None),
            P(FSDP, None),
            P(FSDP, None),
            P(FSDP, None),
            P(FSDP, None),
            P(FSDP, None),
            P(FSDP, None),
            P(FSDP, None),
            P(FSDP, None),
            P(FSDP, None),
            P(FSDP, None),
            P(FSDP, None),
            P(FSDP, None),
            P(FSDP, None),
            P(FSDP, None),
        ),
        check_vma=False,
    )
```
